32 devices in a mesh: dp: 8 (over z, x), mp: 4 (over y, core).
Axes of the slice: x: 2, y: 2, z: 4, core: 2. Of those that a mesh axis runs over, the one named last changes fastest.
Arguments:
- frames: bfloat16 [2048, 16, 512], P('mp', 'dp'), may hold values from -6 to 6
- cotangent: bfloat16 [2048, 16, 512], P('mp', 'dp'), may hold values from -6 to 6
- lengths: int32 [16], P('dp'), may hold values from 128 to 2048, as said below
- weight_project: float32 [3, 512, 512], P(None, 'dp', 'mp'), may hold values from -0.25 to 0.25
- weight_combine: float32 [512, 512], P('dp', 'mp'), may hold values from -0.5 to 0.5
- weight_expand: float32 [512, 2048], P('dp', 'mp'), may hold values from -0.25 to 0.25
- weight_reduce: float32 [512, 2048], P('dp', 'mp'), may hold values from -0.125 to 0.125
- moment_project: float32 [3, 512, 512], P(None, 'dp', 'mp'), may hold values from -512 to 512
- moment_combine: float32 [512, 512], P('dp', 'mp'), may hold values from -512 to 512
- moment_expand: float32 [512, 2048], P('dp', 'mp'), may hold values from -256 to 256
- moment_reduce: float32 [512, 2048], P('dp', 'mp'), may hold values from -512 to 512
- average_project: float32 [3, 512, 512], P(None, 'dp', 'mp'), may hold values from -0.25 to 0.25
- average_combine: float32 [512, 512], P('dp', 'mp'), may hold values from -0.5 to 0.5
- average_expand: float32 [512, 2048], P('dp', 'mp'), may hold values from -0.25 to 0.25
- average_reduce: float32 [512, 2048], P('dp', 'mp'), may hold values from -0.125 to 0.125
- norm_params: float32 [4, 512], replicated, may hold values from -0.5 to 1.4, as said below
- norm_moment: float32 [4, 512], replicated, may hold values from -512 to 512
- norm_average: float32 [4, 512], replicated, may hold values from -0.5 to 1.4, as said below
Outputs:
- layer_out: bfloat16 [2048, 16, 512], P('mp', 'dp')
- input_gradient: float32 [2048, 16, 512], P('mp', 'dp')
- gradient_project: float32 [3, 512, 512], P(None, 'dp', 'mp')
- gradient_combine: float32 [512, 512], P('dp', 'mp')
- gradient_expand: float32 [512, 2048], P('dp', 'mp')
- gradient_reduce: float32 [512, 2048], P('dp', 'mp')
- momentum_project: float32 [3, 512, 512], P(None, 'dp', 'mp')
- momentum_combine: float32 [512, 512], P('dp', 'mp')
- momentum_expand: float32 [512, 2048], P('dp', 'mp')
- momentum_reduce: float32 [512, 2048], P('dp', 'mp')
- smoothed_project: float32 [3, 512, 512], P(None, 'dp', 'mp')
- smoothed_combine: float32 [512, 512], P('dp', 'mp')
- smoothed_expand: float32 [512, 2048], P('dp', 'mp')
- smoothed_reduce: float32 [512, 2048], P('dp', 'mp')
- updated_project: float32 [3, 512, 512], P(None, 'dp', 'mp')
- updated_combine: float32 [512, 512], P('dp', 'mp')
- updated_expand: float32 [512, 2048], P('dp', 'mp')
- updated_reduce: float32 [512, 2048], P('dp', 'mp')
- rounded_project: bfloat16 [3, 512, 512], P(None, 'dp', 'mp')
- rounded_combine: bfloat16 [512, 512], P('dp', 'mp')
- rounded_expand: bfloat16 [512, 2048], P('dp', 'mp')
- rounded_reduce: bfloat16 [512, 2048], P('dp', 'mp')
- norm_gradient: float32 [4, 512], replicated
- norm_momentum: float32 [4, 512], replicated
- norm_smoothed: float32 [4, 512], replicated
- norm_updated: float32 [4, 512], replicated
The draws below stay inside these ranges and needn't reach their ends.
Inputs may be any that keep to these rules, and one draw needn't show every extreme that they name: `lengths`: among the 2 utterances of each index of dp, at least one has 2048 frames. `norm_params`: rows 0 and 2 are gains, rows 1 and 3 shifts. `norm_average`: rows 0 and 2 are gains, rows 1 and 3 shifts.
All inputs are finite; a program needn't handle non-finite values.
Results may differ from the reference program's by a relative error of at most 0.014.
Values may be sent and summed in bfloat16 or wider, within the bound.
No kernel may reach another device: no remote copies, remote signals or barrier semaphores. Data moves between devices by JAX's collectives and lax.ppermute only.
A program may use at most 192 MiB of HBM per device.

```python
import math
import jax
import jax.numpy as jnp
from jax import lax

D = 512
HEADS = 8
HEAD_DIM = 64
FF = 2048
WINDOW = 10
LEN = 2048
UTT_DEV = 2
UTTS = 16
QBLK = 512
N_DP = 8


def draw_lengths(key, part):
    blocks = UTTS // UTT_DEV
    key_pick = jax.random.fold_in(key, 11)
    key_size = jax.random.fold_in(key, 12)
    shortest = LEN // 16
    draws = jax.random.randint(key_size, (blocks, UTT_DEV), 0, 64)
    sizes = shortest + (LEN - shortest) * draws * draws * draws // 250047
    pick = jax.random.randint(key_pick, (blocks, 1), 0, UTT_DEV)
    slots = jnp.arange(UTT_DEV, dtype=jnp.int32)[None, :]
    sizes = jnp.where(slots == pick, LEN, sizes)
    return sizes.reshape(UTTS).astype(jnp.int32)


def norm_rows(key):
    key_gain = jax.random.fold_in(key, 21)
    key_shift = jax.random.fold_in(key, 22)
    gains = jax.random.uniform(key_gain, (2, D), jnp.float32, 0.6, 1.4)
    shifts = jax.random.uniform(key_shift, (2, D), jnp.float32, -0.4, 0.4)
    return jnp.stack([gains[0], shifts[0], gains[1], shifts[1]]).astype(jnp.float32)


def draw_norm_params(key, part):
    return norm_rows(jax.random.fold_in(key, 31))


def draw_norm_average(key, part):
    return norm_rows(jax.random.fold_in(key, 32))


def shard_levels(stream_key, shape, split, low, largest):
    level = 1.0
    for axis_at, parts in split:
        steps = jax.random.uniform(jax.random.fold_in(jax.random.fold_in(stream_key, 6), axis_at), (parts,), jnp.float32, low / len(split), largest / len(split))
        level = level * jnp.repeat(jnp.exp(steps), shape[axis_at] // parts).reshape((-1,) + (1,) * (len(shape) - 1 - axis_at))
    return level


def scatter_about(rng, extent, scale, bound, shards=(), kind=jnp.bfloat16):
    drawn = jax.random.normal(rng, extent, jnp.float32) * scale
    if len(shards) > 0:
        drawn = shard_levels(rng, extent, shards, -0.22, 0.18) * drawn
    return jnp.clip(drawn, min=-bound, max=bound).astype(kind)


def setup_inputs(seed: int = 0) -> dict:
    streams_of = jax.random.split(jax.random.key(seed), 19)
    frames = scatter_about(streams_of[0], (LEN, UTTS, D), 1.0, 6.0, ((0, 4), (1, 8)))
    cotangent = scatter_about(streams_of[1], (LEN, UTTS, D), 1.0, 6.0, ((0, 4), (1, 8)))
    lengths = draw_lengths(jax.random.fold_in(streams_of[18], 71), 0)
    weight_project = scatter_about(streams_of[3], (3, D, D), D ** -0.5, 0.25, ((1, 8), (2, 4)), jnp.float32)
    weight_combine = scatter_about(streams_of[4], (D, D), (D // 4) ** -0.5, 0.5, ((0, 8), (1, 4)), jnp.float32)
    weight_expand = scatter_about(streams_of[5], (D, FF), D ** -0.5, 0.25, ((0, 8), (1, 4)), jnp.float32)
    weight_reduce = scatter_about(streams_of[6], (D, FF), FF ** -0.5, 0.125, ((0, 8), (1, 4)), jnp.float32)
    moment_project = scatter_about(streams_of[7], (3, D, D), ((UTT_DEV * N_DP * LEN // 4) ** 0.5), 512.0, ((1, 8), (2, 4)), jnp.float32)
    moment_combine = scatter_about(streams_of[8], (D, D), ((UTT_DEV * N_DP * LEN // 4) ** 0.5), 512.0, ((0, 8), (1, 4)), jnp.float32)
    moment_expand = scatter_about(streams_of[9], (D, FF), (0.5 * (UTT_DEV * N_DP * LEN // 4) ** 0.5), 256.0, ((0, 8), (1, 4)), jnp.float32)
    moment_reduce = scatter_about(streams_of[10], (D, FF), ((UTT_DEV * N_DP * LEN // 4) ** 0.5), 512.0, ((0, 8), (1, 4)), jnp.float32)
    average_project = scatter_about(streams_of[11], (3, D, D), D ** -0.5, 0.25, ((1, 8), (2, 4)), jnp.float32)
    average_combine = scatter_about(streams_of[12], (D, D), (D // 4) ** -0.5, 0.5, ((0, 8), (1, 4)), jnp.float32)
    average_expand = scatter_about(streams_of[13], (D, FF), D ** -0.5, 0.25, ((0, 8), (1, 4)), jnp.float32)
    average_reduce = scatter_about(streams_of[14], (D, FF), FF ** -0.5, 0.125, ((0, 8), (1, 4)), jnp.float32)
    norm_params = draw_norm_params(jax.random.fold_in(streams_of[18], 71), 0)
    norm_moment = scatter_about(streams_of[16], (4, D), ((UTT_DEV * N_DP * LEN // 4) ** 0.5), 512.0, (), jnp.float32)
    norm_average = draw_norm_average(jax.random.fold_in(streams_of[18], 71), 0)
    return {"frames": frames, "cotangent": cotangent, "lengths": lengths, "weight_project": weight_project, "weight_combine": weight_combine, "weight_expand": weight_expand, "weight_reduce": weight_reduce, "moment_project": moment_project, "moment_combine": moment_combine, "moment_expand": moment_expand, "moment_reduce": moment_reduce, "average_project": average_project, "average_combine": average_combine, "average_expand": average_expand, "average_reduce": average_reduce, "norm_params": norm_params, "norm_moment": norm_moment, "norm_average": norm_average}


eps_norm = 1e-05
momentum_decay = 0.9
average_decay = 0.6
matrix_rate = 0.0001
norm_rate = 0.001
key_margin = 128
masked_score = -1e+30
highest = lax.Precision.HIGHEST

@jax.custom_vjp
def low(v):
    return lax.optimization_barrier(v.astype(jnp.bfloat16)).astype(jnp.float32)

@jax.custom_vjp
def low_back(v):
    return v

def low_keep(v):
    return (low(v), None)

def low_pass(kept, grad):
    return (grad,)

def back_keep(v):
    return (v, None)

def back_low(kept, grad):
    return (low(grad),)
low.defvjp(low_keep, low_pass)
low_back.defvjp(back_keep, back_low)

def layer_norm(values, gain, shift):
    center = values - lax.optimization_barrier(jnp.mean(values, axis=-1, keepdims=True))
    spread = lax.optimization_barrier(jnp.mean(center * center, axis=-1, keepdims=True))
    return center * lax.rsqrt(spread + eps_norm) * gain + shift

def allowed_mask(offset, rows, lengths):
    query_time = offset + jnp.arange(rows, dtype=jnp.int32)
    key_time = offset - key_margin + jnp.arange(rows + key_margin, dtype=jnp.int32)
    behind = query_time[:, None] - key_time[None, :]
    nearby = (behind >= 0) & (behind <= WINDOW) & (key_time >= 0)[None, :]
    inside = (key_time[None, None, :] < lengths[:, None, None]) | (behind == 0)[None]
    return nearby[None] & inside

def attention(queries, keyset, valset, lengths):
    margin = jnp.zeros((key_margin,) + keyset.shape[1:], jnp.float32)
    key_pad = jnp.concatenate([margin, keyset], axis=0)
    value_pad = jnp.concatenate([margin, valset], axis=0)
    scale = 1.0 / math.sqrt(HEAD_DIM)

    def one_block(offset):
        block_queries = lax.dynamic_slice_in_dim(queries, offset, QBLK, 0)
        block_keys = lax.dynamic_slice_in_dim(key_pad, offset, QBLK + key_margin, 0)
        block_values = lax.dynamic_slice_in_dim(value_pad, offset, QBLK + key_margin, 0)
        scores = jnp.einsum('quhe,kuhe->uhqk', block_queries, block_keys, precision=highest)
        scores = low_back(scores * scale)
        allowed = allowed_mask(offset, QBLK, lengths)
        scores = jnp.where(allowed[:, None], scores, masked_score)
        weights = low(jax.nn.softmax(scores, axis=-1))
        return jnp.einsum('uhqk,kuhe->quhe', weights, block_values, precision=highest)
    offsets = jnp.arange(LEN // QBLK, dtype=jnp.int32) * QBLK
    blocks = lax.map(jax.checkpoint(one_block), offsets)
    return blocks.reshape(queries.shape)

def forward(frames32, weight_project, weight_combine, weight_expand, weight_reduce, norm_params, lengths):
    project_b = low(weight_project)
    combine_b = low(weight_combine)
    expand_b = low(weight_expand)
    reduce_b = low(weight_reduce)
    normed_one = low(layer_norm(frames32, norm_params[0], norm_params[1]))
    projected = jnp.einsum('tud,cde->ctue', normed_one, project_b, precision=highest)
    projected = low(low_back(projected))
    split_heads = projected.reshape(3, LEN, UTTS, HEADS, HEAD_DIM)
    mixed = attention(split_heads[0], split_heads[1], split_heads[2], lengths)
    mixed = low(low_back(mixed.reshape(LEN, UTTS, D)))
    attended = low_back(jnp.einsum('tuc,dc->tud', mixed, combine_b, precision=highest))
    residual = frames32 + attended
    normed_two = low(layer_norm(residual, norm_params[2], norm_params[3]))
    expanded = low_back(jnp.einsum('tud,df->tuf', normed_two, expand_b, precision=highest))
    activated = low(jax.nn.gelu(expanded))
    return residual + jnp.einsum('tuf,df->tud', activated, reduce_b, precision=highest)

def advance(weight, gradient, moment, average, rate):
    momentum = momentum_decay * moment + gradient
    updated = weight - rate * (gradient + momentum_decay * momentum)
    smoothed = average_decay * average + (1.0 - average_decay) * updated
    return (momentum, smoothed, updated)

def reference(frames, cotangent, lengths, weight_project, weight_combine, weight_expand, weight_reduce, moment_project, moment_combine, moment_expand, moment_reduce, average_project, average_combine, average_expand, average_reduce, norm_params, norm_moment, norm_average):
    frames32 = frames.astype(jnp.float32)

    def closed(inputs, project, combine, expand, reduce_w, norms):
        return forward(inputs, project, combine, expand, reduce_w, norms, lengths)
    result, pull = jax.vjp(closed, frames32, weight_project, weight_combine, weight_expand, weight_reduce, norm_params)
    valid = jnp.arange(LEN, dtype=jnp.int32)[:, None] < lengths[None, :]
    seed_grad = jnp.where(valid[:, :, None], cotangent.astype(jnp.float32), 0.0)
    input_gradient, grad_project, grad_combine, grad_expand, grad_reduce, grad_norms = pull(seed_grad)
    mom_p, avg_p, new_p = advance(weight_project, grad_project, moment_project, average_project, matrix_rate)
    mom_c, avg_c, new_c = advance(weight_combine, grad_combine, moment_combine, average_combine, matrix_rate)
    mom_e, avg_e, new_e = advance(weight_expand, grad_expand, moment_expand, average_expand, matrix_rate)
    mom_r, avg_r, new_r = advance(weight_reduce, grad_reduce, moment_reduce, average_reduce, matrix_rate)
    mom_n, avg_n, new_n = advance(norm_params, grad_norms, norm_moment, norm_average, norm_rate)
    return (result.astype(jnp.bfloat16), input_gradient, grad_project, grad_combine, grad_expand, grad_reduce, mom_p, mom_c, mom_e, mom_r, avg_p, avg_c, avg_e, avg_r, new_p, new_c, new_e, new_r, new_p.astype(jnp.bfloat16), new_c.astype(jnp.bfloat16), new_e.astype(jnp.bfloat16), new_r.astype(jnp.bfloat16), grad_norms, mom_n, avg_n, new_n)
```

```python
import math

import jax
import jax.numpy as jnp
from jax import lax
from jax.experimental import pallas as pl
from jax.experimental.pallas import tpu as pltpu
from jax.sharding import PartitionSpec as P

HEADS = 8
HEAD_DIM = 64
WINDOW = 10
HALO = 16

eps_norm = 1e-05
momentum_decay = 0.9
average_decay = 0.6
matrix_rate = 0.0001
norm_rate = 0.001
masked_score = -1e30

GROUP = 4
LANES = GROUP * HEAD_DIM
QUERIES = 112
KEYS = QUERIES + HALO
VMEM_LIMIT = 56 * 1024 * 1024

f32 = jnp.float32
bf16 = jnp.bfloat16


def mm(a, b):
    return lax.dot_general(a, b, (((1,), (0,)), ((), ())), preferred_element_type=f32)


def mm_bt(a, b):
    return lax.dot_general(a, b, (((1,), (1,)), ((), ())), preferred_element_type=f32)


def mm_at(a, b):
    return lax.dot_general(a, b, (((0,), (0,)), ((), ())), preferred_element_type=f32)


def normalise(values):
    center = values - jnp.mean(values, axis=-1, keepdims=True)
    spread = jnp.mean(center * center, axis=-1, keepdims=True)
    inverse = lax.rsqrt(spread + eps_norm)
    return center * inverse, inverse


def norm_backward(values, gain, upstream):
    scaled, inverse = normalise(values)
    weighted = upstream * gain
    inner = (
        weighted
        - jnp.mean(weighted, axis=-1, keepdims=True)
        - scaled * jnp.mean(weighted * scaled, axis=-1, keepdims=True)
    )
    return inner * inverse, upstream * scaled


def query_blocks(total):
    blocks = []
    at = HALO
    while at < total:
        rows = min(QUERIES, total - at)
        blocks.append((at, rows, min(at - HALO, total - KEYS)))
        at += rows
    return blocks


def band(block, start, length):
    q0, rows, k0 = block
    query = lax.broadcasted_iota(jnp.int32, (rows, KEYS), 0)
    key = lax.broadcasted_iota(jnp.int32, (rows, KEYS), 1)
    behind = query - key + (q0 - k0)
    time = key + (start + k0 - HALO)
    inside = (time < length) | (behind == 0)
    return (behind >= 0) & (behind <= WINDOW) & (time >= 0) & inside


def head_lanes():
    lane = lax.broadcasted_iota(jnp.int32, (1, LANES), 1)
    return [(lane >= h * HEAD_DIM) & (lane < (h + 1) * HEAD_DIM) for h in range(GROUP)]


def stack_heads(block):
    zero = jnp.zeros_like(block)
    return jnp.concatenate([jnp.where(m, block, zero) for m in head_lanes()], axis=0)


def merge_heads(stacked, rows):
    masks = head_lanes()
    out = jnp.where(masks[0], stacked[:rows], 0.0)
    for h in range(1, GROUP):
        out = jnp.where(masks[h], stacked[h * rows : (h + 1) * rows], out)
    return out


def softmax_rows(scores, allowed):
    scores = jnp.where(allowed, scores * (1.0 / math.sqrt(HEAD_DIM)), masked_score)
    raised = jnp.exp(scores - jnp.max(scores, axis=-1, keepdims=True))
    return raised / jnp.sum(raised, axis=-1, keepdims=True)


def place_weights(wa_ref, wb_ref, wp_ref, wc_ref):
    parts, cols = wa_ref.shape[1], wa_ref.shape[3]
    width = wc_ref.shape[1]
    for m in range(parts):
        at = m * cols
        wp_ref[:, at : at + cols] = wa_ref[0, m]
        wp_ref[:, width + at : width + at + cols] = wa_ref[1, m]
        wp_ref[:, 2 * width + at : 2 * width + at + cols] = wb_ref[0, m]
        wc_ref[:, at : at + cols] = wb_ref[1, m]


def attend_kernel(
    place_ref, frames_ref, wa_ref, wb_ref, norms_ref,
    qkv_ref, first_ref, mixed_ref, residual_ref, second_ref, wp_ref, wc_ref,
):
    batch, total, width = frames_ref.shape
    place_weights(wa_ref, wb_ref, wp_ref, wc_ref)
    start = place_ref[0]

    def one(u, carry):
        frames = frames_ref[u].astype(f32)
        scaled, _ = normalise(frames)
        normed = (scaled * norms_ref[0:1] + norms_ref[1:2]).astype(bf16)
        first_ref[u] = normed[HALO : total - HALO]
        qkv_ref[u] = mm(normed, wp_ref[...]).astype(bf16)
        length = place_ref[1 + u]
        for block in query_blocks(total):
            q0, rows, k0 = block
            allowed = band(block, start, length)
            for at in range(0, width, LANES):
                queries = stack_heads(qkv_ref[u, q0 : q0 + rows, at : at + LANES])
                keys = qkv_ref[u, k0 : k0 + KEYS, width + at : width + at + LANES]
                values = qkv_ref[u, k0 : k0 + KEYS, 2 * width + at : 2 * width + at + LANES]
                scores = mm_bt(queries, keys)
                probs = jnp.concatenate(
                    [
                        softmax_rows(scores[h * rows : (h + 1) * rows], allowed).astype(bf16)
                        for h in range(GROUP)
                    ],
                    axis=0,
                )
                out = merge_heads(mm(probs, values), rows)
                mixed_ref[u, q0 - HALO : q0 - HALO + rows, at : at + LANES] = out.astype(bf16)
        residual = frames_ref[u, HALO:total].astype(f32) + mm_bt(mixed_ref[u], wc_ref[...])
        residual_ref[u] = residual
        scaled, _ = normalise(residual)
        second_ref[u] = (scaled * norms_ref[2:3] + norms_ref[3:4]).astype(bf16)
        return carry

    lax.fori_loop(0, batch, one, 0)


def feed_kernel(
    second_ref, seed_ref, residual_ref, we_ref, wr_ref,
    out_ref, back_ref, ge_ref, gr_ref, fed_ref, second_t_ref, seed_t_ref,
):
    step = pl.program_id(0)
    last = pl.num_programs(0) - 1
    batch, own = out_ref.shape[:2]

    @pl.when(step == 0)
    def _():
        for u in range(batch):
            second_t_ref[u] = second_ref[u, :own].T
            seed_t_ref[u] = seed_ref[u, :own].T
        fed_ref[...] = jnp.zeros_like(fed_ref)
        back_ref[...] = jnp.zeros_like(back_ref)

    we, wr = we_ref[...], wr_ref[...]
    for u in range(batch):
        value = mm(second_ref[u], we)
        slope = math.sqrt(2.0 / math.pi)
        square = value * value
        tanh = jnp.tanh(value * (slope + (slope * 0.044715) * square))
        half = 0.5 + 0.5 * tanh
        active = (value * half).astype(bf16)
        fed_ref[u] += mm_bt(active[:own], wr)
        grad = mm(seed_ref[u], wr)
        curve = half + (0.5 * value) * (1.0 - tanh * tanh) * (
            slope + (slope * 3.0 * 0.044715) * square
        )
        grad = (grad * curve).astype(bf16)
        back_ref[u] += mm_bt(grad, we)
        part_r = mm(seed_t_ref[u], active[:own])
        part_e = mm(second_t_ref[u], grad[:own])
        if u == 0:
            total_r, total_e = part_r, part_e
        else:
            total_r, total_e = total_r + part_r, total_e + part_e
    gr_ref[...] = total_r.astype(bf16)
    ge_ref[...] = total_e.astype(bf16)

    @pl.when(step == last)
    def _():
        out_ref[...] = (residual_ref[:, :own] + fed_ref[...]).astype(bf16)


def pull_kernel(
    place_ref, qkv_ref, first_ref, mixed_ref, residual_ref, back_ref, seed_ref, wc_ref, norms_ref,
    wide_ref, grad_ref, parts_a_ref, parts_b_ref, norm_ref, grad_kv_ref, mixed_g_ref, gp_ref, gc_ref,
):
    batch, total, _ = qkv_ref.shape
    width = wc_ref.shape[0]
    own = first_ref.shape[1]
    start = place_ref[0]
    gp_ref[...] = jnp.zeros_like(gp_ref)
    gc_ref[...] = jnp.zeros_like(gc_ref)
    norm_ref[...] = jnp.zeros_like(norm_ref)

    def one(u, carry):
        upstream = back_ref[u]
        back, gained = norm_backward(residual_ref[u], norms_ref[2:3], upstream)
        norm_ref[0:1] += jnp.sum(gained[:own], axis=0, keepdims=True)
        norm_ref[1:2] += jnp.sum(upstream[:own], axis=0, keepdims=True)
        wide = seed_ref[u].astype(f32) + back
        wide_ref[u] = wide[:own]
        low = wide.astype(bf16)
        gc_ref[...] += mm_at(low[:own], mixed_ref[u, :own])
        mixed_g_ref[...] = mm(low, wc_ref[...]).astype(bf16)
        grad_kv_ref[...] = jnp.zeros_like(grad_kv_ref)
        length = place_ref[1 + u]
        scale = 1.0 / math.sqrt(HEAD_DIM)
        for block in query_blocks(total):
            q0, rows, k0 = block
            allowed = band(block, start, length)
            for at in range(0, width, LANES):
                queries = stack_heads(qkv_ref[u, q0 : q0 + rows, at : at + LANES])
                keys = qkv_ref[u, k0 : k0 + KEYS, width + at : width + at + LANES]
                values = qkv_ref[u, k0 : k0 + KEYS, 2 * width + at : 2 * width + at + LANES]
                upper = stack_heads(mixed_g_ref[q0 - HALO : q0 - HALO + rows, at : at + LANES])
                scores = mm_bt(queries, keys)
                grad_probs = mm_bt(upper, values)
                low_probs, grad_scores = [], []
                for h in range(GROUP):
                    probs = softmax_rows(scores[h * rows : (h + 1) * rows], allowed)
                    grad = grad_probs[h * rows : (h + 1) * rows]
                    inner = jnp.sum(probs * grad, axis=-1, keepdims=True)
                    low_probs.append(probs.astype(bf16))
                    grad_scores.append((probs * (grad - inner)).astype(bf16))
                low_probs = jnp.concatenate(low_probs, axis=0)
                grad_scores = jnp.concatenate(grad_scores, axis=0)
                grad_q = merge_heads(mm(grad_scores, keys), rows) * scale
                mine = min(rows, HALO + own - q0)
                if mine > 0:
                    grad_ref[u, q0 - HALO : q0 - HALO + mine, at : at + LANES] = grad_q[:mine].astype(bf16)
                grad_kv_ref[k0 : k0 + KEYS, at : at + LANES] += mm_at(grad_scores, queries) * scale
                grad_kv_ref[k0 : k0 + KEYS, width + at : width + at + LANES] += mm_at(low_probs, upper)
        grad_ref[u, :, width:] = grad_kv_ref[HALO : HALO + own].astype(bf16)
        gp_ref[...] += mm_at(first_ref[u], grad_ref[u])
        return carry

    lax.fori_loop(0, batch, one, 0)
    parts, cols = parts_a_ref.shape[1], parts_a_ref.shape[3]
    for m in range(parts):
        at = m * cols
        parts_a_ref[0, m] = gp_ref[:, at : at + cols].astype(bf16)
        parts_a_ref[1, m] = gp_ref[:, width + at : width + at + cols].astype(bf16)
        parts_b_ref[0, m] = gp_ref[:, 2 * width + at : 2 * width + at + cols].astype(bf16)
        parts_b_ref[1, m] = gc_ref[:, at : at + cols].astype(bf16)


def finish_kernel(grad_ref, frames_ref, wide_ref, wp_ref, norms_ref, out_ref, norm_ref):
    batch, own = grad_ref.shape[:2]
    norm_ref[...] = jnp.zeros_like(norm_ref)

    def one(u, carry):
        upstream = mm_bt(grad_ref[u], wp_ref[...])
        back, gained = norm_backward(
            frames_ref[u, HALO : HALO + own].astype(f32), norms_ref[0:1], upstream
        )
        norm_ref[0:1] += jnp.sum(gained, axis=0, keepdims=True)
        norm_ref[1:2] += jnp.sum(upstream, axis=0, keepdims=True)
        out_ref[u] = wide_ref[u] + back
        return carry

    lax.fori_loop(0, batch, one, 0)


def params():
    return pltpu.CompilerParams(vmem_limit_bytes=VMEM_LIMIT)


VM = pl.BlockSpec(memory_space=pltpu.VMEM)
SM = pl.BlockSpec(memory_space=pltpu.SMEM)


def cost(flops, moved, exps=0):
    return pl.CostEstimate(flops=int(flops), bytes_accessed=int(moved), transcendentals=int(exps))


def swap(value, axis, bit):
    n = lax.axis_size(axis)
    return lax.ppermute(value, axis, [(i, i ^ (1 << bit)) for i in range(n)])


def dp_bits():
    return (lax.axis_size("dp") - 1).bit_length()


def order():
    return [("mp", 1), ("mp", 0)] + [("dp", b) for b in reversed(range(dp_bits()))]


def side(label):
    return (lax.axis_index(label[0]) >> label[1]) & 1


def gathered(value, steps):
    have = []
    for label in steps:
        got = swap(value, *label)
        high = side(label) == 1
        have = [other for other in order() if other in have or other == label]
        at = 1 + have.index(label)
        value = jnp.stack([jnp.where(high, got, value), jnp.where(high, value, got)], axis=at)
    k, rows, cols = value.shape[0], value.shape[-2], value.shape[-1]
    return value.reshape(k, lax.axis_size("mp"), lax.axis_size("dp") * rows, cols)


def scattered(value, steps):
    k, _, rows, cols = value.shape
    have = order()
    value = value.reshape(k, *[2] * len(have), rows // lax.axis_size("dp"), cols)
    for label in steps:
        at = 1 + have.index(label)
        mine = side(label)
        sent = lax.dynamic_index_in_dim(value, 1 - mine, at, keepdims=False).astype(bf16)
        kept = lax.dynamic_index_in_dim(value, mine, at, keepdims=False).astype(f32)
        value = kept + swap(sent, *label).astype(f32)
        have.remove(label)
    return value


def routes():
    far = [("dp", b) for b in reversed(range(1, dp_bits()))]
    one, two, core = ("mp", 1), ("dp", 0), ("mp", 0)
    out = ([*far, one, two, core], [*far, two, one, core])
    back = ([core, one, two, *reversed(far)], [core, two, one, *reversed(far)])
    return out, back


def summed(value):
    for label in order():
        value = value + swap(value, *label)
    return value


def advance(weight, gradient, moment, average, rate):
    momentum = momentum_decay * moment + gradient
    updated = weight - rate * (gradient + momentum_decay * momentum)
    smoothed = average_decay * average + (1.0 - average_decay) * updated
    return (momentum, smoothed, updated)


def on_device(
    frames,
    cotangent,
    lengths,
    weight_project,
    weight_combine,
    weight_expand,
    weight_reduce,
    moment_project,
    moment_combine,
    moment_expand,
    moment_reduce,
    average_project,
    average_combine,
    average_expand,
    average_reduce,
    norm_params,
    norm_moment,
    norm_average,
):
    own, batch, width = frames.shape
    total, rows = own + 2 * HALO, own + HALO
    parts, n_dp = lax.axis_size("mp"), lax.axis_size("dp")
    me = lax.axis_index("mp")
    start = me * own
    (out_a, out_b), (back_a, back_b) = routes()

    low_project = weight_project.astype(bf16)
    project_a = gathered(low_project[:2], out_a)
    project_b = gathered(
        jnp.concatenate([low_project[2:], weight_combine.astype(bf16)[None]], axis=0), out_b
    )
    frames_u = jnp.transpose(frames, (1, 0, 2))
    cotangent_u = jnp.transpose(cotangent, (1, 0, 2))
    left = lax.ppermute(frames_u[:, own - HALO :], "mp", [(i, i + 1) for i in range(parts - 1)])
    right = lax.ppermute(
        jnp.stack([frames_u[:, :HALO], cotangent_u[:, :HALO]]),
        "mp",
        [(i + 1, i) for i in range(parts - 1)],
    )
    frames_x = jnp.concatenate([left, frames_u, right[0]], axis=1)
    times = start + jnp.arange(rows, dtype=jnp.int32)
    valid = times[None, :] < lengths[:, None]
    seed = jnp.concatenate([cotangent_u, right[1]], axis=1)
    seed = jnp.where(valid[:, :, None], seed, jnp.zeros_like(seed))
    place = jnp.concatenate([start[None].astype(jnp.int32), lengths])

    expand = gathered(weight_expand.astype(bf16)[None], out_a)[0]
    reduce_w = gathered(weight_reduce.astype(bf16)[None], out_b)[0]

    qkv, first, mixed, residual, second, wp, wc = pl.pallas_call(
        attend_kernel,
        out_shape=(
            jax.ShapeDtypeStruct((batch, total, 3 * width), bf16),
            jax.ShapeDtypeStruct((batch, own, width), bf16),
            jax.ShapeDtypeStruct((batch, rows, width), bf16),
            jax.ShapeDtypeStruct((batch, rows, width), f32),
            jax.ShapeDtypeStruct((batch, rows, width), bf16),
            jax.ShapeDtypeStruct((width, 3 * width), bf16),
            jax.ShapeDtypeStruct((width, width), bf16),
        ),
        in_specs=[SM, VM, VM, VM, VM],
        out_specs=(VM,) * 7,
        compiler_params=params(),
        cost_estimate=cost(8e9, 12e6),
        name="attend",
    )(place, frames_x, project_a, project_b, norm_params)

    hidden = expand.shape[2]
    whole = lambda *shape: pl.BlockSpec(shape, lambda f: (0,) * len(shape))
    piece = pl.BlockSpec((None, width, hidden), lambda f: (f, 0, 0))
    layer, back, grad_e, grad_r = pl.pallas_call(
        feed_kernel,
        grid=(parts,),
        out_shape=(
            jax.ShapeDtypeStruct((batch, own, width), bf16),
            jax.ShapeDtypeStruct((batch, rows, width), f32),
            jax.ShapeDtypeStruct((parts, width, hidden), bf16),
            jax.ShapeDtypeStruct((parts, width, hidden), bf16),
        ),
        in_specs=[
            whole(batch, rows, width),
            whole(batch, rows, width),
            whole(batch, rows, width),
            piece,
            piece,
        ],
        out_specs=(whole(batch, own, width), whole(batch, rows, width), piece, piece),
        scratch_shapes=[
            pltpu.VMEM((batch, own, width), f32),
            pltpu.VMEM((batch, width, own), bf16),
            pltpu.VMEM((batch, width, own), bf16),
        ],
        compiler_params=params(),
        cost_estimate=cost(14e9, 20e6),
        name="feed",
    )(second, seed, residual, expand, reduce_w)

    gradient_expand = scattered(grad_e[None], back_a)[0]
    gradient_reduce = scattered(grad_r[None], back_b)[0]

    cols = width // parts
    wide, grad_p, parts_a, parts_b, norm_two = pl.pallas_call(
        pull_kernel,
        out_shape=(
            jax.ShapeDtypeStruct((batch, own, width), f32),
            jax.ShapeDtypeStruct((batch, own, 3 * width), bf16),
            jax.ShapeDtypeStruct((2, parts, width, cols), bf16),
            jax.ShapeDtypeStruct((2, parts, width, cols), bf16),
            jax.ShapeDtypeStruct((2, width), f32),
        ),
        in_specs=[SM] + [VM] * 8,
        out_specs=(VM,) * 5,
        scratch_shapes=[
            pltpu.VMEM((total, 2 * width), f32),
            pltpu.VMEM((rows, width), bf16),
            pltpu.VMEM((width, 3 * width), f32),
            pltpu.VMEM((width, width), f32),
        ],
        compiler_params=params(),
        cost_estimate=cost(12e9, 20e6),
        name="pull",
    )(place, qkv, first, mixed, residual, back, seed, wc, norm_params)

    sum_a = scattered(parts_a, back_a)
    sum_b = scattered(parts_b, back_b)

    grad_in, norm_one = pl.pallas_call(
        finish_kernel,
        out_shape=(
            jax.ShapeDtypeStruct((batch, own, width), f32),
            jax.ShapeDtypeStruct((2, width), f32),
        ),
        in_specs=[VM] * 5,
        out_specs=(VM, VM),
        compiler_params=params(),
        cost_estimate=cost(2e9, 10e6),
        name="finish",
    )(grad_p, frames_x, wide, wp, norm_params)

    norm_gradient = summed(jnp.concatenate([norm_one, norm_two], axis=0))
    layer_out = jnp.transpose(layer, (1, 0, 2))
    input_gradient = jnp.transpose(grad_in, (1, 0, 2))
    gradient_project = jnp.concatenate([sum_a, sum_b[:1]], axis=0)
    gradient_combine = sum_b[1]

    mom_project, avg_project, new_project = advance(
        weight_project, gradient_project, moment_project, average_project, matrix_rate
    )
    mom_combine, avg_combine, new_combine = advance(
        weight_combine, gradient_combine, moment_combine, average_combine, matrix_rate
    )
    mom_expand, avg_expand, new_expand = advance(
        weight_expand, gradient_expand, moment_expand, average_expand, matrix_rate
    )
    mom_reduce, avg_reduce, new_reduce = advance(
        weight_reduce, gradient_reduce, moment_reduce, average_reduce, matrix_rate
    )
    mom_norms, avg_norms, new_norms = advance(
        norm_params, norm_gradient, norm_moment, norm_average, norm_rate
    )
    return (
        layer_out,
        input_gradient,
        gradient_project,
        gradient_combine,
        gradient_expand,
        gradient_reduce,
        mom_project,
        mom_combine,
        mom_expand,
        mom_reduce,
        avg_project,
        avg_combine,
        avg_expand,
        avg_reduce,
        new_project,
        new_combine,
        new_expand,
        new_reduce,
        new_project.astype(bf16),
        new_combine.astype(bf16),
        new_expand.astype(bf16),
        new_reduce.astype(bf16),
        norm_gradient,
        mom_norms,
        avg_norms,
        new_norms,
    )


def solution(mesh):
    tokens = P("mp", "dp", None)
    stacked, matrix = P(None, "dp", "mp"), P("dp", "mp")
    weights = (stacked, matrix, matrix, matrix)
    in_specs = (tokens, tokens, P("dp")) + weights * 3 + (P(),) * 3
    out_specs = (tokens, tokens) + weights * 5 + (P(),) * 4
    return jax.shard_map(
        on_device, mesh=mesh, in_specs=in_specs, out_specs=out_specs, check_vma=False
    )
```

```python
import functools
import math

import jax
import jax.numpy as jnp
from jax import lax
from jax.experimental import pallas as pl
from jax.experimental.pallas import tpu as pltpu
from jax.sharding import PartitionSpec as P

HEADS = 8
HEAD_DIM = 64
WINDOW = 10
HALO = 16

eps_norm = 1e-05
momentum_decay = 0.9
average_decay = 0.6
matrix_rate = 0.0001
norm_rate = 0.001
masked_score = -1e30

GROUP = 4
LANES = GROUP * HEAD_DIM
QUERIES = 112
KEYS = QUERIES + HALO

f32 = jnp.float32
bf16 = jnp.bfloat16


def mm(a, b):
    return lax.dot_general(a, b, (((1,), (0,)), ((), ())), preferred_element_type=f32)


def mm_bt(a, b):
    return lax.dot_general(a, b, (((1,), (1,)), ((), ())), preferred_element_type=f32)


def mm_at(a, b):
    return lax.dot_general(a, b, (((0,), (0,)), ((), ())), preferred_element_type=f32)


def normalise(values):
    center = values - jnp.mean(values, axis=-1, keepdims=True)
    spread = jnp.mean(center * center, axis=-1, keepdims=True)
    inverse = lax.rsqrt(spread + eps_norm)
    return center * inverse, inverse


def norm_backward(values, gain, upstream):
    scaled, inverse = normalise(values)
    weighted = upstream * gain
    inner = (
        weighted
        - jnp.mean(weighted, axis=-1, keepdims=True)
        - scaled * jnp.mean(weighted * scaled, axis=-1, keepdims=True)
    )
    return inner * inverse, upstream * scaled


def query_blocks(total):
    blocks = []
    at = HALO
    while at < total:
        rows = min(QUERIES, total - at)
        blocks.append((at, rows, min(at - HALO, total - KEYS)))
        at += rows
    return blocks


def band(block, start, length):
    q0, rows, k0 = block
    query = lax.broadcasted_iota(jnp.int32, (rows, KEYS), 0)
    key = lax.broadcasted_iota(jnp.int32, (rows, KEYS), 1)
    behind = query - key + (q0 - k0)
    time = key + (start + k0 - HALO)
    inside = (time < length) | (behind == 0)
    return (behind >= 0) & (behind <= WINDOW) & (time >= 0) & inside


def head_lanes():
    lane = lax.broadcasted_iota(jnp.int32, (1, LANES), 1)
    return [(lane >= h * HEAD_DIM) & (lane < (h + 1) * HEAD_DIM) for h in range(GROUP)]


def stack_heads(block):
    zero = jnp.zeros_like(block)
    return jnp.concatenate([jnp.where(m, block, zero) for m in head_lanes()], axis=0)


def merge_heads(stacked, rows):
    masks = head_lanes()
    out = jnp.where(masks[0], stacked[:rows], 0.0)
    for h in range(1, GROUP):
        out = jnp.where(masks[h], stacked[h * rows : (h + 1) * rows], out)
    return out


def softmax_rows(scores, allowed):
    scores = jnp.where(allowed, scores * (1.0 / math.sqrt(HEAD_DIM)), masked_score)
    raised = jnp.exp(scores - jnp.max(scores, axis=-1, keepdims=True))
    return raised / jnp.sum(raised, axis=-1, keepdims=True)


def block_order(n_dp, near_first):
    bits = (n_dp // 2 - 1).bit_length()
    flip = [sum(((z >> b) & 1) << (bits - 1 - b) for b in range(bits)) for z in range(n_dp // 2)]
    if near_first:
        outer = [(x, y) for x in range(2) for y in range(2)]
    else:
        outer = [(x, y) for y in range(2) for x in range(2)]
    return [(y, 2 * z + x) for x, y in outer for z in flip]


def place_weights(n_dp, core, own_a, own_b, got_a, got_b, wp_ref, wc_ref):
    width, cols = wc_ref.shape[0], own_a.shape[1]
    r = width // n_dp
    for which, ref_a, ref_b in ((core, own_a, own_b), (1 - core, got_a, got_b)):
        for ref, first, near_first in ((ref_a, 0, True), (ref_b, 2, False)):
            for p, (y, d) in enumerate(block_order(n_dp, near_first)):
                at = pl.multiple_of((2 * y + which) * cols, cols)
                for i in range(2):
                    block = ref[(2 * p + i) * r : (2 * p + i + 1) * r]
                    if first + i < 3:
                        wp_ref[d * r : (d + 1) * r, pl.ds((first + i) * width + at, cols)] = block
                    else:
                        wc_ref[d * r : (d + 1) * r, pl.ds(at, cols)] = block


def attend_one(
    u, place_ref, frames_ref, norms_ref, wp_ref, wc_ref,
    qkv_ref, first_ref, mixed_ref, residual_ref, second_ref, second_t_ref,
):
    total, width = frames_ref.shape
    own = first_ref.shape[0]
    start, length = place_ref[0], place_ref[2 + u]
    scaled, _ = normalise(frames_ref[...].astype(f32))
    normed = (scaled * norms_ref[0:1] + norms_ref[1:2]).astype(bf16)
    first_ref[...] = normed[HALO : HALO + own]
    qkv_ref[...] = mm(normed, wp_ref[...]).astype(bf16)
    for block in query_blocks(total):
        q0, rows, k0 = block
        allowed = band(block, start, length)
        for at in range(0, width, LANES):
            queries = stack_heads(qkv_ref[q0 : q0 + rows, at : at + LANES])
            keys = qkv_ref[k0 : k0 + KEYS, width + at : width + at + LANES]
            values = qkv_ref[k0 : k0 + KEYS, 2 * width + at : 2 * width + at + LANES]
            scores = mm_bt(queries, keys)
            probs = jnp.concatenate(
                [
                    softmax_rows(scores[h * rows : (h + 1) * rows], allowed).astype(bf16)
                    for h in range(GROUP)
                ],
                axis=0,
            )
            out = merge_heads(mm(probs, values), rows)
            mixed_ref[q0 - HALO : q0 - HALO + rows, at : at + LANES] = out.astype(bf16)
    residual = frames_ref[HALO:total].astype(f32) + mm_bt(mixed_ref[...], wc_ref[...])
    residual_ref[...] = residual
    scaled, _ = normalise(residual)
    second_ref[...] = (scaled * norms_ref[2:3] + norms_ref[3:4]).astype(bf16)
    second_t_ref[...] = second_ref[:own].T


def attend_first_kernel(
    n_dp, place_ref, frames_ref, norms_ref, own_a, own_b, got_a, got_b, *refs
):
    *outs, wp_ref, wc_ref = refs
    place_weights(n_dp, place_ref[1], own_a, own_b, got_a, got_b, wp_ref, wc_ref)
    attend_one(0, place_ref, frames_ref, norms_ref, wp_ref, wc_ref, *outs)


def attend_next_kernel(place_ref, frames_ref, norms_ref, wp_ref, wc_ref, *refs):
    attend_one(1, place_ref, frames_ref, norms_ref, wp_ref, wc_ref, *refs)


def gelu_parts(value):
    slope = math.sqrt(2.0 / math.pi)
    square = value * value
    tanh = jnp.tanh(value * (slope + (slope * 0.044715) * square))
    half = 0.5 + 0.5 * tanh
    curve = half + (0.5 * value) * (1.0 - tanh * tanh) * (
        slope + (slope * 3.0 * 0.044715) * square
    )
    return value * half, curve


def feed_half(
    n_dp, seconds, seconds_t, seed_ref, seed_t_ref, we_ref, wr_ref, ge_ref, gr_ref,
    wide_e, wide_r, active_ref, grad_ref, add_fed, add_back,
):
    own = seconds_t[0].shape[1]
    width, hidden = wide_e.shape[0], we_ref.shape[1]
    r = width // n_dp
    for ref, wide, near_first in ((we_ref, wide_e, True), (wr_ref, wide_r, False)):
        for p, (y, d) in enumerate(block_order(n_dp, near_first)):
            wide[d * r : (d + 1) * r, y * hidden : (y + 1) * hidden] = ref[p * r : (p + 1) * r]
    for u, second_ref in enumerate(seconds):
        rows = slice(u * own, (u + 1) * own)
        active, curve = gelu_parts(mm(second_ref[...], wide_e[...]))
        active_ref[rows] = active[:own].astype(bf16)
        grad_ref[u] = (mm(seed_ref[u], wide_r[...]) * curve).astype(bf16)
        add_fed(u, mm_bt(active_ref[rows], wide_r[...]))
        add_back(u, mm_bt(grad_ref[u], wide_e[...]))
    total_r = mm(seed_t_ref[...], active_ref[...])
    total_e = mm(seconds_t[0][...], grad_ref[0, :own]) + mm(seconds_t[1][...], grad_ref[1, :own])
    for total, ref, near_first in ((total_e, ge_ref, True), (total_r, gr_ref, False)):
        for p, (y, d) in enumerate(block_order(n_dp, near_first)):
            block = total[d * r : (d + 1) * r, y * hidden : (y + 1) * hidden]
            ref[p * r : (p + 1) * r] = block.astype(bf16)


def feed_first_kernel(n_dp, we_ref, wr_ref, n0, seed_ref, n1, seed_t_ref, t0, t1, *refs):
    fed_ref, back_ref, ge_ref, gr_ref, *scratch = refs

    def add_fed(u, value):
        fed_ref[u] = value

    def add_back(u, value):
        back_ref[u] = value

    feed_half(
        n_dp, (n0, n1), (t0, t1), seed_ref, seed_t_ref, we_ref, wr_ref, ge_ref, gr_ref,
        *scratch, add_fed, add_back,
    )


def feed_last_kernel(
    n_dp, we_ref, wr_ref, n0, seed_ref, fed_in, back_in, n1, r0, r1, seed_t_ref, t0, t1, *refs
):
    out_ref, back_ref, ge_ref, gr_ref, *scratch = refs
    own = out_ref.shape[1]

    def add_fed(u, value):
        out_ref[u] = ((r0, r1)[u][:own] + (fed_in[u] + value)).astype(bf16)

    def add_back(u, value):
        back_ref[u] = back_in[u] + value

    feed_half(
        n_dp, (n0, n1), (t0, t1), seed_ref, seed_t_ref, we_ref, wr_ref, ge_ref, gr_ref,
        *scratch, add_fed, add_back,
    )


def pull_one(
    u, place_ref, back_ref, residual_ref, seed_ref, wc_ref, norms_ref, qkv_ref,
    wide_ref, low_ref, grad_ref, norm_ref, grad_kv_ref, mixed_g_ref,
):
    total = qkv_ref.shape[0]
    own, width = low_ref.shape
    start, length = place_ref[0], place_ref[2 + u]
    upstream = back_ref[u]
    back, gained = norm_backward(residual_ref[...], norms_ref[2:3], upstream)
    norm_ref[0:1] = jnp.sum(gained[:own], axis=0, keepdims=True)
    norm_ref[1:2] = jnp.sum(upstream[:own], axis=0, keepdims=True)
    wide = seed_ref[u].astype(f32) + back
    wide_ref[...] = wide[:own]
    low = wide.astype(bf16)
    low_ref[...] = low[:own]
    mixed_g_ref[...] = mm(low, wc_ref[...]).astype(bf16)
    grad_kv_ref[...] = jnp.zeros_like(grad_kv_ref)
    scale = 1.0 / math.sqrt(HEAD_DIM)
    for block in query_blocks(total):
        q0, rows, k0 = block
        allowed = band(block, start, length)
        for at in range(0, width, LANES):
            queries = stack_heads(qkv_ref[q0 : q0 + rows, at : at + LANES])
            keys = qkv_ref[k0 : k0 + KEYS, width + at : width + at + LANES]
            values = qkv_ref[k0 : k0 + KEYS, 2 * width + at : 2 * width + at + LANES]
            upper = stack_heads(mixed_g_ref[q0 - HALO : q0 - HALO + rows, at : at + LANES])
            scores = mm_bt(queries, keys)
            grad_probs = mm_bt(upper, values)
            low_probs, grad_scores = [], []
            for h in range(GROUP):
                probs = softmax_rows(scores[h * rows : (h + 1) * rows], allowed)
                grad = grad_probs[h * rows : (h + 1) * rows]
                inner = jnp.sum(probs * grad, axis=-1, keepdims=True)
                low_probs.append(probs.astype(bf16))
                grad_scores.append((probs * (grad - inner)).astype(bf16))
            low_probs = jnp.concatenate(low_probs, axis=0)
            grad_scores = jnp.concatenate(grad_scores, axis=0)
            grad_q = merge_heads(mm(grad_scores, keys), rows) * scale
            mine = min(rows, HALO + own - q0)
            if mine > 0:
                grad_ref[q0 - HALO : q0 - HALO + mine, at : at + LANES] = grad_q[:mine].astype(bf16)
            grad_kv_ref[k0 : k0 + KEYS, at : at + LANES] += mm_at(grad_scores, queries) * scale
            grad_kv_ref[k0 : k0 + KEYS, width + at : width + at + LANES] += mm_at(low_probs, upper)
    grad_ref[:, width:] = grad_kv_ref[HALO : HALO + own].astype(bf16)


def pull_first_kernel(*refs):
    pull_one(0, *refs)


def pull_last_kernel(
    n_dp, place_ref, back_ref, residual_ref, seed_ref, wc_ref, norms_ref, qkv_ref,
    first_0, first_1, mixed_0, mixed_1, grad_0, low_0, *refs,
):
    wide_ref, low_ref, grad_ref, norm_ref, keep_a, keep_b, send_a, send_b, grad_kv_ref, mixed_g_ref, gp_ref = refs
    pull_one(
        1, place_ref, back_ref, residual_ref, seed_ref, wc_ref, norms_ref, qkv_ref,
        wide_ref, low_ref, grad_ref, norm_ref, grad_kv_ref, mixed_g_ref,
    )
    own, width = low_ref.shape
    gp_ref[:, : 3 * width] = mm_at(first_0[...], grad_0[...]) + mm_at(first_1[...], grad_ref[...])
    gp_ref[:, 3 * width :] = mm_at(low_0[...], mixed_0[:own]) + mm_at(low_ref[...], mixed_1[:own])
    cols, r = keep_a.shape[1], width // n_dp
    core = place_ref[1]
    for which, ref_a, ref_b in ((core, keep_a, keep_b), (1 - core, send_a, send_b)):
        for ref, first, near_first in ((ref_a, 0, True), (ref_b, 2, False)):
            for p, (y, d) in enumerate(block_order(n_dp, near_first)):
                at = pl.multiple_of((2 * y + which) * cols, cols)
                for i in range(2):
                    block = gp_ref[d * r : (d + 1) * r, pl.ds((first + i) * width + at, cols)]
                    ref[(2 * p + i) * r : (2 * p + i + 1) * r] = block.astype(bf16)


def fold_norm(ref, first, value):
    cols = ref.shape[1]
    for j in range(value.shape[1] // cols):
        ref[4 * j + first : 4 * j + first + value.shape[0]] = value[:, j * cols : (j + 1) * cols]


def finish_kernel(norms_ref, wp_ref, grad_0, frames_0, wide_0, grad_1, frames_1, wide_1, norm_0, norm_1, out_0, out_1, norm_ref):
    own = out_0.shape[0]
    gains, shifts = [], []
    for grad_ref, frames_ref, wide_ref, out_ref in (
        (grad_0, frames_0, wide_0, out_0),
        (grad_1, frames_1, wide_1, out_1),
    ):
        upstream = mm_bt(grad_ref[...], wp_ref[...])
        back, gained = norm_backward(
            frames_ref[HALO : HALO + own].astype(f32), norms_ref[0:1], upstream
        )
        gains.append(jnp.sum(gained, axis=0, keepdims=True))
        shifts.append(jnp.sum(upstream, axis=0, keepdims=True))
        out_ref[...] = wide_ref[...] + back
    fold_norm(norm_ref, 0, gains[0] + gains[1])
    fold_norm(norm_ref, 1, shifts[0] + shifts[1])
    fold_norm(norm_ref, 2, norm_0[...] + norm_1[...])


VM = pl.BlockSpec(memory_space=pltpu.VMEM)
SM = pl.BlockSpec(memory_space=pltpu.SMEM)
MIB = 1024 * 1024


def call(kernel, ins, outs, scratch=(), waits=(), flops=1e9, smem=1, mib=16):
    n, m = len(ins), len(outs)

    def body(*refs):
        kernel(*refs[:n], *refs[n + len(waits) :])

    return pl.pallas_call(
        body,
        out_shape=tuple(jax.ShapeDtypeStruct(shape, kind) for shape, kind in outs),
        in_specs=[SM] * smem + [VM] * (n - smem) + [pl.BlockSpec(memory_space=pl.ANY)] * len(waits),
        out_specs=(VM,) * m,
        scratch_shapes=[pltpu.VMEM(shape, kind) for shape, kind in scratch],
        compiler_params=pltpu.CompilerParams(vmem_limit_bytes=mib * MIB),
        cost_estimate=pl.CostEstimate(flops=int(flops), bytes_accessed=6000000, transcendentals=0),
    )(*ins, *waits)


def swap(value, axis, bit):
    n = lax.axis_size(axis)
    return lax.ppermute(value, axis, [(i, i ^ (1 << bit)) for i in range(n)])


CORE, ROW, NEAR = ("mp", 0), ("mp", 1), ("dp", 0)


def far():
    return [("dp", b) for b in range(1, (lax.axis_size("dp") - 1).bit_length())]


def side(label):
    return (lax.axis_index(label[0]) >> label[1]) & 1


def spot(label):
    return {CORE: 1, ROW: 4, NEAR: 5}.get(label, 5 + label[1])


def paired(place, streams, waits=()):
    def kernel(place_ref, *refs):
        outs = list(refs[2 * len(streams) :])
        for i, (_, _, label, parts) in enumerate(streams):
            mine, got = refs[2 * i], refs[2 * i + 1]
            high = place_ref[spot(label)]
            for part in range(parts):
                out = outs.pop(0)
                out[high] = mine[:, part]
                out[1 - high] = got[:, part]

    ins, outs = [place], []
    for mine, got, label, parts in streams:
        blocks = lax.axis_size("dp") // 4 if parts > 1 else 1
        shape = (blocks, parts, mine.shape[0] // blocks // parts, mine.shape[1])
        ins += [mine.reshape(shape), got.reshape(shape)]
        outs += [((2, blocks, *shape[2:]), mine.dtype)] * parts
    return [x.reshape(-1, x.shape[-1]) for x in call(kernel, ins, outs, waits=waits, flops=1e8, mib=8)]


def lowered(arrays, waits):
    rows = [x.shape[0] for x in arrays]

    def kernel(*refs):
        at = 0
        for ref, count in zip(refs, rows):
            refs[-1][at : at + count] = ref[...].astype(bf16)
            at += count

    return call(kernel, arrays, [((sum(rows), arrays[0].shape[1]), bf16)], waits=waits, flops=1e8, smem=0, mib=8)[0]


def halved(place, streams, joint=False, waits=()):
    counts = [len(terms) for terms, _ in streams]
    n = len(streams)

    def kernel(place_ref, *refs):
        refs = list(refs)
        groups = [[refs.pop(0) for _ in range(count)] for count in counts]
        kept, sent = refs[:n], refs[n:]
        for i, (group, (_, label)) in enumerate(zip(groups, streams)):
            mine = place_ref[spot(label)]
            kept[i][...] = total([ref[mine] for ref in group])
            gone = total([ref[1 - mine] for ref in group]).astype(bf16)
            if joint:
                sent[0][i] = gone
            else:
                sent[i][...] = gone

    ins, keeps, sends = [place], [], []
    for terms, _ in streams:
        half, cols = terms[0].size // terms[0].shape[-1] // 2, terms[0].shape[-1]
        ins += [term.reshape(2, half, cols) for term in terms]
        keeps.append(((half, cols), f32))
        sends.append(((half, cols), bf16))
    if joint:
        sends = [((n, *sends[0][0]), bf16)]
    done = call(kernel, ins, keeps + sends, waits=waits, flops=1e8, mib=8)
    return done[:n], done[n:]


def halved_joint(place, keeps, got, label):
    n = len(keeps)
    half, cols = keeps[0].shape[0] // 2, keeps[0].shape[1]

    def kernel(place_ref, *refs):
        mine = place_ref[spot(label)]
        for i in range(n):
            kept = refs[i][mine] + refs[n][i, mine].astype(f32)
            gone = refs[i][1 - mine] + refs[n][i, 1 - mine].astype(f32)
            refs[n + 1 + i][...] = kept
            refs[2 * n + 1][i] = gone.astype(bf16)

    ins = [place, *[keep.reshape(2, half, cols) for keep in keeps], got.reshape(n, 2, half, cols)]
    done = call(kernel, ins, [((half, cols), f32)] * n + [((n, half, cols), bf16)], flops=1e8, mib=8)
    return done[:n], done[n]


def halved_norm(place, keeps, gots, labels, norms, joint):
    rows, cols = keeps[0].shape
    half, extra = rows // 2, norms[0].shape[0]
    n = len(gots)

    def kernel(place_ref, *refs):
        keep, got, norm, outs = refs[:2], refs[2 : 2 + n], refs[2 + n : -5 if not joint else -4], refs[-5 if not joint else -4 :]
        arrived = [(got[0], 0), (got[-1], 0 if n == 2 else rows)]
        for i in range(2):
            mine = place_ref[spot(labels[i])]
            ref, at = arrived[i]
            here = keep[i][pl.ds(pl.multiple_of(mine * half, half), half)].astype(f32)
            there = keep[i][pl.ds(pl.multiple_of((1 - mine) * half, half), half)].astype(f32)
            here += ref[pl.ds(pl.multiple_of(at + mine * half, half), half)].astype(f32)
            there += ref[pl.ds(pl.multiple_of(at + (1 - mine) * half, half), half)].astype(f32)
            outs[i][...] = here
            if joint:
                outs[3][i * half : (i + 1) * half] = there.astype(bf16)
            else:
                outs[3 + i][:half] = there.astype(bf16)
        if len(norm) == 2:
            value = norm[0][...] + norm[1][...]
        else:
            ref, at = arrived[1]
            value = joined_norm(norm[0][...], ref[at + rows : at + rows + 2 * extra])
        outs[2][...] = value
        split_norm(value, outs[-1], 2 * half if joint else half)

    small = [((half, cols), f32)] * 2 + [((extra, cols), f32)]
    if joint:
        sends = [((2 * half + 2 * extra, cols), bf16)]
    else:
        sends = [((half, cols), bf16), ((half + 2 * extra, cols), bf16)]
    done = call(kernel, (place, *keeps, *gots, *norms), small + sends, flops=1e8, mib=8)
    return done[:2], done[2], done[3:]


def split_norm(value, ref, at):
    rows = value.shape[0]
    high = value.astype(bf16)
    ref[at : at + rows] = high
    ref[at + rows : at + 2 * rows] = (value - high.astype(f32)).astype(bf16)


def joined_norm(value, got):
    rows = value.shape[0]
    high = value.astype(bf16).astype(f32)
    low = (value - high).astype(bf16).astype(f32)
    return (high + low) + (got[:rows].astype(f32) + got[rows:].astype(f32))


def total(terms):
    terms = [term.astype(f32) for term in terms]
    return functools.reduce(jnp.add, terms)


def write_update(outs, at, gradient, states, rate):
    values = advance(*states[:1], gradient, *states[1:], rate)
    for out, value in zip(outs, (gradient, *values)):
        out[at] = value
    if len(outs) > 4:
        outs[4][at] = values[2].astype(bf16)


def update_feed_kernel(keep_e, keep_r, got_ref, *refs):
    states, outs = refs[:6], refs[6:]
    for i, keep in enumerate((keep_e, keep_r)):
        gradient = keep[...] + got_ref[i].astype(f32)
        state = [ref[...] for ref in states[3 * i : 3 * i + 3]]
        write_update(outs[5 * i : 5 * i + 5], slice(None), gradient, state, matrix_rate)


def update_rest_kernel(keep_a, keep_b, got_ref, norm_ref, *refs):
    states, outs = refs[:9], refs[9:]
    rows, cols = keep_a.shape
    r, extra = rows // 2, norm_ref.shape[0]
    for i in range(4):
        keep = (keep_a, keep_b)[i // 2]
        at = (i % 2) * r
        gradient = keep[at : at + r] + got_ref[i * r : (i + 1) * r].astype(f32)
        which, entry = (0, i) if i < 3 else (1, slice(None))
        state = [ref[entry] for ref in states[3 * which : 3 * which + 3]]
        write_update(outs[5 * which : 5 * which + 5], entry, gradient, state, matrix_rate)
    value = joined_norm(norm_ref[...], got_ref[2 * rows : 2 * rows + 2 * extra])
    for j in range(extra // 4):
        at = (slice(None), slice(j * cols, (j + 1) * cols))
        state = [ref[at] for ref in states[6:]]
        write_update(outs[10:], at, value[4 * j : 4 * j + 4], state, norm_rate)


def advance(weight, gradient, moment, average, rate):
    momentum = momentum_decay * moment + gradient
    updated = weight - rate * (gradient + momentum_decay * momentum)
    smoothed = average_decay * average + (1.0 - average_decay) * updated
    return (momentum, smoothed, updated)


def on_device(
    frames,
    cotangent,
    lengths,
    weight_project,
    weight_combine,
    weight_expand,
    weight_reduce,
    moment_project,
    moment_combine,
    moment_expand,
    moment_reduce,
    average_project,
    average_combine,
    average_expand,
    average_reduce,
    norm_params,
    norm_moment,
    norm_average,
):
    own, batch, width = frames.shape
    long, rows = own + 2 * HALO, own + HALO
    parts, n_dp = lax.axis_size("mp"), lax.axis_size("dp")
    me = lax.axis_index("mp")
    start = me * own
    cols, hidden = width // parts, weight_expand.shape[1]
    r = width // n_dp

    sides = [side(label) for label in (ROW, NEAR, *far())]
    place = jnp.concatenate(
        [jnp.stack([start, side(CORE)]).astype(jnp.int32), lengths, jnp.stack(sides).astype(jnp.int32)]
    )
    *outer, last = reversed(far())

    matrices = jnp.concatenate([weight_project, weight_combine[None]], axis=0).astype(bf16)
    one = matrices.reshape(-1, cols)
    for label in outer:
        (one,) = paired(place, [(one, swap(one, *label), label, 1)])
    one_got = swap(one, *last)

    frames_u = jnp.transpose(frames, (1, 0, 2))
    cotangent_u = jnp.transpose(cotangent, (1, 0, 2))
    left = lax.ppermute(frames_u[:, own - HALO :], "mp", [(i, i + 1) for i in range(parts - 1)])
    right = lax.ppermute(
        jnp.stack([frames_u[:, :HALO], cotangent_u[:, :HALO]]),
        "mp",
        [(i + 1, i) for i in range(parts - 1)],
    )
    frames_x = [jnp.concatenate([left[u], frames_u[u], right[0, u]], axis=0) for u in range(batch)]
    times = start + jnp.arange(rows, dtype=jnp.int32)
    valid = times[None, :] < lengths[:, None]
    seed = jnp.concatenate([cotangent_u, right[1]], axis=1)
    seed = jnp.where(valid[:, :, None], seed, jnp.zeros_like(seed))
    seed_t = jnp.transpose(seed[:, :own], (2, 0, 1)).reshape(width, batch * own)

    one_a, one_b = paired(place, [(one, one_got, last, 2)], waits=(*frames_x, seed, seed_t))
    got_a, got_b = swap(one_a, *ROW), swap(one_b, *NEAR)
    two = lowered([weight_expand, weight_reduce], waits=(one_a,))
    one_a, one_b = paired(place, [(one_a, got_a, ROW, 1), (one_b, got_b, NEAR, 1)])
    got_a, got_b = swap(one_a, *NEAR), swap(one_b, *ROW)
    for label in outer:
        (two,) = paired(place, [(two, swap(two, *label), label, 1)], waits=(one_a,))
    two_got = swap(two, *last)
    one_a, one_b = paired(
        place, [(one_a, got_a, NEAR, 1), (one_b, got_b, ROW, 1)], waits=(two,)
    )
    core_a, core_b = swap(one_a, *CORE), swap(one_b, *CORE)
    two_a, two_b = paired(place, [(two, two_got, last, 2)], waits=(one_a,))

    per_u = [
        ((long, 3 * width), bf16),
        ((own, width), bf16),
        ((rows, width), bf16),
        ((rows, width), f32),
        ((rows, width), bf16),
        ((width, own), bf16),
    ]
    qkv_0, first_0, mixed_0, residual_0, second_0, second_t_0, wp, wc = call(
        functools.partial(attend_first_kernel, n_dp),
        (place, frames_x[0], norm_params, one_a, one_b, core_a, core_b),
        per_u + [((width, 3 * width), bf16), ((width, width), bf16)],
        waits=(two_a, two_b),
        flops=5e9,
    )
    got_a, got_b = swap(two_a, *ROW), swap(two_b, *NEAR)
    two_a, two_b = paired(place, [(two_a, got_a, ROW, 1), (two_b, got_b, NEAR, 1)], waits=(wc,))
    qkv_1, first_1, mixed_1, residual_1, second_1, second_t_1 = call(
        attend_next_kernel,
        (place, frames_x[1], norm_params, wp, wc),
        per_u,
        waits=(two_a, two_b),
        flops=5e9,
    )
    got_a, got_b = swap(two_a, *NEAR), swap(two_b, *ROW)
    expand, reduce_w = paired(
        place, [(two_a, got_a, NEAR, 1), (two_b, got_b, ROW, 1)], waits=(second_1,)
    )
    expand_got, reduce_got = swap(expand, *CORE), swap(reduce_w, *CORE)

    grads = [((2 * width, hidden), bf16)] * 2
    carried = [((batch, own, width), f32), ((batch, rows, width), f32)]
    feed_scratch = [((width, 2 * hidden), bf16)] * 2 + [
        ((batch * own, 2 * hidden), bf16),
        ((batch, rows, 2 * hidden), bf16),
    ]
    transposed = (seed_t, second_t_0, second_t_1)
    fed, back, keep_e, keep_r = call(
        functools.partial(feed_first_kernel, n_dp),
        (expand, reduce_w, second_0, seed, second_1, *transposed),
        carried + grads,
        feed_scratch,
        flops=8e9,
        smem=0,
    )
    layer, back, send_e, send_r = call(
        functools.partial(feed_last_kernel, n_dp),
        (expand_got, reduce_got, second_0, seed, fed, back, second_1, residual_0, residual_1, *transposed),
        [((batch, own, width), bf16), carried[1]] + grads,
        feed_scratch,
        flops=8e9,
        smem=0,
    )

    two_a, two_b = [keep_e, swap(send_e, *CORE)], [keep_r, swap(send_r, *CORE)]
    pulled = [((own, width), f32), ((own, width), bf16), ((own, 3 * width), bf16), ((2, width), f32)]
    pull_scratch = [((long, 2 * width), f32), ((rows, width), bf16)]
    wide_0, low_0, grad_0, norm_0 = call(
        pull_first_kernel,
        (place, back, residual_0, seed, wc, norm_params, qkv_0),
        pulled,
        pull_scratch,
        flops=8e9,
    )
    (keep_e, keep_r), (send_e, send_r) = halved(place, [(two_a, NEAR), (two_b, ROW)], waits=(grad_0,))
    two_a, two_b = [keep_e, swap(send_e, *NEAR)], [keep_r, swap(send_r, *ROW)]
    wide_1, low_1, grad_1, norm_1, keep_a, keep_b, send_a, send_b = call(
        functools.partial(pull_last_kernel, n_dp),
        (
            place, back, residual_1, seed, wc, norm_params, qkv_1,
            first_0, first_1, mixed_0, mixed_1, grad_0, low_0,
        ),
        pulled + [((4 * width, cols), bf16)] * 4,
        pull_scratch + [((width, 4 * width), f32)],
        waits=(send_e,),
        flops=10e9,
    )
    one_a, one_b = [keep_a, swap(send_a, *CORE)], [keep_b, swap(send_b, *CORE)]
    (keep_e, keep_r), (send_e, send_r) = halved(place, [(two_a, ROW), (two_b, NEAR)], waits=(keep_a,))
    two_a, two_b = [keep_e, swap(send_e, *ROW)], [keep_r, swap(send_r, *NEAR)]
    (keep_a, keep_b), (send_a, send_b) = halved(
        place, [(one_a, NEAR), (one_b, ROW)], waits=(send_e,)
    )
    gots = swap(send_a, *NEAR), swap(send_b, *ROW)
    grad_in_0, grad_in_1, norm = call(
        finish_kernel,
        (norm_params, wp, grad_0, frames_x[0], wide_0, grad_1, frames_x[1], wide_1, norm_0, norm_1),
        [((own, width), f32), ((own, width), f32), ((4 * parts, cols), f32)],
        waits=(send_a,),
        flops=3e9,
        smem=0,
    )
    norm = norm + swap(norm, *CORE)
    norms = (norm, swap(norm, *ROW))

    first, *others = far()
    (keep_e, keep_r), (sent,) = halved(
        place, [(two_a, first), (two_b, first)], joint=True, waits=(norm,)
    )
    two_got = swap(sent, *first)
    (keep_a, keep_b), norm, (send_a, send_b) = halved_norm(
        place, (keep_a, keep_b), gots, (ROW, NEAR), norms, False
    )
    gots = swap(send_a, *ROW), swap(send_b, *NEAR)
    for label in others:
        (keep_e, keep_r), sent = halved_joint(place, (keep_e, keep_r), two_got, label)
        two_got = swap(sent, *label)
    for label in far():
        (keep_a, keep_b), norm, (sent,) = halved_norm(
            place, (keep_a, keep_b), gots, (label, label), (norm,), True
        )
        gots = (swap(sent, *label),)

    plain = lambda x: [(x.shape, f32)] * 4
    weighed = lambda x: plain(x) + [(x.shape, bf16)]
    updated = call(
        update_feed_kernel,
        (
            keep_e, keep_r, two_got, weight_expand, moment_expand, average_expand,
            weight_reduce, moment_reduce, average_reduce,
        ),
        weighed(weight_expand) + weighed(weight_reduce),
        flops=1e8,
        smem=0,
        mib=8,
    )
    gradient_expand, mom_expand, avg_expand, new_expand, low_expand = updated[:5]
    gradient_reduce, mom_reduce, avg_reduce, new_reduce, low_reduce = updated[5:]
    updated = call(
        update_rest_kernel,
        (
            keep_a, keep_b, gots[0], norm, weight_project, moment_project, average_project,
            weight_combine, moment_combine, average_combine, norm_params, norm_moment, norm_average,
        ),
        weighed(weight_project) + weighed(weight_combine) + plain(norm_params),
        flops=1e8,
        smem=0,
        mib=8,
    )
    gradient_project, mom_project, avg_project, new_project, low_project = updated[:5]
    gradient_combine, mom_combine, avg_combine, new_combine, low_combine = updated[5:10]
    norm_gradient, mom_norms, avg_norms, new_norms = updated[10:]
    layer_out = jnp.transpose(layer, (1, 0, 2))
    input_gradient = jnp.transpose(jnp.stack([grad_in_0, grad_in_1]), (1, 0, 2))
    return (
        layer_out,
        input_gradient,
        gradient_project,
        gradient_combine,
        gradient_expand,
        gradient_reduce,
        mom_project,
        mom_combine,
        mom_expand,
        mom_reduce,
        avg_project,
        avg_combine,
        avg_expand,
        avg_reduce,
        new_project,
        new_combine,
        new_expand,
        new_reduce,
        low_project,
        low_combine,
        low_expand,
        low_reduce,
        norm_gradient,
        mom_norms,
        avg_norms,
        new_norms,
    )


def solution(mesh):
    tokens = P("mp", "dp", None)
    stacked, matrix = P(None, "dp", "mp"), P("dp", "mp")
    weights = (stacked, matrix, matrix, matrix)
    in_specs = (tokens, tokens, P("dp")) + weights * 3 + (P(),) * 3
    out_specs = (tokens, tokens) + weights * 5 + (P(),) * 4
    return jax.shard_map(
        on_device, mesh=mesh, in_specs=in_specs, out_specs=out_specs, check_vma=False
    )
```

```python
import functools
import math

import jax
import jax.numpy as jnp
from jax import lax
from jax.experimental import pallas as pl
from jax.experimental.pallas import tpu as pltpu
from jax.sharding import PartitionSpec as P

HEADS = 8
HEAD_DIM = 64
WINDOW = 10
HALO = 16

eps_norm = 1e-05
momentum_decay = 0.9
average_decay = 0.6
matrix_rate = 0.0001
norm_rate = 0.001
masked_score = -1e30

GROUP = 4
LANES = GROUP * HEAD_DIM
QUERIES = 112
KEYS = QUERIES + HALO

f32 = jnp.float32
bf16 = jnp.bfloat16


def mm(a, b):
    return lax.dot_general(a, b, (((1,), (0,)), ((), ())), preferred_element_type=f32)


def mm_bt(a, b):
    return lax.dot_general(a, b, (((1,), (1,)), ((), ())), preferred_element_type=f32)


def mm_at(a, b):
    return lax.dot_general(a, b, (((0,), (0,)), ((), ())), preferred_element_type=f32)


def normalise(values):
    center = values - jnp.mean(values, axis=-1, keepdims=True)
    spread = jnp.mean(center * center, axis=-1, keepdims=True)
    inverse = lax.rsqrt(spread + eps_norm)
    return center * inverse, inverse


def norm_backward(values, gain, upstream):
    scaled, inverse = normalise(values)
    weighted = upstream * gain
    inner = (
        weighted
        - jnp.mean(weighted, axis=-1, keepdims=True)
        - scaled * jnp.mean(weighted * scaled, axis=-1, keepdims=True)
    )
    return inner * inverse, upstream * scaled


def query_blocks(total):
    blocks = []
    at = HALO
    while at < total:
        rows = min(QUERIES, total - at)
        blocks.append((at, rows, min(at - HALO, total - KEYS)))
        at += rows
    return blocks


def band(block, start, length):
    q0, rows, k0 = block
    query = lax.broadcasted_iota(jnp.int32, (rows, KEYS), 0)
    key = lax.broadcasted_iota(jnp.int32, (rows, KEYS), 1)
    behind = query - key + (q0 - k0)
    time = key + (start + k0 - HALO)
    inside = (time < length) | (behind == 0)
    return (behind >= 0) & (behind <= WINDOW) & (time >= 0) & inside


def head_lanes():
    lane = lax.broadcasted_iota(jnp.int32, (1, LANES), 1)
    return [(lane >= h * HEAD_DIM) & (lane < (h + 1) * HEAD_DIM) for h in range(GROUP)]


def stack_heads(block):
    zero = jnp.zeros_like(block)
    return jnp.concatenate([jnp.where(m, block, zero) for m in head_lanes()], axis=0)


def merge_heads(stacked, rows):
    masks = head_lanes()
    out = jnp.where(masks[0], stacked[:rows], 0.0)
    for h in range(1, GROUP):
        out = jnp.where(masks[h], stacked[h * rows : (h + 1) * rows], out)
    return out


def softmax_rows(scores, allowed):
    scores = jnp.where(allowed, scores * (1.0 / math.sqrt(HEAD_DIM)), masked_score)
    raised = jnp.exp(scores - jnp.max(scores, axis=-1, keepdims=True))
    return raised / jnp.sum(raised, axis=-1, keepdims=True)


def block_order(n_dp, near_first):
    bits = (n_dp // 2 - 1).bit_length()
    flip = [sum(((z >> b) & 1) << (bits - 1 - b) for b in range(bits)) for z in range(n_dp // 2)]
    if near_first:
        outer = [(x, y) for x in range(2) for y in range(2)]
    else:
        outer = [(x, y) for y in range(2) for x in range(2)]
    return [(y, 2 * z + x) for x, y in outer for z in flip]


def place_weights(n_dp, core, own_a, own_b, got_a, got_b, wp_ref, wc_ref):
    width, cols = wc_ref.shape[0], own_a.shape[1]
    r = width // n_dp
    for which, ref_a, ref_b in ((core, own_a, own_b), (1 - core, got_a, got_b)):
        for ref, first, near_first in ((ref_a, 0, True), (ref_b, 2, False)):
            for p, (y, d) in enumerate(block_order(n_dp, near_first)):
                at = pl.multiple_of((2 * y + which) * cols, cols)
                for i in range(2):
                    block = ref[(2 * p + i) * r : (2 * p + i + 1) * r]
                    if first + i < 3:
                        wp_ref[d * r : (d + 1) * r, pl.ds((first + i) * width + at, cols)] = block
                    else:
                        wc_ref[d * r : (d + 1) * r, pl.ds(at, cols)] = block


def edge_kernel(place_ref, frames_ref, cotangent_ref, near_ref, over_ref):
    last = frames_ref.shape[1] - HALO
    for core, early, late in ((0, over_ref, near_ref), (1, near_ref, over_ref)):

        @pl.when(place_ref[1] == core)
        def _():
            early[0] = frames_ref[:, :HALO]
            early[1] = cotangent_ref[:, :HALO]
            late[0] = frames_ref[:, last:]
            late[1] = frames_ref[:, last:]


def frames_kernel(place_ref, frames_ref, near_ref, over_ref, *outs):
    own = frames_ref.shape[1]
    for u, out in enumerate(outs):
        out[HALO : HALO + own] = frames_ref[u]
    for core, left, right in ((0, over_ref, near_ref), (1, near_ref, over_ref)):

        @pl.when(place_ref[1] == core)
        def _():
            for u, out in enumerate(outs):
                out[:HALO] = left[0, u]
                out[HALO + own :] = right[0, u]


def seed_kernel(place_ref, cotangent_ref, near_ref, over_ref, seed_ref, seed_t_ref):
    own = cotangent_ref.shape[1]
    for u in range(seed_ref.shape[0]):

        def valid(first, count):
            time = lax.broadcasted_iota(jnp.int32, (count, 1), 0) + (place_ref[0] + first)
            return time < place_ref[2 + u]

        mine = cotangent_ref[u]
        mine = jnp.where(valid(0, own), mine, jnp.zeros_like(mine))
        seed_ref[u, :own] = mine
        seed_t_ref[:, u * own : (u + 1) * own] = mine.T
        theirs = jnp.where(place_ref[1] == 0, near_ref[1, u], over_ref[1, u])
        seed_ref[u, own:] = jnp.where(valid(own, HALO), theirs, jnp.zeros_like(theirs))


def attend_one(
    u, place_ref, frames_ref, norms_ref, wp_ref, wc_ref,
    qkv_ref, probs_ref, first_ref, mixed_ref, residual_ref, second_ref, second_t_ref,
):
    total, width = frames_ref.shape
    own = first_ref.shape[0]
    start, length = place_ref[0], place_ref[2 + u]
    scaled, _ = normalise(frames_ref[...].astype(f32))
    normed = (scaled * norms_ref[0:1] + norms_ref[1:2]).astype(bf16)
    first_ref[...] = normed[HALO : HALO + own]
    qkv_ref[...] = mm(normed, wp_ref[...]).astype(bf16)
    for b, block in enumerate(query_blocks(total)):
        q0, rows, k0 = block
        allowed = band(block, start, length)
        for at in range(0, width, LANES):
            queries = stack_heads(qkv_ref[q0 : q0 + rows, at : at + LANES])
            keys = qkv_ref[k0 : k0 + KEYS, width + at : width + at + LANES]
            values = qkv_ref[k0 : k0 + KEYS, 2 * width + at : 2 * width + at + LANES]
            scores = mm_bt(queries, keys)
            low_probs = []
            for h in range(GROUP):
                probs = softmax_rows(scores[h * rows : (h + 1) * rows], allowed)
                probs_ref[b, h, :rows, at // LANES * KEYS : (at // LANES + 1) * KEYS] = probs
                low_probs.append(probs.astype(bf16))
            out = merge_heads(mm(jnp.concatenate(low_probs, axis=0), values), rows)
            mixed_ref[q0 - HALO : q0 - HALO + rows, at : at + LANES] = out.astype(bf16)
    residual = frames_ref[HALO:total].astype(f32) + mm_bt(mixed_ref[...], wc_ref[...])
    residual_ref[...] = residual
    scaled, _ = normalise(residual)
    second_ref[...] = (scaled * norms_ref[2:3] + norms_ref[3:4]).astype(bf16)
    second_t_ref[...] = second_ref[:own].T


def attend_first_kernel(
    n_dp, place_ref, frames_ref, norms_ref, own_a, own_b, got_a, got_b, *refs
):
    *outs, wp_ref, wc_ref = refs
    place_weights(n_dp, place_ref[1], own_a, own_b, got_a, got_b, wp_ref, wc_ref)
    attend_one(0, place_ref, frames_ref, norms_ref, wp_ref, wc_ref, *outs)


def attend_next_kernel(place_ref, frames_ref, norms_ref, wp_ref, wc_ref, *refs):
    attend_one(1, place_ref, frames_ref, norms_ref, wp_ref, wc_ref, *refs)


def gelu_parts(value):
    slope = math.sqrt(2.0 / math.pi)
    square = value * value
    tanh = jnp.tanh(value * (slope + (slope * 0.044715) * square))
    half = 0.5 + 0.5 * tanh
    curve = half + (0.5 * value) * (1.0 - tanh * tanh) * (
        slope + (slope * 3.0 * 0.044715) * square
    )
    return value * half, curve


def feed_half(
    n_dp, seconds, seconds_t, seed_ref, seed_t_ref, we_ref, wr_ref, ge_ref, gr_ref,
    wide_e, wide_r, active_ref, grad_ref, add_fed, add_back,
):
    own = seconds_t[0].shape[1]
    width, hidden = wide_e.shape[0], we_ref.shape[1]
    r = width // n_dp
    for ref, wide, near_first in ((we_ref, wide_e, True), (wr_ref, wide_r, False)):
        for p, (y, d) in enumerate(block_order(n_dp, near_first)):
            wide[d * r : (d + 1) * r, y * hidden : (y + 1) * hidden] = ref[p * r : (p + 1) * r]
    for u, second_ref in enumerate(seconds):
        rows = slice(u * own, (u + 1) * own)
        active, curve = gelu_parts(mm(second_ref[...], wide_e[...]))
        active_ref[rows] = active[:own].astype(bf16)
        grad_ref[u] = (mm(seed_ref[u], wide_r[...]) * curve).astype(bf16)
        add_fed(u, mm_bt(active_ref[rows], wide_r[...]))
        add_back(u, mm_bt(grad_ref[u], wide_e[...]))
    total_r = mm(seed_t_ref[...], active_ref[...])
    total_e = mm(seconds_t[0][...], grad_ref[0, :own]) + mm(seconds_t[1][...], grad_ref[1, :own])
    for total, ref, near_first in ((total_e, ge_ref, True), (total_r, gr_ref, False)):
        for p, (y, d) in enumerate(block_order(n_dp, near_first)):
            block = total[d * r : (d + 1) * r, y * hidden : (y + 1) * hidden]
            ref[p * r : (p + 1) * r] = block.astype(bf16)


def feed_first_kernel(n_dp, we_ref, wr_ref, n0, seed_ref, n1, seed_t_ref, t0, t1, *refs):
    fed_ref, back_ref, ge_ref, gr_ref, *scratch = refs

    def add_fed(u, value):
        fed_ref[u] = value

    def add_back(u, value):
        back_ref[u] = value

    feed_half(
        n_dp, (n0, n1), (t0, t1), seed_ref, seed_t_ref, we_ref, wr_ref, ge_ref, gr_ref,
        *scratch, add_fed, add_back,
    )


def feed_last_kernel(
    n_dp, we_ref, wr_ref, n0, seed_ref, fed_in, back_in, n1, r0, r1, seed_t_ref, t0, t1, *refs
):
    out_ref, back_ref, ge_ref, gr_ref, *scratch = refs
    own = out_ref.shape[1]

    def add_fed(u, value):
        out_ref[u] = ((r0, r1)[u][:own] + (fed_in[u] + value)).astype(bf16)

    def add_back(u, value):
        back_ref[u] = back_in[u] + value

    feed_half(
        n_dp, (n0, n1), (t0, t1), seed_ref, seed_t_ref, we_ref, wr_ref, ge_ref, gr_ref,
        *scratch, add_fed, add_back,
    )


def pull_one(
    u, back_ref, residual_ref, seed_ref, wc_ref, norms_ref, qkv_ref, probs_ref,
    wide_ref, low_ref, grad_ref, norm_ref, grad_kv_ref, mixed_g_ref,
):
    total = qkv_ref.shape[0]
    own, width = low_ref.shape
    upstream = back_ref[u]
    back, gained = norm_backward(residual_ref[...], norms_ref[2:3], upstream)
    norm_ref[0:1] = jnp.sum(gained[:own], axis=0, keepdims=True)
    norm_ref[1:2] = jnp.sum(upstream[:own], axis=0, keepdims=True)
    wide = seed_ref[u].astype(f32) + back
    wide_ref[...] = wide[:own]
    low = wide.astype(bf16)
    low_ref[...] = low[:own]
    mixed_g_ref[...] = mm(low, wc_ref[...]).astype(bf16)
    grad_kv_ref[...] = jnp.zeros_like(grad_kv_ref)
    scale = 1.0 / math.sqrt(HEAD_DIM)
    for b, block in enumerate(query_blocks(total)):
        q0, rows, k0 = block
        for at in range(0, width, LANES):
            queries = stack_heads(qkv_ref[q0 : q0 + rows, at : at + LANES])
            keys = qkv_ref[k0 : k0 + KEYS, width + at : width + at + LANES]
            values = qkv_ref[k0 : k0 + KEYS, 2 * width + at : 2 * width + at + LANES]
            upper = stack_heads(mixed_g_ref[q0 - HALO : q0 - HALO + rows, at : at + LANES])
            grad_probs = mm_bt(upper, values)
            low_probs, grad_scores = [], []
            for h in range(GROUP):
                probs = probs_ref[b, h, :rows, at // LANES * KEYS : (at // LANES + 1) * KEYS]
                grad = grad_probs[h * rows : (h + 1) * rows]
                inner = jnp.sum(probs * grad, axis=-1, keepdims=True)
                low_probs.append(probs.astype(bf16))
                grad_scores.append((probs * (grad - inner)).astype(bf16))
            low_probs = jnp.concatenate(low_probs, axis=0)
            grad_scores = jnp.concatenate(grad_scores, axis=0)
            grad_q = merge_heads(mm(grad_scores, keys), rows) * scale
            mine = min(rows, HALO + own - q0)
            if mine > 0:
                grad_ref[q0 - HALO : q0 - HALO + mine, at : at + LANES] = grad_q[:mine].astype(bf16)
            grad_kv_ref[k0 : k0 + KEYS, at : at + LANES] += mm_at(grad_scores, queries) * scale
            grad_kv_ref[k0 : k0 + KEYS, width + at : width + at + LANES] += mm_at(low_probs, upper)
    grad_ref[:, width:] = grad_kv_ref[HALO : HALO + own].astype(bf16)


def pull_first_kernel(*refs):
    pull_one(0, *refs)


def pull_last_kernel(
    n_dp, place_ref, back_ref, residual_ref, seed_ref, wc_ref, norms_ref, qkv_ref, probs_ref,
    first_0, first_1, mixed_0, mixed_1, grad_0, low_0, *refs,
):
    wide_ref, low_ref, grad_ref, norm_ref, keep_a, keep_b, send_a, send_b, grad_kv_ref, mixed_g_ref, gp_ref = refs
    pull_one(
        1, back_ref, residual_ref, seed_ref, wc_ref, norms_ref, qkv_ref, probs_ref,
        wide_ref, low_ref, grad_ref, norm_ref, grad_kv_ref, mixed_g_ref,
    )
    own, width = low_ref.shape
    gp_ref[:, : 3 * width] = mm_at(first_0[...], grad_0[...]) + mm_at(first_1[...], grad_ref[...])
    gp_ref[:, 3 * width :] = mm_at(low_0[...], mixed_0[:own]) + mm_at(low_ref[...], mixed_1[:own])
    cols, r = keep_a.shape[1], width // n_dp
    core = place_ref[1]
    for which, ref_a, ref_b in ((core, keep_a, keep_b), (1 - core, send_a, send_b)):
        for ref, first, near_first in ((ref_a, 0, True), (ref_b, 2, False)):
            for p, (y, d) in enumerate(block_order(n_dp, near_first)):
                at = pl.multiple_of((2 * y + which) * cols, cols)
                for i in range(2):
                    block = gp_ref[d * r : (d + 1) * r, pl.ds((first + i) * width + at, cols)]
                    ref[(2 * p + i) * r : (2 * p + i + 1) * r] = block.astype(bf16)


def fold_norm(ref, first, value):
    cols = ref.shape[1]
    for j in range(value.shape[1] // cols):
        ref[4 * j + first : 4 * j + first + value.shape[0]] = value[:, j * cols : (j + 1) * cols]


def finish_kernel(norms_ref, wp_ref, grad_0, frames_0, wide_0, grad_1, frames_1, wide_1, norm_0, norm_1, out_0, out_1, norm_ref):
    own = out_0.shape[0]
    gains, shifts = [], []
    for grad_ref, frames_ref, wide_ref, out_ref in (
        (grad_0, frames_0, wide_0, out_0),
        (grad_1, frames_1, wide_1, out_1),
    ):
        upstream = mm_bt(grad_ref[...], wp_ref[...])
        back, gained = norm_backward(
            frames_ref[HALO : HALO + own].astype(f32), norms_ref[0:1], upstream
        )
        gains.append(jnp.sum(gained, axis=0, keepdims=True))
        shifts.append(jnp.sum(upstream, axis=0, keepdims=True))
        out_ref[...] = wide_ref[...] + back
    fold_norm(norm_ref, 0, gains[0] + gains[1])
    fold_norm(norm_ref, 1, shifts[0] + shifts[1])
    fold_norm(norm_ref, 2, norm_0[...] + norm_1[...])


VM = pl.BlockSpec(memory_space=pltpu.VMEM)
SM = pl.BlockSpec(memory_space=pltpu.SMEM)
MIB = 1024 * 1024


def call(kernel, ins, outs, scratch=(), waits=(), flops=1e9, smem=1, mib=16):
    n, m = len(ins), len(outs)
    away = pl.BlockSpec(memory_space=pl.ANY)

    def body(*refs):
        kernel(*refs[:n], *refs[n + len(waits) :])

    return pl.pallas_call(
        body,
        out_shape=tuple(jax.ShapeDtypeStruct(shape, kind) for shape, kind in outs),
        in_specs=[SM] * smem + [VM] * (n - smem) + [away] * len(waits),
        out_specs=(VM,) * m,
        scratch_shapes=[pltpu.VMEM(shape, kind) for shape, kind in scratch],
        compiler_params=pltpu.CompilerParams(vmem_limit_bytes=mib * MIB),
        cost_estimate=pl.CostEstimate(flops=int(flops), bytes_accessed=6000000, transcendentals=0),
    )(*ins, *waits)


def swap(value, axis, bit):
    n = lax.axis_size(axis)
    return lax.ppermute(value, axis, [(i, i ^ (1 << bit)) for i in range(n)])


CORE, ROW, NEAR = ("mp", 0), ("mp", 1), ("dp", 0)


def far():
    return [("dp", b) for b in range(1, (lax.axis_size("dp") - 1).bit_length())]


def side(label):
    return (lax.axis_index(label[0]) >> label[1]) & 1


def spot(label):
    return {CORE: 1, ROW: 4, NEAR: 5}.get(label, 5 + label[1])


def paired(place, streams, waits=()):
    def kernel(place_ref, *refs):
        outs = list(refs[2 * len(streams) :])
        for i, (_, _, label, parts) in enumerate(streams):
            mine, got = refs[2 * i], refs[2 * i + 1]
            high = place_ref[spot(label)]
            for part in range(parts):
                out = outs.pop(0)
                out[high] = mine[:, part]
                out[1 - high] = got[:, part]

    ins, outs = [place], []
    for mine, got, label, parts in streams:
        blocks = lax.axis_size("dp") // 4 if parts > 1 else 1
        shape = (blocks, parts, mine.shape[0] // blocks // parts, mine.shape[1])
        ins += [mine.reshape(shape), got.reshape(shape)]
        outs += [((2, blocks, *shape[2:]), mine.dtype)] * parts
    return [x.reshape(-1, x.shape[-1]) for x in call(kernel, ins, outs, waits=waits, flops=1e8, mib=8)]


def lowered(arrays, waits):
    rows = [x.shape[0] for x in arrays]

    def kernel(*refs):
        at = 0
        for ref, count in zip(refs, rows):
            refs[-1][at : at + count] = ref[...].astype(bf16)
            at += count

    return call(kernel, arrays, [((sum(rows), arrays[0].shape[1]), bf16)], waits=waits, flops=1e8, smem=0, mib=8)[0]


def halved(place, streams, joint=False, waits=()):
    counts = [len(terms) for terms, _ in streams]
    n = len(streams)

    def kernel(place_ref, *refs):
        refs = list(refs)
        groups = [[refs.pop(0) for _ in range(count)] for count in counts]
        kept, sent = refs[:n], refs[n:]
        for i, (group, (_, label)) in enumerate(zip(groups, streams)):
            mine = place_ref[spot(label)]
            kept[i][...] = total([ref[mine] for ref in group])
            gone = total([ref[1 - mine] for ref in group]).astype(bf16)
            if joint:
                sent[0][i] = gone
            else:
                sent[i][...] = gone

    ins, keeps, sends = [place], [], []
    for terms, _ in streams:
        half, cols = terms[0].size // terms[0].shape[-1] // 2, terms[0].shape[-1]
        ins += [term.reshape(2, half, cols) for term in terms]
        keeps.append(((half, cols), f32))
        sends.append(((half, cols), bf16))
    if joint:
        sends = [((n, *sends[0][0]), bf16)]
    done = call(kernel, ins, keeps + sends, waits=waits, flops=1e8, mib=8)
    return done[:n], done[n:]


def halved_joint(place, keeps, got, label):
    n = len(keeps)
    half, cols = keeps[0].shape[0] // 2, keeps[0].shape[1]

    def kernel(place_ref, *refs):
        mine = place_ref[spot(label)]
        for i in range(n):
            kept = refs[i][mine] + refs[n][i, mine].astype(f32)
            gone = refs[i][1 - mine] + refs[n][i, 1 - mine].astype(f32)
            refs[n + 1 + i][...] = kept
            refs[2 * n + 1][i] = gone.astype(bf16)

    ins = [place, *[keep.reshape(2, half, cols) for keep in keeps], got.reshape(n, 2, half, cols)]
    done = call(kernel, ins, [((half, cols), f32)] * n + [((n, half, cols), bf16)], flops=1e8, mib=8)
    return done[:n], done[n]


def halved_norm(place, keeps, gots, labels, norms, joint, waits=()):
    rows, cols = keeps[0].shape
    half, extra = rows // 2, norms[0].shape[0]
    n = len(gots)

    def kernel(place_ref, *refs):
        keep, got, norm, outs = refs[:2], refs[2 : 2 + n], refs[2 + n : -5 if not joint else -4], refs[-5 if not joint else -4 :]
        arrived = [(got[0], 0), (got[-1], 0 if n == 2 else rows)]
        for i in range(2):
            mine = place_ref[spot(labels[i])]
            ref, at = arrived[i]
            here = keep[i][pl.ds(pl.multiple_of(mine * half, half), half)].astype(f32)
            there = keep[i][pl.ds(pl.multiple_of((1 - mine) * half, half), half)].astype(f32)
            here += ref[pl.ds(pl.multiple_of(at + mine * half, half), half)].astype(f32)
            there += ref[pl.ds(pl.multiple_of(at + (1 - mine) * half, half), half)].astype(f32)
            outs[i][...] = here
            if joint:
                outs[3][i * half : (i + 1) * half] = there.astype(bf16)
            else:
                outs[3 + i][:half] = there.astype(bf16)
        if len(norm) == 2:
            value = norm[0][...] + norm[1][...]
        else:
            ref, at = arrived[1]
            value = joined_norm(norm[0][...], ref[at + rows : at + rows + 2 * extra])
        outs[2][...] = value
        split_norm(value, outs[-1], 2 * half if joint else half)

    small = [((half, cols), f32)] * 2 + [((extra, cols), f32)]
    if joint:
        sends = [((2 * half + 2 * extra, cols), bf16)]
    else:
        sends = [((half, cols), bf16), ((half + 2 * extra, cols), bf16)]
    done = call(kernel, (place, *keeps, *gots, *norms), small + sends, waits=waits, flops=1e8, mib=8)
    return done[:2], done[2], done[3:]


def split_norm(value, ref, at):
    rows = value.shape[0]
    high = value.astype(bf16)
    ref[at : at + rows] = high
    ref[at + rows : at + 2 * rows] = (value - high.astype(f32)).astype(bf16)


def joined_norm(value, got):
    rows = value.shape[0]
    high = value.astype(bf16).astype(f32)
    low = (value - high).astype(bf16).astype(f32)
    return (high + low) + (got[:rows].astype(f32) + got[rows:].astype(f32))


def total(terms):
    terms = [term.astype(f32) for term in terms]
    return functools.reduce(jnp.add, terms)


def write_update(outs, at, gradient, states, rate):
    values = advance(*states[:1], gradient, *states[1:], rate)
    for out, value in zip(outs, (gradient, *values)):
        out[at] = value
    if len(outs) > 4:
        outs[4][at] = values[2].astype(bf16)


def update_feed_kernel(keep_e, keep_r, got_ref, *refs):
    states, outs = refs[:6], refs[6:]
    for i, keep in enumerate((keep_e, keep_r)):
        gradient = keep[...] + got_ref[i].astype(f32)
        state = [ref[...] for ref in states[3 * i : 3 * i + 3]]
        write_update(outs[5 * i : 5 * i + 5], slice(None), gradient, state, matrix_rate)


def update_rest_kernel(keep_a, keep_b, got_ref, norm_ref, *refs):
    states, outs = refs[:9], refs[9:]
    rows, cols = keep_a.shape
    r, extra = rows // 2, norm_ref.shape[0]
    for i in range(4):
        keep = (keep_a, keep_b)[i // 2]
        at = (i % 2) * r
        gradient = keep[at : at + r] + got_ref[i * r : (i + 1) * r].astype(f32)
        which, entry = (0, i) if i < 3 else (1, slice(None))
        state = [ref[entry] for ref in states[3 * which : 3 * which + 3]]
        write_update(outs[5 * which : 5 * which + 5], entry, gradient, state, matrix_rate)
    value = joined_norm(norm_ref[...], got_ref[2 * rows : 2 * rows + 2 * extra])
    for j in range(extra // 4):
        at = (slice(None), slice(j * cols, (j + 1) * cols))
        state = [ref[at] for ref in states[6:]]
        write_update(outs[10:], at, value[4 * j : 4 * j + 4], state, norm_rate)


def advance(weight, gradient, moment, average, rate):
    momentum = momentum_decay * moment + gradient
    updated = weight - rate * (gradient + momentum_decay * momentum)
    smoothed = average_decay * average + (1.0 - average_decay) * updated
    return (momentum, smoothed, updated)


def on_device(
    frames,
    cotangent,
    lengths,
    weight_project,
    weight_combine,
    weight_expand,
    weight_reduce,
    moment_project,
    moment_combine,
    moment_expand,
    moment_reduce,
    average_project,
    average_combine,
    average_expand,
    average_reduce,
    norm_params,
    norm_moment,
    norm_average,
):
    own, batch, width = frames.shape
    long, rows = own + 2 * HALO, own + HALO
    parts, n_dp = lax.axis_size("mp"), lax.axis_size("dp")
    me = lax.axis_index("mp")
    start = me * own
    cols, hidden = width // parts, weight_expand.shape[1]
    r = width // n_dp

    sides = [side(label) for label in (ROW, NEAR, *far())]
    place = jnp.concatenate(
        [jnp.stack([start, side(CORE)]).astype(jnp.int32), lengths, jnp.stack(sides).astype(jnp.int32)]
    )
    *outer, last = reversed(far())

    matrices = jnp.concatenate([weight_project, weight_combine[None]], axis=0).astype(bf16)
    one = matrices.reshape(-1, cols)
    for label in outer:
        (one,) = paired(place, [(one, swap(one, *label), label, 1)])
    one_got = swap(one, *last)

    two = lowered([weight_expand, weight_reduce], waits=(one,))
    one_a, one_b = paired(place, [(one, one_got, last, 2)])
    frames_u = jnp.transpose(frames, (1, 0, 2))
    cotangent_u = jnp.transpose(cotangent, (1, 0, 2))
    strip = ((2, batch, HALO, width), bf16)
    near, over = call(
        edge_kernel,
        (place, frames_u, cotangent_u),
        [strip] * 2,
        waits=(one_got,),
        flops=1e8,
        mib=8,
    )
    near = swap(near, *CORE)
    pairs = [(i, i + 1) for i in range(1, parts - 1, 2)]
    over = lax.ppermute(over, "mp", pairs + [(b, a) for a, b in pairs])
    frames_x = call(
        frames_kernel, (place, frames_u, near, over), [((long, width), bf16)] * 2, flops=1e8, mib=8
    )
    got_a, got_b = swap(one_a, *ROW), swap(one_b, *NEAR)
    for label in outer:
        (two,) = paired(place, [(two, swap(two, *label), label, 1)])
    one_a, one_b = paired(
        place, [(one_a, got_a, ROW, 1), (one_b, got_b, NEAR, 1)], waits=(two,)
    )
    got_a, got_b = swap(one_a, *NEAR), swap(one_b, *ROW)
    two_a, two_b = paired(place, [(two, swap(two, *last), last, 2)])
    one_a, one_b = paired(
        place, [(one_a, got_a, NEAR, 1), (one_b, got_b, ROW, 1)], waits=(two_a, *frames_x)
    )
    core_a, core_b = swap(one_a, *CORE), swap(one_b, *CORE)

    per_u = [
        ((long, 3 * width), bf16),
        ((-(-rows // QUERIES), GROUP, QUERIES, width // LANES * KEYS), f32),
        ((own, width), bf16),
        ((rows, width), bf16),
        ((rows, width), f32),
        ((rows, width), bf16),
        ((width, own), bf16),
    ]
    qkv_0, probs_0, first_0, mixed_0, residual_0, second_0, second_t_0, wp, wc = call(
        functools.partial(attend_first_kernel, n_dp),
        (place, frames_x[0], norm_params, one_a, one_b, core_a, core_b),
        per_u + [((width, 3 * width), bf16), ((width, width), bf16)],
        flops=5e9,
    )
    seed, seed_t = call(
        seed_kernel,
        (place, cotangent_u, near, over),
        [((batch, rows, width), bf16), ((width, batch * own), bf16)],
        waits=(second_0,),
        flops=1e8,
        mib=8,
    )

    got_a, got_b = swap(two_a, *ROW), swap(two_b, *NEAR)
    two_a, two_b = paired(place, [(two_a, got_a, ROW, 1), (two_b, got_b, NEAR, 1)], waits=(seed,))
    qkv_1, probs_1, first_1, mixed_1, residual_1, second_1, second_t_1 = call(
        attend_next_kernel,
        (place, frames_x[1], norm_params, wp, wc),
        per_u,
        flops=5e9,
    )
    got_a, got_b = swap(two_a, *NEAR), swap(two_b, *ROW)
    expand, reduce_w = paired(
        place, [(two_a, got_a, NEAR, 1), (two_b, got_b, ROW, 1)], waits=(second_1,)
    )
    expand_got, reduce_got = swap(expand, *CORE), swap(reduce_w, *CORE)

    grads = [((2 * width, hidden), bf16)] * 2
    carried = [((batch, own, width), f32), ((batch, rows, width), f32)]
    feed_scratch = [((width, 2 * hidden), bf16)] * 2 + [
        ((batch * own, 2 * hidden), bf16),
        ((batch, rows, 2 * hidden), bf16),
    ]
    transposed = (seed_t, second_t_0, second_t_1)
    fed, back, keep_e, keep_r = call(
        functools.partial(feed_first_kernel, n_dp),
        (expand, reduce_w, second_0, seed, second_1, *transposed),
        carried + grads,
        feed_scratch,
        flops=8e9,
        smem=0,
    )
    layer, back, send_e, send_r = call(
        functools.partial(feed_last_kernel, n_dp),
        (expand_got, reduce_got, second_0, seed, fed, back, second_1, residual_0, residual_1, *transposed),
        [((batch, own, width), bf16), carried[1]] + grads,
        feed_scratch,
        flops=8e9,
        smem=0,
    )

    two_a, two_b = [keep_e, swap(send_e, *CORE)], [keep_r, swap(send_r, *CORE)]
    pulled = [((own, width), f32), ((own, width), bf16), ((own, 3 * width), bf16), ((2, width), f32)]
    pull_scratch = [((long, 2 * width), f32), ((rows, width), bf16)]
    wide_0, low_0, grad_0, norm_0 = call(
        pull_first_kernel,
        (back, residual_0, seed, wc, norm_params, qkv_0, probs_0),
        pulled,
        pull_scratch,
        flops=8e9,
        smem=0,
    )
    (keep_e, keep_r), (send_e, send_r) = halved(place, [(two_a, NEAR), (two_b, ROW)], waits=(grad_0,))
    two_a, two_b = [keep_e, swap(send_e, *NEAR)], [keep_r, swap(send_r, *ROW)]
    wide_1, low_1, grad_1, norm_1, keep_a, keep_b, send_a, send_b = call(
        functools.partial(pull_last_kernel, n_dp),
        (
            place, back, residual_1, seed, wc, norm_params, qkv_1, probs_1,
            first_0, first_1, mixed_0, mixed_1, grad_0, low_0,
        ),
        pulled + [((4 * width, cols), bf16)] * 4,
        pull_scratch + [((width, 4 * width), f32)],
        waits=(send_e,),
        flops=10e9,
    )
    one_a, one_b = [keep_a, swap(send_a, *CORE)], [keep_b, swap(send_b, *CORE)]
    grad_in_0, grad_in_1, norm = call(
        finish_kernel,
        (norm_params, wp, grad_0, frames_x[0], wide_0, grad_1, frames_x[1], wide_1, norm_0, norm_1),
        [((own, width), f32), ((own, width), f32), ((4 * parts, cols), f32)],
        waits=(keep_a,),
        flops=3e9,
        smem=0,
    )
    norms = (norm, swap(norm, *CORE))
    (keep_e, keep_r), (send_e, send_r) = halved(place, [(two_a, ROW), (two_b, NEAR)], waits=(norm,))
    two_a, two_b = [keep_e, swap(send_e, *ROW)], [keep_r, swap(send_r, *NEAR)]
    (keep_a, keep_b), norm, (send_a, send_b) = halved_norm(
        place, (one_a[0], one_b[0]), (one_a[1], one_b[1]), (NEAR, ROW), norms, False, waits=(send_e,)
    )
    gots = swap(send_a, *NEAR), swap(send_b, *ROW)

    first, *others = far()
    (keep_e, keep_r), (sent,) = halved(place, [(two_a, first), (two_b, first)], joint=True)
    two_got = swap(sent, *first)
    (keep_a, keep_b), norm, (send_a, send_b) = halved_norm(
        place, (keep_a, keep_b), gots, (ROW, NEAR), (norm,), False
    )
    gots = swap(send_a, *ROW), swap(send_b, *NEAR)
    for label in others:
        (keep_e, keep_r), sent = halved_joint(place, (keep_e, keep_r), two_got, label)
        two_got = swap(sent, *label)
    for label in far():
        (keep_a, keep_b), norm, (sent,) = halved_norm(
            place, (keep_a, keep_b), gots, (label, label), (norm,), True
        )
        gots = (swap(sent, *label),)

    plain = lambda x: [(x.shape, f32)] * 4
    weighed = lambda x: plain(x) + [(x.shape, bf16)]
    updated = call(
        update_feed_kernel,
        (
            keep_e, keep_r, two_got, weight_expand, moment_expand, average_expand,
            weight_reduce, moment_reduce, average_reduce,
        ),
        weighed(weight_expand) + weighed(weight_reduce),
        flops=1e8,
        smem=0,
        mib=8,
    )
    gradient_expand, mom_expand, avg_expand, new_expand, low_expand = updated[:5]
    gradient_reduce, mom_reduce, avg_reduce, new_reduce, low_reduce = updated[5:]
    updated = call(
        update_rest_kernel,
        (
            keep_a, keep_b, gots[0], norm, weight_project, moment_project, average_project,
            weight_combine, moment_combine, average_combine, norm_params, norm_moment, norm_average,
        ),
        weighed(weight_project) + weighed(weight_combine) + plain(norm_params),
        flops=1e8,
        smem=0,
        mib=8,
    )
    gradient_project, mom_project, avg_project, new_project, low_project = updated[:5]
    gradient_combine, mom_combine, avg_combine, new_combine, low_combine = updated[5:10]
    norm_gradient, mom_norms, avg_norms, new_norms = updated[10:]
    layer_out = jnp.transpose(layer, (1, 0, 2))
    input_gradient = jnp.transpose(jnp.stack([grad_in_0, grad_in_1]), (1, 0, 2))
    return (
        layer_out,
        input_gradient,
        gradient_project,
        gradient_combine,
        gradient_expand,
        gradient_reduce,
        mom_project,
        mom_combine,
        mom_expand,
        mom_reduce,
        avg_project,
        avg_combine,
        avg_expand,
        avg_reduce,
        new_project,
        new_combine,
        new_expand,
        new_reduce,
        low_project,
        low_combine,
        low_expand,
        low_reduce,
        norm_gradient,
        mom_norms,
        avg_norms,
        new_norms,
    )


def solution(mesh):
    tokens = P("mp", "dp", None)
    stacked, matrix = P(None, "dp", "mp"), P("dp", "mp")
    weights = (stacked, matrix, matrix, matrix)
    in_specs = (tokens, tokens, P("dp")) + weights * 3 + (P(),) * 3
    out_specs = (tokens, tokens) + weights * 5 + (P(),) * 4
    return jax.shard_map(
        on_device, mesh=mesh, in_specs=in_specs, out_specs=out_specs, check_vma=False
    )
```

```python
import functools
import math

import jax
import jax.numpy as jnp
from jax import lax
from jax.experimental import pallas as pl
from jax.experimental.pallas import tpu as pltpu
from jax.sharding import PartitionSpec as P

HEADS = 8
HEAD_DIM = 64
WINDOW = 10
HALO = 16

eps_norm = 1e-05
momentum_decay = 0.9
average_decay = 0.6
matrix_rate = 0.0001
norm_rate = 0.001
masked_score = -1e30

GROUP = 4
LANES = GROUP * HEAD_DIM
QUERIES = 112
KEYS = QUERIES + HALO

f32 = jnp.float32
bf16 = jnp.bfloat16


def mm(a, b):
    return lax.dot_general(a, b, (((1,), (0,)), ((), ())), preferred_element_type=f32)


def mm_bt(a, b):
    return lax.dot_general(a, b, (((1,), (1,)), ((), ())), preferred_element_type=f32)


def mm_at(a, b):
    return lax.dot_general(a, b, (((0,), (0,)), ((), ())), preferred_element_type=f32)


def normalise(values):
    center = values - jnp.mean(values, axis=-1, keepdims=True)
    spread = jnp.mean(center * center, axis=-1, keepdims=True)
    inverse = lax.rsqrt(spread + eps_norm)
    return center * inverse, inverse


def norm_backward(values, gain, upstream):
    scaled, inverse = normalise(values)
    weighted = upstream * gain
    inner = (
        weighted
        - jnp.mean(weighted, axis=-1, keepdims=True)
        - scaled * jnp.mean(weighted * scaled, axis=-1, keepdims=True)
    )
    return inner * inverse, upstream * scaled


def query_blocks(total):
    blocks = []
    at = HALO
    while at < total:
        rows = min(QUERIES, total - at)
        blocks.append((at, rows, min(at - HALO, total - KEYS)))
        at += rows
    return blocks


def band(block, start, length):
    q0, rows, k0 = block
    query = lax.broadcasted_iota(jnp.int32, (rows, KEYS), 0)
    key = lax.broadcasted_iota(jnp.int32, (rows, KEYS), 1)
    behind = query - key + (q0 - k0)
    time = key + (start + k0 - HALO)
    inside = (time < length) | (behind == 0)
    return (behind >= 0) & (behind <= WINDOW) & (time >= 0) & inside


def head_lanes():
    lane = lax.broadcasted_iota(jnp.int32, (1, LANES), 1)
    return [(lane >= h * HEAD_DIM) & (lane < (h + 1) * HEAD_DIM) for h in range(GROUP)]


def stack_heads(block):
    zero = jnp.zeros_like(block)
    return jnp.concatenate([jnp.where(m, block, zero) for m in head_lanes()], axis=0)


def merge_heads(stacked, rows):
    masks = head_lanes()
    out = jnp.where(masks[0], stacked[:rows], 0.0)
    for h in range(1, GROUP):
        out = jnp.where(masks[h], stacked[h * rows : (h + 1) * rows], out)
    return out


def softmax_rows(scores, allowed):
    scores = jnp.where(allowed, scores * (1.0 / math.sqrt(HEAD_DIM)), masked_score)
    raised = jnp.exp(scores - jnp.max(scores, axis=-1, keepdims=True))
    return raised / jnp.sum(raised, axis=-1, keepdims=True)


def block_order(n_dp, near_first, split=False):
    row, near, far_bits = -1, 0, list(range(1, (n_dp - 1).bit_length()))
    first, second = (near, row) if near_first else (row, near)
    bits = [first, far_bits[0], second, *far_bits[1:]] if split else [first, second, *far_bits]
    blocks = []
    for at in range(2 * n_dp):
        value = {bit: (at >> (len(bits) - 1 - i)) & 1 for i, bit in enumerate(bits)}
        blocks.append((value[row], sum(value[bit] << bit for bit in bits if bit != row)))
    return blocks


def place_weights(n_dp, core, own_a, own_b, got_a, got_b, wp_ref, wc_ref):
    width, cols = wc_ref.shape[0], own_a.shape[1]
    r = width // n_dp
    for which, ref_a, ref_b in ((core, own_a, own_b), (1 - core, got_a, got_b)):
        for ref, first, near_first in ((ref_a, 0, True), (ref_b, 2, False)):
            for p, (y, d) in enumerate(block_order(n_dp, near_first)):
                at = pl.multiple_of((2 * y + which) * cols, cols)
                for i in range(2):
                    block = ref[(2 * p + i) * r : (2 * p + i + 1) * r]
                    if first + i < 3:
                        wp_ref[d * r : (d + 1) * r, pl.ds((first + i) * width + at, cols)] = block
                    else:
                        wc_ref[d * r : (d + 1) * r, pl.ds(at, cols)] = block


def edge_kernel(place_ref, frames_ref, cotangent_ref, near_ref, over_ref):
    last = frames_ref.shape[1] - HALO
    for core, early, late in ((0, over_ref, near_ref), (1, near_ref, over_ref)):

        @pl.when(place_ref[1] == core)
        def _():
            early[0] = frames_ref[:, :HALO]
            early[1] = cotangent_ref[:, :HALO]
            late[0] = frames_ref[:, last:]
            late[1] = frames_ref[:, last:]


def frames_kernel(place_ref, frames_ref, near_ref, over_ref, *outs):
    own = frames_ref.shape[1]
    for u, out in enumerate(outs):
        out[HALO : HALO + own] = frames_ref[u]
    for core, left, right in ((0, over_ref, near_ref), (1, near_ref, over_ref)):

        @pl.when(place_ref[1] == core)
        def _():
            for u, out in enumerate(outs):
                out[:HALO] = left[0, u]
                out[HALO + own :] = right[0, u]


def seed_kernel(place_ref, cotangent_ref, near_ref, over_ref, seed_ref, seed_t_ref):
    own = cotangent_ref.shape[1]
    for u in range(seed_ref.shape[0]):

        def valid(first, count):
            time = lax.broadcasted_iota(jnp.int32, (count, 1), 0) + (place_ref[0] + first)
            return time < place_ref[2 + u]

        mine = cotangent_ref[u]
        mine = jnp.where(valid(0, own), mine, jnp.zeros_like(mine))
        seed_ref[u, :own] = mine
        seed_t_ref[:, u * own : (u + 1) * own] = mine.T
        theirs = jnp.where(place_ref[1] == 0, near_ref[1, u], over_ref[1, u])
        seed_ref[u, own:] = jnp.where(valid(own, HALO), theirs, jnp.zeros_like(theirs))


def attend_one(
    u, place_ref, frames_ref, norms_ref, wp_ref, wc_ref,
    qkv_ref, probs_ref, first_ref, mixed_ref, residual_ref, second_ref, second_t_ref,
):
    total, width = frames_ref.shape
    own = first_ref.shape[0]
    start, length = place_ref[0], place_ref[2 + u]
    scaled, _ = normalise(frames_ref[...].astype(f32))
    normed = (scaled * norms_ref[0:1] + norms_ref[1:2]).astype(bf16)
    first_ref[...] = normed[HALO : HALO + own]
    qkv_ref[...] = mm(normed, wp_ref[...]).astype(bf16)
    for b, block in enumerate(query_blocks(total)):
        q0, rows, k0 = block
        allowed = band(block, start, length)
        for at in range(0, width, LANES):
            queries = stack_heads(qkv_ref[q0 : q0 + rows, at : at + LANES])
            keys = qkv_ref[k0 : k0 + KEYS, width + at : width + at + LANES]
            values = qkv_ref[k0 : k0 + KEYS, 2 * width + at : 2 * width + at + LANES]
            scores = mm_bt(queries, keys)
            low_probs = []
            for h in range(GROUP):
                probs = softmax_rows(scores[h * rows : (h + 1) * rows], allowed)
                probs_ref[b, h, :rows, at // LANES * KEYS : (at // LANES + 1) * KEYS] = probs
                low_probs.append(probs.astype(bf16))
            out = merge_heads(mm(jnp.concatenate(low_probs, axis=0), values), rows)
            mixed_ref[q0 - HALO : q0 - HALO + rows, at : at + LANES] = out.astype(bf16)
    residual = frames_ref[HALO:total].astype(f32) + mm_bt(mixed_ref[...], wc_ref[...])
    residual_ref[...] = residual
    scaled, _ = normalise(residual)
    second_ref[...] = (scaled * norms_ref[2:3] + norms_ref[3:4]).astype(bf16)
    second_t_ref[...] = second_ref[:own].T


def attend_first_kernel(
    n_dp, place_ref, frames_ref, norms_ref, own_a, own_b, got_a, got_b, *refs
):
    *outs, wp_ref, wc_ref = refs
    place_weights(n_dp, place_ref[1], own_a, own_b, got_a, got_b, wp_ref, wc_ref)
    attend_one(0, place_ref, frames_ref, norms_ref, wp_ref, wc_ref, *outs)


def attend_next_kernel(place_ref, frames_ref, norms_ref, wp_ref, wc_ref, *refs):
    attend_one(1, place_ref, frames_ref, norms_ref, wp_ref, wc_ref, *refs)


def gelu_parts(value):
    slope = math.sqrt(2.0 / math.pi)
    square = value * value
    tanh = jnp.tanh(value * (slope + (slope * 0.044715) * square))
    half = 0.5 + 0.5 * tanh
    curve = half + (0.5 * value) * (1.0 - tanh * tanh) * (
        slope + (slope * 3.0 * 0.044715) * square
    )
    return value * half, curve


def feed_half(
    n_dp, seconds, seconds_t, seed_ref, seed_t_ref, we_ref, wr_ref, ge_ref, gr_ref,
    wide_e, wide_r, active_ref, grad_ref, add_fed, add_back,
):
    own = seconds_t[0].shape[1]
    width, hidden = wide_e.shape[0], we_ref.shape[1]
    r = width // n_dp
    for ref, wide, near_first in ((we_ref, wide_e, True), (wr_ref, wide_r, False)):
        for p, (y, d) in enumerate(block_order(n_dp, near_first)):
            wide[d * r : (d + 1) * r, y * hidden : (y + 1) * hidden] = ref[p * r : (p + 1) * r]
    for u, second_ref in enumerate(seconds):
        rows = slice(u * own, (u + 1) * own)
        active, curve = gelu_parts(mm(second_ref[...], wide_e[...]))
        active_ref[rows] = active[:own].astype(bf16)
        grad_ref[u] = (mm(seed_ref[u], wide_r[...]) * curve).astype(bf16)
        add_fed(u, mm_bt(active_ref[rows], wide_r[...]))
        add_back(u, mm_bt(grad_ref[u], wide_e[...]))
    total_r = mm(seed_t_ref[...], active_ref[...])
    total_e = mm(seconds_t[0][...], grad_ref[0, :own]) + mm(seconds_t[1][...], grad_ref[1, :own])
    for total, ref, near_first in ((total_e, ge_ref, True), (total_r, gr_ref, False)):
        for p, (y, d) in enumerate(block_order(n_dp, near_first, True)):
            block = total[d * r : (d + 1) * r, y * hidden : (y + 1) * hidden]
            ref[p * r : (p + 1) * r] = block.astype(bf16)


def feed_first_kernel(n_dp, we_ref, wr_ref, n0, seed_ref, n1, seed_t_ref, t0, t1, *refs):
    fed_ref, back_ref, ge_ref, gr_ref, *scratch = refs

    def add_fed(u, value):
        fed_ref[u] = value

    def add_back(u, value):
        back_ref[u] = value

    feed_half(
        n_dp, (n0, n1), (t0, t1), seed_ref, seed_t_ref, we_ref, wr_ref, ge_ref, gr_ref,
        *scratch, add_fed, add_back,
    )


def feed_last_kernel(
    n_dp, we_ref, wr_ref, n0, seed_ref, fed_in, back_in, n1, r0, r1, seed_t_ref, t0, t1, *refs
):
    out_ref, back_ref, ge_ref, gr_ref, *scratch = refs
    own = out_ref.shape[1]

    def add_fed(u, value):
        out_ref[u] = ((r0, r1)[u][:own] + (fed_in[u] + value)).astype(bf16)

    def add_back(u, value):
        back_ref[u] = back_in[u] + value

    feed_half(
        n_dp, (n0, n1), (t0, t1), seed_ref, seed_t_ref, we_ref, wr_ref, ge_ref, gr_ref,
        *scratch, add_fed, add_back,
    )


def pull_one(
    u, back_ref, residual_ref, seed_ref, wc_ref, norms_ref, qkv_ref, probs_ref,
    wide_ref, low_ref, grad_ref, norm_ref, grad_kv_ref, mixed_g_ref,
):
    total = qkv_ref.shape[0]
    own, width = low_ref.shape
    upstream = back_ref[u]
    back, gained = norm_backward(residual_ref[...], norms_ref[2:3], upstream)
    norm_ref[0:1] = jnp.sum(gained[:own], axis=0, keepdims=True)
    norm_ref[1:2] = jnp.sum(upstream[:own], axis=0, keepdims=True)
    wide = seed_ref[u].astype(f32) + back
    wide_ref[...] = wide[:own]
    low = wide.astype(bf16)
    low_ref[...] = low[:own]
    mixed_g_ref[...] = mm(low, wc_ref[...]).astype(bf16)
    grad_kv_ref[...] = jnp.zeros_like(grad_kv_ref)
    scale = 1.0 / math.sqrt(HEAD_DIM)
    for b, block in enumerate(query_blocks(total)):
        q0, rows, k0 = block
        for at in range(0, width, LANES):
            queries = stack_heads(qkv_ref[q0 : q0 + rows, at : at + LANES])
            keys = qkv_ref[k0 : k0 + KEYS, width + at : width + at + LANES]
            values = qkv_ref[k0 : k0 + KEYS, 2 * width + at : 2 * width + at + LANES]
            upper = stack_heads(mixed_g_ref[q0 - HALO : q0 - HALO + rows, at : at + LANES])
            grad_probs = mm_bt(upper, values)
            low_probs, grad_scores = [], []
            for h in range(GROUP):
                probs = probs_ref[b, h, :rows, at // LANES * KEYS : (at // LANES + 1) * KEYS]
                grad = grad_probs[h * rows : (h + 1) * rows]
                inner = jnp.sum(probs * grad, axis=-1, keepdims=True)
                low_probs.append(probs.astype(bf16))
                grad_scores.append((probs * (grad - inner)).astype(bf16))
            low_probs = jnp.concatenate(low_probs, axis=0)
            grad_scores = jnp.concatenate(grad_scores, axis=0)
            grad_q = merge_heads(mm(grad_scores, keys), rows) * scale
            mine = min(rows, HALO + own - q0)
            if mine > 0:
                grad_ref[q0 - HALO : q0 - HALO + mine, at : at + LANES] = grad_q[:mine].astype(bf16)
            grad_kv_ref[k0 : k0 + KEYS, at : at + LANES] += mm_at(grad_scores, queries) * scale
            grad_kv_ref[k0 : k0 + KEYS, width + at : width + at + LANES] += mm_at(low_probs, upper)
    grad_ref[:, width:] = grad_kv_ref[HALO : HALO + own].astype(bf16)


def pull_first_kernel(*refs):
    pull_one(0, *refs)


def pull_last_kernel(
    n_dp, place_ref, back_ref, residual_ref, seed_ref, wc_ref, norms_ref, qkv_ref, probs_ref,
    first_0, first_1, mixed_0, mixed_1, grad_0, low_0, *refs,
):
    wide_ref, low_ref, grad_ref, norm_ref, keep_a, keep_b, send_a, send_b, grad_kv_ref, mixed_g_ref = refs
    pull_one(
        1, back_ref, residual_ref, seed_ref, wc_ref, norms_ref, qkv_ref, probs_ref,
        wide_ref, low_ref, grad_ref, norm_ref, grad_kv_ref, mixed_g_ref,
    )
    own, width = low_ref.shape
    core, cols, r = place_ref[1], keep_a.shape[1], width // n_dp
    firsts = first_0[...].T, first_1[...].T
    lows = low_0[...].T, low_ref[...].T
    where = {
        near_first: {block: p for p, block in enumerate(block_order(n_dp, near_first))}
        for near_first in (True, False)
    }
    for i in range(4):
        keep, send, at = (keep_a, send_a, where[True]) if i < 2 else (keep_b, send_b, where[False])
        for y in range(2):
            lanes = slice(2 * y * cols, 2 * (y + 1) * cols)
            if i < 3:
                inner = slice(i * width + lanes.start, i * width + lanes.stop)
                value = mm(firsts[0], grad_0[:, inner]) + mm(firsts[1], grad_ref[:, inner])
            else:
                value = mm(lows[0], mixed_0[:own, lanes]) + mm(lows[1], mixed_1[:own, lanes])
            mine = jnp.where(core == 0, value[:, :cols], value[:, cols:])
            other = jnp.where(core == 0, value[:, cols:], value[:, :cols])
            for d in range(n_dp):
                to = (2 * at[y, d] + i % 2) * r
                keep[to : to + r] = mine[d * r : (d + 1) * r].astype(bf16)
                send[to : to + r] = other[d * r : (d + 1) * r].astype(bf16)


def fold_norm(ref, first, value):
    cols = ref.shape[1]
    for j in range(value.shape[1] // cols):
        ref[4 * j + first : 4 * j + first + value.shape[0]] = value[:, j * cols : (j + 1) * cols]


def finish_kernel(norms_ref, wp_ref, grad_0, frames_0, wide_0, grad_1, frames_1, wide_1, norm_0, norm_1, out_0, out_1, norm_ref):
    own = out_0.shape[0]
    gains, shifts = [], []
    for grad_ref, frames_ref, wide_ref, out_ref in (
        (grad_0, frames_0, wide_0, out_0),
        (grad_1, frames_1, wide_1, out_1),
    ):
        upstream = mm_bt(grad_ref[...], wp_ref[...])
        back, gained = norm_backward(
            frames_ref[HALO : HALO + own].astype(f32), norms_ref[0:1], upstream
        )
        gains.append(jnp.sum(gained, axis=0, keepdims=True))
        shifts.append(jnp.sum(upstream, axis=0, keepdims=True))
        out_ref[...] = wide_ref[...] + back
    fold_norm(norm_ref, 0, gains[0] + gains[1])
    fold_norm(norm_ref, 1, shifts[0] + shifts[1])
    fold_norm(norm_ref, 2, norm_0[...] + norm_1[...])


VM = pl.BlockSpec(memory_space=pltpu.VMEM)
SM = pl.BlockSpec(memory_space=pltpu.SMEM)
MIB = 1024 * 1024


def call(kernel, ins, outs, scratch=(), waits=(), flops=1e9, smem=1, mib=16):
    n, m = len(ins), len(outs)
    away = pl.BlockSpec(memory_space=pl.ANY)

    def body(*refs):
        kernel(*refs[:n], *refs[n + len(waits) :])

    return pl.pallas_call(
        body,
        out_shape=tuple(jax.ShapeDtypeStruct(shape, kind) for shape, kind in outs),
        in_specs=[SM] * smem + [VM] * (n - smem) + [away] * len(waits),
        out_specs=(VM,) * m,
        scratch_shapes=[pltpu.VMEM(shape, kind) for shape, kind in scratch],
        compiler_params=pltpu.CompilerParams(vmem_limit_bytes=mib * MIB),
        cost_estimate=pl.CostEstimate(flops=int(flops), bytes_accessed=6000000, transcendentals=0),
    )(*ins, *waits)


def swap(value, axis, bit):
    n = lax.axis_size(axis)
    return lax.ppermute(value, axis, [(i, i ^ (1 << bit)) for i in range(n)])


CORE, ROW, NEAR = ("mp", 0), ("mp", 1), ("dp", 0)


def far():
    return [("dp", b) for b in range(1, (lax.axis_size("dp") - 1).bit_length())]


def side(label):
    return (lax.axis_index(label[0]) >> label[1]) & 1


def spot(label):
    return {CORE: 1, ROW: 4, NEAR: 5}.get(label, 5 + label[1])


def paired(place, streams, waits=()):
    def kernel(place_ref, *refs):
        outs = list(refs[2 * len(streams) :])
        for i, (_, _, label, parts) in enumerate(streams):
            mine, got = refs[2 * i], refs[2 * i + 1]
            high = place_ref[spot(label)]
            for part in range(parts):
                out = outs.pop(0)
                out[high] = mine[:, part]
                out[1 - high] = got[:, part]

    ins, outs = [place], []
    for mine, got, label, parts in streams:
        blocks = lax.axis_size("dp") // 4 if parts > 1 else 1
        shape = (blocks, parts, mine.shape[0] // blocks // parts, mine.shape[1])
        ins += [mine.reshape(shape), got.reshape(shape)]
        outs += [((2, blocks, *shape[2:]), mine.dtype)] * parts
    return [x.reshape(-1, x.shape[-1]) for x in call(kernel, ins, outs, waits=waits, flops=1e8, mib=8)]


def lowered(arrays, waits):
    rows = [x.shape[0] for x in arrays]

    def kernel(*refs):
        at = 0
        for ref, count in zip(refs, rows):
            refs[-1][at : at + count] = ref[...].astype(bf16)
            at += count

    return call(kernel, arrays, [((sum(rows), arrays[0].shape[1]), bf16)], waits=waits, flops=1e8, smem=0, mib=8)[0]


def halved(place, streams, joint=0, waits=()):
    counts = [len(terms) for terms, _ in streams]
    n = len(streams)

    def kernel(place_ref, *refs):
        refs = list(refs)
        groups = [[refs.pop(0) for _ in range(count)] for count in counts]
        kept, sent = refs[:n], refs[n:]
        for i, (group, (_, label)) in enumerate(zip(groups, streams)):
            mine = place_ref[spot(label)]
            kept[i][...] = total([ref[mine] for ref in group])
            gone = total([ref[1 - mine] for ref in group]).astype(bf16)
            if i < joint:
                sent[0][i] = gone
            else:
                sent[i - max(0, joint - 1)][...] = gone

    ins, keeps, sends = [place], [], []
    for terms, _ in streams:
        half, cols = terms[0].size // terms[0].shape[-1] // 2, terms[0].shape[-1]
        ins += [term.reshape(2, half, cols) for term in terms]
        keeps.append(((half, cols), f32))
        sends.append(((half, cols), bf16))
    if joint:
        sends = [((joint, *sends[0][0]), bf16), *sends[joint:]]
    done = call(kernel, ins, keeps + sends, waits=waits, flops=1e8, mib=8)
    return done[:n], done[n:]


def halved_joint(place, keeps, got, labels, joint=True, waits=()):
    n = len(keeps)
    half, cols = keeps[0].shape[0] // 2, keeps[0].shape[1]

    def kernel(place_ref, *refs):
        for i in range(n):
            mine = place_ref[spot(labels[i])]
            kept = refs[i][mine] + refs[n][i, mine].astype(f32)
            gone = refs[i][1 - mine] + refs[n][i, 1 - mine].astype(f32)
            refs[n + 1 + i][...] = kept
            if joint:
                refs[2 * n + 1][i] = gone.astype(bf16)
            else:
                refs[2 * n + 1 + i][...] = gone.astype(bf16)

    ins = [place, *[keep.reshape(2, half, cols) for keep in keeps], got.reshape(n, 2, half, cols)]
    sends = [((n, half, cols), bf16)] if joint else [((half, cols), bf16)] * n
    done = call(kernel, ins, [((half, cols), f32)] * n + sends, waits=waits, flops=1e8, mib=8)
    return done[:n], done[n:]


def halved_norm(place, keeps, gots, labels, norms, joint, waits=()):
    rows, cols = keeps[0].shape
    half, extra = rows // 2, norms[0].shape[0]
    n = len(gots)

    def kernel(place_ref, *refs):
        keep, got, norm, outs = refs[:2], refs[2 : 2 + n], refs[2 + n : -5 if not joint else -4], refs[-5 if not joint else -4 :]
        arrived = [(got[0], 0), (got[-1], 0 if n == 2 else rows)]
        for i in range(2):
            mine = place_ref[spot(labels[i])]
            ref, at = arrived[i]
            here = keep[i][pl.ds(pl.multiple_of(mine * half, half), half)].astype(f32)
            there = keep[i][pl.ds(pl.multiple_of((1 - mine) * half, half), half)].astype(f32)
            here += ref[pl.ds(pl.multiple_of(at + mine * half, half), half)].astype(f32)
            there += ref[pl.ds(pl.multiple_of(at + (1 - mine) * half, half), half)].astype(f32)
            outs[i][...] = here
            if joint:
                outs[3][i * half : (i + 1) * half] = there.astype(bf16)
            else:
                outs[3 + i][:half] = there.astype(bf16)
        if len(norm) == 2:
            value = norm[0][...] + norm[1][...]
        else:
            ref, at = arrived[1]
            value = joined_norm(norm[0][...], ref[at + rows : at + rows + 2 * extra])
        outs[2][...] = value
        split_norm(value, outs[-1], 2 * half if joint else half)

    small = [((half, cols), f32)] * 2 + [((extra, cols), f32)]
    if joint:
        sends = [((2 * half + 2 * extra, cols), bf16)]
    else:
        sends = [((half, cols), bf16), ((half + 2 * extra, cols), bf16)]
    done = call(kernel, (place, *keeps, *gots, *norms), small + sends, waits=waits, flops=1e8, mib=8)
    return done[:2], done[2], done[3:]


def split_norm(value, ref, at):
    rows = value.shape[0]
    high = value.astype(bf16)
    ref[at : at + rows] = high
    ref[at + rows : at + 2 * rows] = (value - high.astype(f32)).astype(bf16)


def joined_norm(value, got):
    rows = value.shape[0]
    high = value.astype(bf16).astype(f32)
    low = (value - high).astype(bf16).astype(f32)
    return (high + low) + (got[:rows].astype(f32) + got[rows:].astype(f32))


def total(terms):
    terms = [term.astype(f32) for term in terms]
    return functools.reduce(jnp.add, terms)


def write_update(outs, at, gradient, states, rate):
    values = advance(*states[:1], gradient, *states[1:], rate)
    for out, value in zip(outs, (gradient, *values)):
        out[at] = value
    if len(outs) > 4:
        outs[4][at] = values[2].astype(bf16)


def update_feed_kernel(keep_e, keep_r, got_ref, *refs):
    states, outs = refs[:6], refs[6:]
    for i, keep in enumerate((keep_e, keep_r)):
        gradient = keep[...] + got_ref[i].astype(f32)
        state = [ref[...] for ref in states[3 * i : 3 * i + 3]]
        write_update(outs[5 * i : 5 * i + 5], slice(None), gradient, state, matrix_rate)


def update_rest_kernel(keep_a, keep_b, got_ref, norm_ref, *refs):
    states, outs = refs[:9], refs[9:]
    rows, cols = keep_a.shape
    r, extra = rows // 2, norm_ref.shape[0]
    for i in range(4):
        keep = (keep_a, keep_b)[i // 2]
        at = (i % 2) * r
        gradient = keep[at : at + r] + got_ref[i * r : (i + 1) * r].astype(f32)
        which, entry = (0, i) if i < 3 else (1, slice(None))
        state = [ref[entry] for ref in states[3 * which : 3 * which + 3]]
        write_update(outs[5 * which : 5 * which + 5], entry, gradient, state, matrix_rate)
    value = joined_norm(norm_ref[...], got_ref[2 * rows : 2 * rows + 2 * extra])
    for j in range(extra // 4):
        at = (slice(None), slice(j * cols, (j + 1) * cols))
        state = [ref[at] for ref in states[6:]]
        write_update(outs[10:], at, value[4 * j : 4 * j + 4], state, norm_rate)


def advance(weight, gradient, moment, average, rate):
    momentum = momentum_decay * moment + gradient
    updated = weight - rate * (gradient + momentum_decay * momentum)
    smoothed = average_decay * average + (1.0 - average_decay) * updated
    return (momentum, smoothed, updated)


def on_device(
    frames,
    cotangent,
    lengths,
    weight_project,
    weight_combine,
    weight_expand,
    weight_reduce,
    moment_project,
    moment_combine,
    moment_expand,
    moment_reduce,
    average_project,
    average_combine,
    average_expand,
    average_reduce,
    norm_params,
    norm_moment,
    norm_average,
):
    own, batch, width = frames.shape
    long, rows = own + 2 * HALO, own + HALO
    parts, n_dp = lax.axis_size("mp"), lax.axis_size("dp")
    me = lax.axis_index("mp")
    start = me * own
    cols, hidden = width // parts, weight_expand.shape[1]
    r = width // n_dp

    sides = [side(label) for label in (ROW, NEAR, *far())]
    place = jnp.concatenate(
        [jnp.stack([start, side(CORE)]).astype(jnp.int32), lengths, jnp.stack(sides).astype(jnp.int32)]
    )
    *outer, last = reversed(far())

    matrices = jnp.concatenate([weight_project, weight_combine[None]], axis=0).astype(bf16)
    one = matrices.reshape(-1, cols)
    for label in outer:
        (one,) = paired(place, [(one, swap(one, *label), label, 1)])
    one_got = swap(one, *last)

    two = lowered([weight_expand, weight_reduce], waits=(one,))
    one_a, one_b = paired(place, [(one, one_got, last, 2)])
    frames_u = jnp.transpose(frames, (1, 0, 2))
    cotangent_u = jnp.transpose(cotangent, (1, 0, 2))
    strip = ((2, batch, HALO, width), bf16)
    near, over = call(
        edge_kernel,
        (place, frames_u, cotangent_u),
        [strip] * 2,
        waits=(one_got,),
        flops=1e8,
        mib=8,
    )
    near = swap(near, *CORE)
    pairs = [(i, i + 1) for i in range(1, parts - 1, 2)]
    over = lax.ppermute(over, "mp", pairs + [(b, a) for a, b in pairs])
    frames_x = call(
        frames_kernel, (place, frames_u, near, over), [((long, width), bf16)] * 2, flops=1e8, mib=8
    )
    got_a, got_b = swap(one_a, *ROW), swap(one_b, *NEAR)
    for label in outer:
        (two,) = paired(place, [(two, swap(two, *label), label, 1)])
    one_a, one_b = paired(
        place, [(one_a, got_a, ROW, 1), (one_b, got_b, NEAR, 1)], waits=(two,)
    )
    got_a, got_b = swap(one_a, *NEAR), swap(one_b, *ROW)
    two_a, two_b = paired(place, [(two, swap(two, *last), last, 2)])
    one_a, one_b = paired(
        place, [(one_a, got_a, NEAR, 1), (one_b, got_b, ROW, 1)], waits=(two_a, *frames_x)
    )
    core_a, core_b = swap(one_a, *CORE), swap(one_b, *CORE)

    per_u = [
        ((long, 3 * width), bf16),
        ((-(-rows // QUERIES), GROUP, QUERIES, width // LANES * KEYS), f32),
        ((own, width), bf16),
        ((rows, width), bf16),
        ((rows, width), f32),
        ((rows, width), bf16),
        ((width, own), bf16),
    ]
    qkv_0, probs_0, first_0, mixed_0, residual_0, second_0, second_t_0, wp, wc = call(
        functools.partial(attend_first_kernel, n_dp),
        (place, frames_x[0], norm_params, one_a, one_b, core_a, core_b),
        per_u + [((width, 3 * width), bf16), ((width, width), bf16)],
        flops=5e9,
    )
    seed, seed_t = call(
        seed_kernel,
        (place, cotangent_u, near, over),
        [((batch, rows, width), bf16), ((width, batch * own), bf16)],
        waits=(second_0,),
        flops=1e8,
        mib=8,
    )

    got_a, got_b = swap(two_a, *ROW), swap(two_b, *NEAR)
    two_a, two_b = paired(place, [(two_a, got_a, ROW, 1), (two_b, got_b, NEAR, 1)], waits=(seed,))
    qkv_1, probs_1, first_1, mixed_1, residual_1, second_1, second_t_1 = call(
        attend_next_kernel,
        (place, frames_x[1], norm_params, wp, wc),
        per_u,
        flops=5e9,
    )
    got_a, got_b = swap(two_a, *NEAR), swap(two_b, *ROW)
    expand, reduce_w = paired(
        place, [(two_a, got_a, NEAR, 1), (two_b, got_b, ROW, 1)], waits=(second_1,)
    )
    expand_got, reduce_got = swap(expand, *CORE), swap(reduce_w, *CORE)

    grads = [((2 * width, hidden), bf16)] * 2
    carried = [((batch, own, width), f32), ((batch, rows, width), f32)]
    feed_scratch = [((width, 2 * hidden), bf16)] * 2 + [
        ((batch * own, 2 * hidden), bf16),
        ((batch, rows, 2 * hidden), bf16),
    ]
    transposed = (seed_t, second_t_0, second_t_1)
    fed, back, keep_e, keep_r = call(
        functools.partial(feed_first_kernel, n_dp),
        (expand, reduce_w, second_0, seed, second_1, *transposed),
        carried + grads,
        feed_scratch,
        flops=8e9,
        smem=0,
    )
    layer, back, send_e, send_r = call(
        functools.partial(feed_last_kernel, n_dp),
        (expand_got, reduce_got, second_0, seed, fed, back, second_1, residual_0, residual_1, *transposed),
        [((batch, own, width), bf16), carried[1]] + grads,
        feed_scratch,
        flops=8e9,
        smem=0,
    )

    two_a, two_b = [keep_e, swap(send_e, *CORE)], [keep_r, swap(send_r, *CORE)]
    pulled = [((own, width), f32), ((own, width), bf16), ((own, 3 * width), bf16), ((2, width), f32)]
    pull_scratch = [((long, 2 * width), f32), ((rows, width), bf16)]
    wide_0, low_0, grad_0, norm_0 = call(
        pull_first_kernel,
        (back, residual_0, seed, wc, norm_params, qkv_0, probs_0),
        pulled,
        pull_scratch,
        flops=8e9,
        smem=0,
    )
    (keep_e, keep_r), (send_e, send_r) = halved(place, [(two_a, NEAR), (two_b, ROW)], waits=(grad_0,))
    two_a, two_b = [keep_e, swap(send_e, *NEAR)], [keep_r, swap(send_r, *ROW)]
    wide_1, low_1, grad_1, norm_1, keep_a, keep_b, send_a, send_b = call(
        functools.partial(pull_last_kernel, n_dp),
        (
            place, back, residual_1, seed, wc, norm_params, qkv_1, probs_1,
            first_0, first_1, mixed_0, mixed_1, grad_0, low_0,
        ),
        pulled + [((4 * width, cols), bf16)] * 4,
        pull_scratch,
        waits=(send_e,),
        flops=10e9,
    )
    one_a, one_b = [keep_a, swap(send_a, *CORE)], [keep_b, swap(send_b, *CORE)]
    first, *others = far()
    (keep_e, keep_r), (sent,) = halved(
        place, [(two_a, first), (two_b, first)], joint=2, waits=(keep_a,)
    )
    (keep_a, keep_b), (send_a, send_b) = halved(place, [(one_a, NEAR), (one_b, ROW)], waits=(sent,))
    gots = swap(send_a, *NEAR), swap(send_b, *ROW)
    two_got = swap(sent, *first)
    grad_in_0, grad_in_1, norm = call(
        finish_kernel,
        (norm_params, wp, grad_0, frames_x[0], wide_0, grad_1, frames_x[1], wide_1, norm_0, norm_1),
        [((own, width), f32), ((own, width), f32), ((4 * parts, cols), f32)],
        waits=(send_a,),
        flops=3e9,
        smem=0,
    )
    norm = norm + swap(norm, *CORE)
    norms = (norm, swap(norm, *ROW))
    (keep_a, keep_b), norm, (send_a, send_b) = halved_norm(
        place, (keep_a, keep_b), gots, (ROW, NEAR), norms, False
    )
    gots = swap(send_a, *ROW), swap(send_b, *NEAR)
    (keep_e, keep_r), (send_e, send_r) = halved_joint(
        place, (keep_e, keep_r), two_got, (ROW, NEAR), joint=False, waits=(send_a,)
    )
    two_a, two_b = [keep_e, swap(send_e, *ROW)], [keep_r, swap(send_r, *NEAR)]
    pending = (send_e,)
    second, *others = others
    (keep_e, keep_r), (sent,) = halved(place, [(two_a, second), (two_b, second)], joint=2)
    two_got = swap(sent, *second)
    for label in others:
        (keep_e, keep_r), (sent,) = halved_joint(place, (keep_e, keep_r), two_got, (label, label))
        two_got = swap(sent, *label)
    for label in far():
        (keep_a, keep_b), norm, (sent,) = halved_norm(
            place, (keep_a, keep_b), gots, (label, label), (norm,), True, waits=pending
        )
        gots, pending = (swap(sent, *label),), ()

    plain = lambda x: [(x.shape, f32)] * 4
    weighed = lambda x: plain(x) + [(x.shape, bf16)]
    updated = call(
        update_feed_kernel,
        (
            keep_e, keep_r, two_got, weight_expand, moment_expand, average_expand,
            weight_reduce, moment_reduce, average_reduce,
        ),
        weighed(weight_expand) + weighed(weight_reduce),
        flops=1e8,
        smem=0,
        mib=8,
    )
    gradient_expand, mom_expand, avg_expand, new_expand, low_expand = updated[:5]
    gradient_reduce, mom_reduce, avg_reduce, new_reduce, low_reduce = updated[5:]
    updated = call(
        update_rest_kernel,
        (
            keep_a, keep_b, gots[0], norm, weight_project, moment_project, average_project,
            weight_combine, moment_combine, average_combine, norm_params, norm_moment, norm_average,
        ),
        weighed(weight_project) + weighed(weight_combine) + plain(norm_params),
        flops=1e8,
        smem=0,
        mib=8,
    )
    gradient_project, mom_project, avg_project, new_project, low_project = updated[:5]
    gradient_combine, mom_combine, avg_combine, new_combine, low_combine = updated[5:10]
    norm_gradient, mom_norms, avg_norms, new_norms = updated[10:]
    layer_out = jnp.transpose(layer, (1, 0, 2))
    input_gradient = jnp.transpose(jnp.stack([grad_in_0, grad_in_1]), (1, 0, 2))
    return (
        layer_out,
        input_gradient,
        gradient_project,
        gradient_combine,
        gradient_expand,
        gradient_reduce,
        mom_project,
        mom_combine,
        mom_expand,
        mom_reduce,
        avg_project,
        avg_combine,
        avg_expand,
        avg_reduce,
        new_project,
        new_combine,
        new_expand,
        new_reduce,
        low_project,
        low_combine,
        low_expand,
        low_reduce,
        norm_gradient,
        mom_norms,
        avg_norms,
        new_norms,
    )


def solution(mesh):
    tokens = P("mp", "dp", None)
    stacked, matrix = P(None, "dp", "mp"), P("dp", "mp")
    weights = (stacked, matrix, matrix, matrix)
    in_specs = (tokens, tokens, P("dp")) + weights * 3 + (P(),) * 3
    out_specs = (tokens, tokens) + weights * 5 + (P(),) * 4
    return jax.shard_map(
        on_device, mesh=mesh, in_specs=in_specs, out_specs=out_specs, check_vma=False
    )
```

```python
import functools
import math

import jax
import jax.numpy as jnp
from jax import lax
from jax.experimental import pallas as pl
from jax.experimental.pallas import tpu as pltpu
from jax.sharding import PartitionSpec as P

HEADS = 8
HEAD_DIM = 64
WINDOW = 10
HALO = 16

eps_norm = 1e-05
momentum_decay = 0.9
average_decay = 0.6
matrix_rate = 0.0001
norm_rate = 0.001
masked_score = -1e30

GROUP = 4
LANES = GROUP * HEAD_DIM
QUERIES = 112
KEYS = QUERIES + HALO

f32 = jnp.float32
bf16 = jnp.bfloat16


def mm(a, b):
    return lax.dot_general(a, b, (((1,), (0,)), ((), ())), preferred_element_type=f32)


def mm_bt(a, b):
    return lax.dot_general(a, b, (((1,), (1,)), ((), ())), preferred_element_type=f32)


def mm_at(a, b):
    return lax.dot_general(a, b, (((0,), (0,)), ((), ())), preferred_element_type=f32)


def normalise(values):
    center = values - jnp.mean(values, axis=-1, keepdims=True)
    spread = jnp.mean(center * center, axis=-1, keepdims=True)
    inverse = lax.rsqrt(spread + eps_norm)
    return center * inverse, inverse


def norm_backward(values, gain, upstream):
    scaled, inverse = normalise(values)
    weighted = upstream * gain
    inner = (
        weighted
        - jnp.mean(weighted, axis=-1, keepdims=True)
        - scaled * jnp.mean(weighted * scaled, axis=-1, keepdims=True)
    )
    return inner * inverse, upstream * scaled


def query_blocks(total):
    blocks = []
    at = HALO
    while at < total:
        rows = min(QUERIES, total - at)
        blocks.append((at, rows, min(at - HALO, total - KEYS)))
        at += rows
    return blocks


def band(block, start, length):
    q0, rows, k0 = block
    query = lax.broadcasted_iota(jnp.int32, (rows, KEYS), 0)
    key = lax.broadcasted_iota(jnp.int32, (rows, KEYS), 1)
    behind = query - key + (q0 - k0)
    time = key + (start + k0 - HALO)
    inside = (time < length) | (behind == 0)
    return (behind >= 0) & (behind <= WINDOW) & (time >= 0) & inside


def head_lanes():
    lane = lax.broadcasted_iota(jnp.int32, (1, LANES), 1)
    return [(lane >= h * HEAD_DIM) & (lane < (h + 1) * HEAD_DIM) for h in range(GROUP)]


def stack_heads(block):
    zero = jnp.zeros_like(block)
    return jnp.concatenate([jnp.where(m, block, zero) for m in head_lanes()], axis=0)


def merge_heads(stacked, rows):
    masks = head_lanes()
    out = jnp.where(masks[0], stacked[:rows], 0.0)
    for h in range(1, GROUP):
        out = jnp.where(masks[h], stacked[h * rows : (h + 1) * rows], out)
    return out


def softmax_rows(scores, allowed):
    scores = jnp.where(allowed, scores * (1.0 / math.sqrt(HEAD_DIM)), masked_score)
    raised = jnp.exp(scores - jnp.max(scores, axis=-1, keepdims=True))
    return raised / jnp.sum(raised, axis=-1, keepdims=True)


def block_order(n_dp, near_first, split=False):
    row, near, far_bits = -1, 0, list(range(1, (n_dp - 1).bit_length()))
    first, second = (near, row) if near_first else (row, near)
    bits = [first, far_bits[0], second, *far_bits[1:]] if split else [first, second, *far_bits]
    blocks = []
    for at in range(2 * n_dp):
        value = {bit: (at >> (len(bits) - 1 - i)) & 1 for i, bit in enumerate(bits)}
        blocks.append((value[row], sum(value[bit] << bit for bit in bits if bit != row)))
    return blocks


def place_weights(n_dp, core, own_a, own_b, got_a, got_b, wp_ref, wc_ref):
    width, cols = wc_ref.shape[0], own_a.shape[1]
    r = width // n_dp
    for which, ref_a, ref_b in ((core, own_a, own_b), (1 - core, got_a, got_b)):
        for ref, first, near_first in ((ref_a, 0, True), (ref_b, 2, False)):
            for p, (y, d) in enumerate(block_order(n_dp, near_first)):
                at = pl.multiple_of((2 * y + which) * cols, cols)
                for i in range(2):
                    block = ref[(2 * p + i) * r : (2 * p + i + 1) * r]
                    if first + i < 3:
                        wp_ref[d * r : (d + 1) * r, pl.ds((first + i) * width + at, cols)] = block
                    else:
                        wc_ref[d * r : (d + 1) * r, pl.ds(at, cols)] = block


def edge_kernel(place_ref, frames_ref, cotangent_ref, near_ref, over_ref):
    last = frames_ref.shape[1] - HALO
    for core, early, late in ((0, over_ref, near_ref), (1, near_ref, over_ref)):

        @pl.when(place_ref[1] == core)
        def _():
            early[0] = frames_ref[:, :HALO]
            early[1] = cotangent_ref[:, :HALO]
            late[0] = frames_ref[:, last:]
            late[1] = frames_ref[:, last:]


def frames_kernel(place_ref, frames_ref, near_ref, over_ref, *outs):
    own = frames_ref.shape[1]
    for u, out in enumerate(outs):
        out[HALO : HALO + own] = frames_ref[u]
    for core, left, right in ((0, over_ref, near_ref), (1, near_ref, over_ref)):

        @pl.when(place_ref[1] == core)
        def _():
            for u, out in enumerate(outs):
                out[:HALO] = left[0, u]
                out[HALO + own :] = right[0, u]


def seed_kernel(place_ref, cotangent_ref, near_ref, over_ref, seed_ref, seed_t_ref):
    own = cotangent_ref.shape[1]
    for u in range(seed_ref.shape[0]):

        def valid(first, count):
            time = lax.broadcasted_iota(jnp.int32, (count, 1), 0) + (place_ref[0] + first)
            return time < place_ref[2 + u]

        mine = cotangent_ref[u]
        mine = jnp.where(valid(0, own), mine, jnp.zeros_like(mine))
        seed_ref[u, :own] = mine
        seed_t_ref[:, u * own : (u + 1) * own] = mine.T
        theirs = jnp.where(place_ref[1] == 0, near_ref[1, u], over_ref[1, u])
        seed_ref[u, own:] = jnp.where(valid(own, HALO), theirs, jnp.zeros_like(theirs))


def attend_one(
    u, place_ref, frames_ref, norms_ref, wp_ref, wc_ref,
    qkv_ref, probs_ref, first_ref, mixed_ref, residual_ref, second_ref, second_t_ref,
):
    total, width = frames_ref.shape
    own = first_ref.shape[0]
    start, length = place_ref[0], place_ref[2 + u]
    scaled, _ = normalise(frames_ref[...].astype(f32))
    normed = (scaled * norms_ref[0:1] + norms_ref[1:2]).astype(bf16)
    first_ref[...] = normed[HALO : HALO + own]
    qkv_ref[...] = mm(normed, wp_ref[...]).astype(bf16)
    def group(hg, carry):
        at = pl.multiple_of(hg * LANES, LANES)
        here = pl.ds(pl.multiple_of(hg * KEYS, KEYS), KEYS)
        for b, block in enumerate(query_blocks(total)):
            q0, rows, k0 = block
            allowed = band(block, start, length)
            queries = stack_heads(qkv_ref[q0 : q0 + rows, pl.ds(at, LANES)])
            keys = qkv_ref[k0 : k0 + KEYS, pl.ds(width + at, LANES)]
            values = qkv_ref[k0 : k0 + KEYS, pl.ds(2 * width + at, LANES)]
            scores = mm_bt(queries, keys)
            low_probs = []
            for h in range(GROUP):
                probs = softmax_rows(scores[h * rows : (h + 1) * rows], allowed)
                probs_ref[b, h, :rows, here] = probs
                low_probs.append(probs.astype(bf16))
            out = merge_heads(mm(jnp.concatenate(low_probs, axis=0), values), rows)
            mixed_ref[q0 - HALO : q0 - HALO + rows, pl.ds(at, LANES)] = out.astype(bf16)
        return carry

    lax.fori_loop(0, width // LANES, group, 0)
    residual = frames_ref[HALO:total].astype(f32) + mm_bt(mixed_ref[...], wc_ref[...])
    residual_ref[...] = residual
    scaled, _ = normalise(residual)
    second_ref[...] = (scaled * norms_ref[2:3] + norms_ref[3:4]).astype(bf16)
    second_t_ref[...] = second_ref[:own].T


def attend_first_kernel(
    n_dp, place_ref, frames_ref, norms_ref, own_a, own_b, got_a, got_b, *refs
):
    *outs, wp_ref, wc_ref = refs
    place_weights(n_dp, place_ref[1], own_a, own_b, got_a, got_b, wp_ref, wc_ref)
    attend_one(0, place_ref, frames_ref, norms_ref, wp_ref, wc_ref, *outs)


def attend_next_kernel(place_ref, frames_ref, norms_ref, wp_ref, wc_ref, *refs):
    attend_one(1, place_ref, frames_ref, norms_ref, wp_ref, wc_ref, *refs)


def gelu_parts(value):
    slope = math.sqrt(2.0 / math.pi)
    square = value * value
    tanh = jnp.tanh(value * (slope + (slope * 0.044715) * square))
    half = 0.5 + 0.5 * tanh
    curve = half + (0.5 * value) * (1.0 - tanh * tanh) * (
        slope + (slope * 3.0 * 0.044715) * square
    )
    return value * half, curve


def feed_half(
    n_dp, seconds, seconds_t, seed_ref, seed_t_ref, we_ref, wr_ref, ge_ref, gr_ref,
    wide_e, wide_r, active_ref, grad_ref, second_ref, add_fed, add_back,
):
    own = seconds_t[0].shape[1]
    width, hidden = wide_e.shape[0], we_ref.shape[1]
    r = width // n_dp
    for ref, wide, near_first in ((we_ref, wide_e, True), (wr_ref, wide_r, False)):
        for p, (y, d) in enumerate(block_order(n_dp, near_first)):
            wide[d * r : (d + 1) * r, y * hidden : (y + 1) * hidden] = ref[p * r : (p + 1) * r]
    for u, ref in enumerate(seconds):
        second_ref[u] = ref[...]

    def one(u, carry):
        rows = pl.ds(pl.multiple_of(u * own, own), own)
        active, curve = gelu_parts(mm(second_ref[u], wide_e[...]))
        active_ref[rows] = active[:own].astype(bf16)
        grad_ref[u] = (mm(seed_ref[u], wide_r[...]) * curve).astype(bf16)
        add_fed(u, mm_bt(active_ref[rows], wide_r[...]))
        add_back(u, mm_bt(grad_ref[u], wide_e[...]))
        return carry

    lax.fori_loop(0, len(seconds), one, 0)
    total_r = mm(seed_t_ref[...], active_ref[...])
    total_e = mm(seconds_t[0][...], grad_ref[0, :own]) + mm(seconds_t[1][...], grad_ref[1, :own])
    for total, ref, near_first in ((total_e, ge_ref, True), (total_r, gr_ref, False)):
        for p, (y, d) in enumerate(block_order(n_dp, near_first, True)):
            block = total[d * r : (d + 1) * r, y * hidden : (y + 1) * hidden]
            ref[p * r : (p + 1) * r] = block.astype(bf16)


def feed_first_kernel(n_dp, we_ref, wr_ref, n0, seed_ref, n1, seed_t_ref, t0, t1, *refs):
    fed_ref, back_ref, ge_ref, gr_ref, *scratch = refs

    def add_fed(u, value):
        fed_ref[u] = value

    def add_back(u, value):
        back_ref[u] = value

    feed_half(
        n_dp, (n0, n1), (t0, t1), seed_ref, seed_t_ref, we_ref, wr_ref, ge_ref, gr_ref,
        *scratch, add_fed, add_back,
    )


def feed_last_kernel(
    n_dp, we_ref, wr_ref, n0, seed_ref, fed_in, back_in, n1, r0, r1, seed_t_ref, t0, t1, *refs
):
    out_ref, back_ref, ge_ref, gr_ref, *scratch = refs
    own = out_ref.shape[1]

    def add_fed(u, value):
        residual = jnp.where(u == 0, r0[:own], r1[:own])
        out_ref[u] = (residual + (fed_in[u] + value)).astype(bf16)

    def add_back(u, value):
        back_ref[u] = back_in[u] + value

    feed_half(
        n_dp, (n0, n1), (t0, t1), seed_ref, seed_t_ref, we_ref, wr_ref, ge_ref, gr_ref,
        *scratch, add_fed, add_back,
    )


def pull_one(
    u, back_ref, residual_ref, seed_ref, wc_ref, norms_ref, qkv_ref, probs_ref,
    wide_ref, low_ref, grad_ref, norm_ref, grad_kv_ref, mixed_g_ref,
):
    total = qkv_ref.shape[0]
    own, width = low_ref.shape
    upstream = back_ref[u]
    back, gained = norm_backward(residual_ref[...], norms_ref[2:3], upstream)
    norm_ref[0:1] = jnp.sum(gained[:own], axis=0, keepdims=True)
    norm_ref[1:2] = jnp.sum(upstream[:own], axis=0, keepdims=True)
    wide = seed_ref[u].astype(f32) + back
    wide_ref[...] = wide[:own]
    low = wide.astype(bf16)
    low_ref[...] = low[:own]
    mixed_g_ref[...] = mm(low, wc_ref[...]).astype(bf16)
    grad_kv_ref[...] = jnp.zeros_like(grad_kv_ref)
    scale = 1.0 / math.sqrt(HEAD_DIM)
    def group(hg, carry):
        at = pl.multiple_of(hg * LANES, LANES)
        here = pl.ds(pl.multiple_of(hg * KEYS, KEYS), KEYS)
        first_lanes, second_lanes = pl.ds(at, LANES), pl.ds(width + at, LANES)
        for b, block in enumerate(query_blocks(total)):
            q0, rows, k0 = block
            queries = stack_heads(qkv_ref[q0 : q0 + rows, first_lanes])
            keys = qkv_ref[k0 : k0 + KEYS, second_lanes]
            values = qkv_ref[k0 : k0 + KEYS, pl.ds(2 * width + at, LANES)]
            upper = stack_heads(mixed_g_ref[q0 - HALO : q0 - HALO + rows, first_lanes])
            grad_probs = mm_bt(upper, values)
            low_probs, grad_scores = [], []
            for h in range(GROUP):
                probs = probs_ref[b, h, :rows, here]
                grad = grad_probs[h * rows : (h + 1) * rows]
                inner = jnp.sum(probs * grad, axis=-1, keepdims=True)
                low_probs.append(probs.astype(bf16))
                grad_scores.append((probs * (grad - inner)).astype(bf16))
            low_probs = jnp.concatenate(low_probs, axis=0)
            grad_scores = jnp.concatenate(grad_scores, axis=0)
            grad_q = merge_heads(mm(grad_scores, keys), rows) * scale
            mine = min(rows, HALO + own - q0)
            if mine > 0:
                grad_ref[q0 - HALO : q0 - HALO + mine, first_lanes] = grad_q[:mine].astype(bf16)
            grad_kv_ref[k0 : k0 + KEYS, first_lanes] += mm_at(grad_scores, queries) * scale
            grad_kv_ref[k0 : k0 + KEYS, second_lanes] += mm_at(low_probs, upper)
        return carry

    lax.fori_loop(0, width // LANES, group, 0)
    grad_ref[:, width:] = grad_kv_ref[HALO : HALO + own].astype(bf16)


def pull_first_kernel(*refs):
    pull_one(0, *refs)


def pull_last_kernel(
    n_dp, place_ref, back_ref, residual_ref, seed_ref, wc_ref, norms_ref, qkv_ref, probs_ref,
    first_0, first_1, mixed_0, mixed_1, grad_0, low_0, *refs,
):
    wide_ref, low_ref, grad_ref, norm_ref, keep_a, keep_b, send_a, send_b, grad_kv_ref, mixed_g_ref = refs
    pull_one(
        1, back_ref, residual_ref, seed_ref, wc_ref, norms_ref, qkv_ref, probs_ref,
        wide_ref, low_ref, grad_ref, norm_ref, grad_kv_ref, mixed_g_ref,
    )
    own, width = low_ref.shape
    core, cols, r = place_ref[1], keep_a.shape[1], width // n_dp
    firsts = first_0[...].T, first_1[...].T
    lows = low_0[...].T, low_ref[...].T
    where = {
        near_first: {block: p for p, block in enumerate(block_order(n_dp, near_first))}
        for near_first in (True, False)
    }
    for i in range(4):
        keep, send, at = (keep_a, send_a, where[True]) if i < 2 else (keep_b, send_b, where[False])
        for y in range(2):
            lanes = slice(2 * y * cols, 2 * (y + 1) * cols)
            if i < 3:
                inner = slice(i * width + lanes.start, i * width + lanes.stop)
                value = mm(firsts[0], grad_0[:, inner]) + mm(firsts[1], grad_ref[:, inner])
            else:
                value = mm(lows[0], mixed_0[:own, lanes]) + mm(lows[1], mixed_1[:own, lanes])
            mine = jnp.where(core == 0, value[:, :cols], value[:, cols:])
            other = jnp.where(core == 0, value[:, cols:], value[:, :cols])
            for d in range(n_dp):
                to = (2 * at[y, d] + i % 2) * r
                keep[to : to + r] = mine[d * r : (d + 1) * r].astype(bf16)
                send[to : to + r] = other[d * r : (d + 1) * r].astype(bf16)


def fold_norm(ref, first, value):
    cols = ref.shape[1]
    for j in range(value.shape[1] // cols):
        ref[4 * j + first : 4 * j + first + value.shape[0]] = value[:, j * cols : (j + 1) * cols]


def finish_kernel(norms_ref, wp_ref, grad_0, frames_0, wide_0, grad_1, frames_1, wide_1, norm_0, norm_1, out_0, out_1, norm_ref):
    own = out_0.shape[0]
    gains, shifts = [], []
    for grad_ref, frames_ref, wide_ref, out_ref in (
        (grad_0, frames_0, wide_0, out_0),
        (grad_1, frames_1, wide_1, out_1),
    ):
        upstream = mm_bt(grad_ref[...], wp_ref[...])
        back, gained = norm_backward(
            frames_ref[HALO : HALO + own].astype(f32), norms_ref[0:1], upstream
        )
        gains.append(jnp.sum(gained, axis=0, keepdims=True))
        shifts.append(jnp.sum(upstream, axis=0, keepdims=True))
        out_ref[...] = wide_ref[...] + back
    fold_norm(norm_ref, 0, gains[0] + gains[1])
    fold_norm(norm_ref, 1, shifts[0] + shifts[1])
    fold_norm(norm_ref, 2, norm_0[...] + norm_1[...])


VM = pl.BlockSpec(memory_space=pltpu.VMEM)
SM = pl.BlockSpec(memory_space=pltpu.SMEM)
MIB = 1024 * 1024


def call(kernel, ins, outs, scratch=(), waits=(), flops=1e9, smem=1, mib=16):
    n, m = len(ins), len(outs)
    away = pl.BlockSpec(memory_space=pl.ANY)

    def body(*refs):
        kernel(*refs[:n], *refs[n + len(waits) :])

    return pl.pallas_call(
        body,
        out_shape=tuple(jax.ShapeDtypeStruct(shape, kind) for shape, kind in outs),
        in_specs=[SM] * smem + [VM] * (n - smem) + [away] * len(waits),
        out_specs=(VM,) * m,
        scratch_shapes=[pltpu.VMEM(shape, kind) for shape, kind in scratch],
        compiler_params=pltpu.CompilerParams(vmem_limit_bytes=mib * MIB),
        cost_estimate=pl.CostEstimate(flops=int(flops), bytes_accessed=6000000, transcendentals=0),
    )(*ins, *waits)


def swap(value, axis, bit):
    n = lax.axis_size(axis)
    return lax.ppermute(value, axis, [(i, i ^ (1 << bit)) for i in range(n)])


CORE, ROW, NEAR = ("mp", 0), ("mp", 1), ("dp", 0)


def far():
    return [("dp", b) for b in range(1, (lax.axis_size("dp") - 1).bit_length())]


def side(label):
    return (lax.axis_index(label[0]) >> label[1]) & 1


def spot(label):
    return {CORE: 1, ROW: 4, NEAR: 5}.get(label, 5 + label[1])


def paired(place, streams, waits=()):
    def kernel(place_ref, *refs):
        outs = list(refs[2 * len(streams) :])
        for i, (_, _, label, parts) in enumerate(streams):
            mine, got = refs[2 * i], refs[2 * i + 1]
            high = place_ref[spot(label)]
            for part in range(parts):
                out = outs.pop(0)
                out[high] = mine[:, part]
                out[1 - high] = got[:, part]

    ins, outs = [place], []
    for mine, got, label, parts in streams:
        blocks = lax.axis_size("dp") // 4 if parts > 1 else 1
        shape = (blocks, parts, mine.shape[0] // blocks // parts, mine.shape[1])
        ins += [mine.reshape(shape), got.reshape(shape)]
        outs += [((2, blocks, *shape[2:]), mine.dtype)] * parts
    return [x.reshape(-1, x.shape[-1]) for x in call(kernel, ins, outs, waits=waits, flops=1e8, mib=8)]


def lowered(arrays, waits):
    rows = [x.shape[0] for x in arrays]

    def kernel(*refs):
        at = 0
        for ref, count in zip(refs, rows):
            refs[-1][at : at + count] = ref[...].astype(bf16)
            at += count

    return call(kernel, arrays, [((sum(rows), arrays[0].shape[1]), bf16)], waits=waits, flops=1e8, smem=0, mib=8)[0]


def halved(place, streams, joint=0, waits=()):
    counts = [len(terms) for terms, _ in streams]
    n = len(streams)

    def kernel(place_ref, *refs):
        refs = list(refs)
        groups = [[refs.pop(0) for _ in range(count)] for count in counts]
        kept, sent = refs[:n], refs[n:]
        for i, (group, (_, label)) in enumerate(zip(groups, streams)):
            mine = place_ref[spot(label)]
            kept[i][...] = total([ref[mine] for ref in group])
            gone = total([ref[1 - mine] for ref in group]).astype(bf16)
            if i < joint:
                sent[0][i] = gone
            else:
                sent[i - max(0, joint - 1)][...] = gone

    ins, keeps, sends = [place], [], []
    for terms, _ in streams:
        half, cols = terms[0].size // terms[0].shape[-1] // 2, terms[0].shape[-1]
        ins += [term.reshape(2, half, cols) for term in terms]
        keeps.append(((half, cols), f32))
        sends.append(((half, cols), bf16))
    if joint:
        sends = [((joint, *sends[0][0]), bf16), *sends[joint:]]
    done = call(kernel, ins, keeps + sends, waits=waits, flops=1e8, mib=8)
    return done[:n], done[n:]


def halved_joint(place, keeps, got, labels, joint=True, waits=()):
    n = len(keeps)
    half, cols = keeps[0].shape[0] // 2, keeps[0].shape[1]

    def kernel(place_ref, *refs):
        for i in range(n):
            mine = place_ref[spot(labels[i])]
            kept = refs[i][mine] + refs[n][i, mine].astype(f32)
            gone = refs[i][1 - mine] + refs[n][i, 1 - mine].astype(f32)
            refs[n + 1 + i][...] = kept
            if joint:
                refs[2 * n + 1][i] = gone.astype(bf16)
            else:
                refs[2 * n + 1 + i][...] = gone.astype(bf16)

    ins = [place, *[keep.reshape(2, half, cols) for keep in keeps], got.reshape(n, 2, half, cols)]
    sends = [((n, half, cols), bf16)] if joint else [((half, cols), bf16)] * n
    done = call(kernel, ins, [((half, cols), f32)] * n + sends, waits=waits, flops=1e8, mib=8)
    return done[:n], done[n:]


def halved_norm(place, keeps, gots, labels, norms, joint, waits=()):
    rows, cols = keeps[0].shape
    half, extra = rows // 2, norms[0].shape[0]
    n = len(gots)

    def kernel(place_ref, *refs):
        keep, got, norm, outs = refs[:2], refs[2 : 2 + n], refs[2 + n : -5 if not joint else -4], refs[-5 if not joint else -4 :]
        arrived = [(got[0], 0), (got[-1], 0 if n == 2 else rows)]
        for i in range(2):
            mine = place_ref[spot(labels[i])]
            ref, at = arrived[i]
            here = keep[i][pl.ds(pl.multiple_of(mine * half, half), half)].astype(f32)
            there = keep[i][pl.ds(pl.multiple_of((1 - mine) * half, half), half)].astype(f32)
            here += ref[pl.ds(pl.multiple_of(at + mine * half, half), half)].astype(f32)
            there += ref[pl.ds(pl.multiple_of(at + (1 - mine) * half, half), half)].astype(f32)
            outs[i][...] = here
            if joint:
                outs[3][i * half : (i + 1) * half] = there.astype(bf16)
            else:
                outs[3 + i][:half] = there.astype(bf16)
        if len(norm) == 2:
            value = norm[0][...] + norm[1][...]
        else:
            ref, at = arrived[1]
            value = joined_norm(norm[0][...], ref[at + rows : at + rows + 2 * extra])
        outs[2][...] = value
        split_norm(value, outs[-1], 2 * half if joint else half)

    small = [((half, cols), f32)] * 2 + [((extra, cols), f32)]
    if joint:
        sends = [((2 * half + 2 * extra, cols), bf16)]
    else:
        sends = [((half, cols), bf16), ((half + 2 * extra, cols), bf16)]
    done = call(kernel, (place, *keeps, *gots, *norms), small + sends, waits=waits, flops=1e8, mib=8)
    return done[:2], done[2], done[3:]


def split_norm(value, ref, at):
    rows = value.shape[0]
    high = value.astype(bf16)
    ref[at : at + rows] = high
    ref[at + rows : at + 2 * rows] = (value - high.astype(f32)).astype(bf16)


def joined_norm(value, got):
    rows = value.shape[0]
    high = value.astype(bf16).astype(f32)
    low = (value - high).astype(bf16).astype(f32)
    return (high + low) + (got[:rows].astype(f32) + got[rows:].astype(f32))


def total(terms):
    terms = [term.astype(f32) for term in terms]
    return functools.reduce(jnp.add, terms)


def write_update(outs, at, gradient, states, rate):
    values = advance(*states[:1], gradient, *states[1:], rate)
    for out, value in zip(outs, (gradient, *values)):
        out[at] = value
    if len(outs) > 4:
        outs[4][at] = values[2].astype(bf16)


def update_feed_kernel(keep_e, keep_r, got_ref, *refs):
    states, outs = refs[:6], refs[6:]
    for i, keep in enumerate((keep_e, keep_r)):
        gradient = keep[...] + got_ref[i].astype(f32)
        state = [ref[...] for ref in states[3 * i : 3 * i + 3]]
        write_update(outs[5 * i : 5 * i + 5], slice(None), gradient, state, matrix_rate)


def update_rest_kernel(keep_a, keep_b, got_ref, norm_ref, *refs):
    states, outs = refs[:9], refs[9:]
    rows, cols = keep_a.shape
    r, extra = rows // 2, norm_ref.shape[0]
    for i in range(4):
        keep = (keep_a, keep_b)[i // 2]
        at = (i % 2) * r
        gradient = keep[at : at + r] + got_ref[i * r : (i + 1) * r].astype(f32)
        which, entry = (0, i) if i < 3 else (1, slice(None))
        state = [ref[entry] for ref in states[3 * which : 3 * which + 3]]
        write_update(outs[5 * which : 5 * which + 5], entry, gradient, state, matrix_rate)
    value = joined_norm(norm_ref[...], got_ref[2 * rows : 2 * rows + 2 * extra])
    for j in range(extra // 4):
        at = (slice(None), slice(j * cols, (j + 1) * cols))
        state = [ref[at] for ref in states[6:]]
        write_update(outs[10:], at, value[4 * j : 4 * j + 4], state, norm_rate)


def advance(weight, gradient, moment, average, rate):
    momentum = momentum_decay * moment + gradient
    updated = weight - rate * (gradient + momentum_decay * momentum)
    smoothed = average_decay * average + (1.0 - average_decay) * updated
    return (momentum, smoothed, updated)


def on_device(
    frames,
    cotangent,
    lengths,
    weight_project,
    weight_combine,
    weight_expand,
    weight_reduce,
    moment_project,
    moment_combine,
    moment_expand,
    moment_reduce,
    average_project,
    average_combine,
    average_expand,
    average_reduce,
    norm_params,
    norm_moment,
    norm_average,
):
    own, batch, width = frames.shape
    long, rows = own + 2 * HALO, own + HALO
    parts, n_dp = lax.axis_size("mp"), lax.axis_size("dp")
    me = lax.axis_index("mp")
    start = me * own
    cols, hidden = width // parts, weight_expand.shape[1]
    r = width // n_dp

    sides = [side(label) for label in (ROW, NEAR, *far())]
    place = jnp.concatenate(
        [jnp.stack([start, side(CORE)]).astype(jnp.int32), lengths, jnp.stack(sides).astype(jnp.int32)]
    )
    *outer, last = reversed(far())

    matrices = jnp.concatenate([weight_project, weight_combine[None]], axis=0).astype(bf16)
    one = matrices.reshape(-1, cols)
    for label in outer:
        (one,) = paired(place, [(one, swap(one, *label), label, 1)])
    one_got = swap(one, *last)

    two = lowered([weight_expand, weight_reduce], waits=(one,))
    one_a, one_b = paired(place, [(one, one_got, last, 2)])
    frames_u = jnp.transpose(frames, (1, 0, 2))
    cotangent_u = jnp.transpose(cotangent, (1, 0, 2))
    strip = ((2, batch, HALO, width), bf16)
    near, over = call(
        edge_kernel,
        (place, frames_u, cotangent_u),
        [strip] * 2,
        waits=(one_got,),
        flops=1e8,
        mib=8,
    )
    near = swap(near, *CORE)
    pairs = [(i, i + 1) for i in range(1, parts - 1, 2)]
    over = lax.ppermute(over, "mp", pairs + [(b, a) for a, b in pairs])
    frames_x = call(
        frames_kernel, (place, frames_u, near, over), [((long, width), bf16)] * 2, flops=1e8, mib=8
    )
    got_a, got_b = swap(one_a, *ROW), swap(one_b, *NEAR)
    for label in outer:
        (two,) = paired(place, [(two, swap(two, *label), label, 1)])
    one_a, one_b = paired(
        place, [(one_a, got_a, ROW, 1), (one_b, got_b, NEAR, 1)], waits=(two,)
    )
    got_a, got_b = swap(one_a, *NEAR), swap(one_b, *ROW)
    two_a, two_b = paired(place, [(two, swap(two, *last), last, 2)])
    one_a, one_b = paired(
        place, [(one_a, got_a, NEAR, 1), (one_b, got_b, ROW, 1)], waits=(two_a, *frames_x)
    )
    core_a, core_b = swap(one_a, *CORE), swap(one_b, *CORE)

    per_u = [
        ((long, 3 * width), bf16),
        ((-(-rows // QUERIES), GROUP, QUERIES, width // LANES * KEYS), f32),
        ((own, width), bf16),
        ((rows, width), bf16),
        ((rows, width), f32),
        ((rows, width), bf16),
        ((width, own), bf16),
    ]
    qkv_0, probs_0, first_0, mixed_0, residual_0, second_0, second_t_0, wp, wc = call(
        functools.partial(attend_first_kernel, n_dp),
        (place, frames_x[0], norm_params, one_a, one_b, core_a, core_b),
        per_u + [((width, 3 * width), bf16), ((width, width), bf16)],
        flops=5e9,
    )
    seed, seed_t = call(
        seed_kernel,
        (place, cotangent_u, near, over),
        [((batch, rows, width), bf16), ((width, batch * own), bf16)],
        waits=(second_0,),
        flops=1e8,
        mib=8,
    )

    got_a, got_b = swap(two_a, *ROW), swap(two_b, *NEAR)
    two_a, two_b = paired(place, [(two_a, got_a, ROW, 1), (two_b, got_b, NEAR, 1)], waits=(seed,))
    qkv_1, probs_1, first_1, mixed_1, residual_1, second_1, second_t_1 = call(
        attend_next_kernel,
        (place, frames_x[1], norm_params, wp, wc),
        per_u,
        flops=5e9,
    )
    got_a, got_b = swap(two_a, *NEAR), swap(two_b, *ROW)
    expand, reduce_w = paired(
        place, [(two_a, got_a, NEAR, 1), (two_b, got_b, ROW, 1)], waits=(second_1,)
    )
    expand_got, reduce_got = swap(expand, *CORE), swap(reduce_w, *CORE)

    grads = [((2 * width, hidden), bf16)] * 2
    carried = [((batch, own, width), f32), ((batch, rows, width), f32)]
    feed_scratch = [((width, 2 * hidden), bf16)] * 2 + [
        ((batch * own, 2 * hidden), bf16),
        ((batch, rows, 2 * hidden), bf16),
        ((batch, rows, width), bf16),
    ]
    transposed = (seed_t, second_t_0, second_t_1)
    fed, back, keep_e, keep_r = call(
        functools.partial(feed_first_kernel, n_dp),
        (expand, reduce_w, second_0, seed, second_1, *transposed),
        carried + grads,
        feed_scratch,
        flops=8e9,
        smem=0,
    )
    layer, back, send_e, send_r = call(
        functools.partial(feed_last_kernel, n_dp),
        (expand_got, reduce_got, second_0, seed, fed, back, second_1, residual_0, residual_1, *transposed),
        [((batch, own, width), bf16), carried[1]] + grads,
        feed_scratch,
        flops=8e9,
        smem=0,
    )

    two_a, two_b = [keep_e, swap(send_e, *CORE)], [keep_r, swap(send_r, *CORE)]
    pulled = [((own, width), f32), ((own, width), bf16), ((own, 3 * width), bf16), ((2, width), f32)]
    pull_scratch = [((long, 2 * width), f32), ((rows, width), bf16)]
    wide_0, low_0, grad_0, norm_0 = call(
        pull_first_kernel,
        (back, residual_0, seed, wc, norm_params, qkv_0, probs_0),
        pulled,
        pull_scratch,
        flops=8e9,
        smem=0,
    )
    (keep_e, keep_r), (send_e, send_r) = halved(place, [(two_a, NEAR), (two_b, ROW)], waits=(grad_0,))
    two_a, two_b = [keep_e, swap(send_e, *NEAR)], [keep_r, swap(send_r, *ROW)]
    wide_1, low_1, grad_1, norm_1, keep_a, keep_b, send_a, send_b = call(
        functools.partial(pull_last_kernel, n_dp),
        (
            place, back, residual_1, seed, wc, norm_params, qkv_1, probs_1,
            first_0, first_1, mixed_0, mixed_1, grad_0, low_0,
        ),
        pulled + [((4 * width, cols), bf16)] * 4,
        pull_scratch,
        waits=(send_e,),
        flops=10e9,
    )
    one_a, one_b = [keep_a, swap(send_a, *CORE)], [keep_b, swap(send_b, *CORE)]
    first, *others = far()
    (keep_e, keep_r), (sent,) = halved(
        place, [(two_a, first), (two_b, first)], joint=2, waits=(keep_a,)
    )
    (keep_a, keep_b), (send_a, send_b) = halved(place, [(one_a, NEAR), (one_b, ROW)], waits=(sent,))
    gots = swap(send_a, *NEAR), swap(send_b, *ROW)
    two_got = swap(sent, *first)
    grad_in_0, grad_in_1, norm = call(
        finish_kernel,
        (norm_params, wp, grad_0, frames_x[0], wide_0, grad_1, frames_x[1], wide_1, norm_0, norm_1),
        [((own, width), f32), ((own, width), f32), ((4 * parts, cols), f32)],
        waits=(send_a,),
        flops=3e9,
        smem=0,
    )
    norm = norm + swap(norm, *CORE)
    norms = (norm, swap(norm, *ROW))
    (keep_a, keep_b), norm, (send_a, send_b) = halved_norm(
        place, (keep_a, keep_b), gots, (ROW, NEAR), norms, False
    )
    gots = swap(send_a, *ROW), swap(send_b, *NEAR)
    (keep_e, keep_r), (send_e, send_r) = halved_joint(
        place, (keep_e, keep_r), two_got, (ROW, NEAR), joint=False, waits=(send_a,)
    )
    two_a, two_b = [keep_e, swap(send_e, *ROW)], [keep_r, swap(send_r, *NEAR)]
    pending = (send_e,)
    second, *others = others
    (keep_e, keep_r), (sent,) = halved(place, [(two_a, second), (two_b, second)], joint=2)
    two_got = swap(sent, *second)
    for label in others:
        (keep_e, keep_r), (sent,) = halved_joint(place, (keep_e, keep_r), two_got, (label, label))
        two_got = swap(sent, *label)
    for label in far():
        (keep_a, keep_b), norm, (sent,) = halved_norm(
            place, (keep_a, keep_b), gots, (label, label), (norm,), True, waits=pending
        )
        gots, pending = (swap(sent, *label),), ()

    plain = lambda x: [(x.shape, f32)] * 4
    weighed = lambda x: plain(x) + [(x.shape, bf16)]
    updated = call(
        update_feed_kernel,
        (
            keep_e, keep_r, two_got, weight_expand, moment_expand, average_expand,
            weight_reduce, moment_reduce, average_reduce,
        ),
        weighed(weight_expand) + weighed(weight_reduce),
        flops=1e8,
        smem=0,
        mib=8,
    )
    gradient_expand, mom_expand, avg_expand, new_expand, low_expand = updated[:5]
    gradient_reduce, mom_reduce, avg_reduce, new_reduce, low_reduce = updated[5:]
    updated = call(
        update_rest_kernel,
        (
            keep_a, keep_b, gots[0], norm, weight_project, moment_project, average_project,
            weight_combine, moment_combine, average_combine, norm_params, norm_moment, norm_average,
        ),
        weighed(weight_project) + weighed(weight_combine) + plain(norm_params),
        flops=1e8,
        smem=0,
        mib=8,
    )
    gradient_project, mom_project, avg_project, new_project, low_project = updated[:5]
    gradient_combine, mom_combine, avg_combine, new_combine, low_combine = updated[5:10]
    norm_gradient, mom_norms, avg_norms, new_norms = updated[10:]
    layer_out = jnp.transpose(layer, (1, 0, 2))
    input_gradient = jnp.transpose(jnp.stack([grad_in_0, grad_in_1]), (1, 0, 2))
    return (
        layer_out,
        input_gradient,
        gradient_project,
        gradient_combine,
        gradient_expand,
        gradient_reduce,
        mom_project,
        mom_combine,
        mom_expand,
        mom_reduce,
        avg_project,
        avg_combine,
        avg_expand,
        avg_reduce,
        new_project,
        new_combine,
        new_expand,
        new_reduce,
        low_project,
        low_combine,
        low_expand,
        low_reduce,
        norm_gradient,
        mom_norms,
        avg_norms,
        new_norms,
    )


def solution(mesh):
    tokens = P("mp", "dp", None)
    stacked, matrix = P(None, "dp", "mp"), P("dp", "mp")
    weights = (stacked, matrix, matrix, matrix)
    in_specs = (tokens, tokens, P("dp")) + weights * 3 + (P(),) * 3
    out_specs = (tokens, tokens) + weights * 5 + (P(),) * 4
    return jax.shard_map(
        on_device, mesh=mesh, in_specs=in_specs, out_specs=out_specs, check_vma=False
    )
```

```python
import functools
import math

import jax
import jax.numpy as jnp
from jax import lax
from jax.experimental import pallas as pl
from jax.experimental.pallas import tpu as pltpu
from jax.sharding import PartitionSpec as P

HEADS = 8
HEAD_DIM = 64
WINDOW = 10
HALO = 16

eps_norm = 1e-05
momentum_decay = 0.9
average_decay = 0.6
matrix_rate = 0.0001
norm_rate = 0.001
masked_score = -1e30

GROUP = 4
LANES = GROUP * HEAD_DIM
QUERIES = 112
KEYS = QUERIES + HALO

f32 = jnp.float32
bf16 = jnp.bfloat16


def mm(a, b):
    return lax.dot_general(a, b, (((1,), (0,)), ((), ())), preferred_element_type=f32)


def mm_bt(a, b):
    return lax.dot_general(a, b, (((1,), (1,)), ((), ())), preferred_element_type=f32)


def mm_at(a, b):
    return lax.dot_general(a, b, (((0,), (0,)), ((), ())), preferred_element_type=f32)


def normalise(values):
    center = values - jnp.mean(values, axis=-1, keepdims=True)
    spread = jnp.mean(center * center, axis=-1, keepdims=True)
    inverse = lax.rsqrt(spread + eps_norm)
    return center * inverse, inverse


def norm_backward(values, gain, upstream):
    scaled, inverse = normalise(values)
    weighted = upstream * gain
    inner = (
        weighted
        - jnp.mean(weighted, axis=-1, keepdims=True)
        - scaled * jnp.mean(weighted * scaled, axis=-1, keepdims=True)
    )
    return inner * inverse, upstream * scaled


def query_blocks(total):
    blocks = []
    at = HALO
    while at < total:
        rows = min(QUERIES, total - at)
        blocks.append((at, rows, min(at - HALO, total - KEYS)))
        at += rows
    return blocks


def band(block, start, length):
    q0, rows, k0 = block
    query = lax.broadcasted_iota(jnp.int32, (rows, KEYS), 0)
    key = lax.broadcasted_iota(jnp.int32, (rows, KEYS), 1)
    behind = query - key + (q0 - k0)
    time = key + (start + k0 - HALO)
    inside = (time < length) | (behind == 0)
    return (behind >= 0) & (behind <= WINDOW) & (time >= 0) & inside


def head_lanes():
    lane = lax.broadcasted_iota(jnp.int32, (1, LANES), 1)
    return [(lane >= h * HEAD_DIM) & (lane < (h + 1) * HEAD_DIM) for h in range(GROUP)]


def stack_heads(block):
    zero = jnp.zeros_like(block)
    return jnp.concatenate([jnp.where(m, block, zero) for m in head_lanes()], axis=0)


def merge_heads(stacked, rows):
    masks = head_lanes()
    out = jnp.where(masks[0], stacked[:rows], 0.0)
    for h in range(1, GROUP):
        out = jnp.where(masks[h], stacked[h * rows : (h + 1) * rows], out)
    return out


def softmax_rows(scores, allowed):
    scores = jnp.where(allowed, scores * (1.0 / math.sqrt(HEAD_DIM)), masked_score)
    raised = jnp.exp(scores - jnp.max(scores, axis=-1, keepdims=True))
    return raised / jnp.sum(raised, axis=-1, keepdims=True)


def block_order(n_dp, near_first, split=False):
    row, near, far_bits = -1, 0, list(range(1, (n_dp - 1).bit_length()))
    first, second = (near, row) if near_first else (row, near)
    bits = [first, far_bits[0], second, *far_bits[1:]] if split else [first, second, *far_bits]
    blocks = []
    for at in range(2 * n_dp):
        value = {bit: (at >> (len(bits) - 1 - i)) & 1 for i, bit in enumerate(bits)}
        blocks.append((value[row], sum(value[bit] << bit for bit in bits if bit != row)))
    return blocks


def place_weights(n_dp, core, own_a, own_b, got_a, got_b, wp_ref, wc_ref):
    width, cols = wc_ref.shape[0], own_a.shape[1]
    r = width // n_dp
    for which, ref_a, ref_b in ((core, own_a, own_b), (1 - core, got_a, got_b)):
        for ref, first, near_first in ((ref_a, 0, True), (ref_b, 2, False)):
            for p, (y, d) in enumerate(block_order(n_dp, near_first)):
                at = pl.multiple_of((2 * y + which) * cols, cols)
                for i in range(2):
                    block = ref[(2 * p + i) * r : (2 * p + i + 1) * r]
                    if first + i < 3:
                        wp_ref[d * r : (d + 1) * r, pl.ds((first + i) * width + at, cols)] = block
                    else:
                        wc_ref[d * r : (d + 1) * r, pl.ds(at, cols)] = block


def edge_kernel(place_ref, frames_ref, cotangent_ref, near_ref, over_ref):
    last = frames_ref.shape[1] - HALO
    for core, early, late in ((0, over_ref, near_ref), (1, near_ref, over_ref)):

        @pl.when(place_ref[1] == core)
        def _():
            early[0] = frames_ref[:, :HALO]
            early[1] = cotangent_ref[:, :HALO]
            late[0] = frames_ref[:, last:]
            late[1] = frames_ref[:, last:]


def frames_kernel(place_ref, frames_ref, near_ref, over_ref, *outs):
    own = frames_ref.shape[1]
    for u, out in enumerate(outs):
        out[HALO : HALO + own] = frames_ref[u]
    for core, left, right in ((0, over_ref, near_ref), (1, near_ref, over_ref)):

        @pl.when(place_ref[1] == core)
        def _():
            for u, out in enumerate(outs):
                out[:HALO] = left[0, u]
                out[HALO + own :] = right[0, u]


def seed_kernel(place_ref, cotangent_ref, near_ref, over_ref, seed_ref, seed_t_ref):
    own = cotangent_ref.shape[1]
    for u in range(seed_ref.shape[0]):

        def valid(first, count):
            time = lax.broadcasted_iota(jnp.int32, (count, 1), 0) + (place_ref[0] + first)
            return time < place_ref[2 + u]

        mine = cotangent_ref[u]
        mine = jnp.where(valid(0, own), mine, jnp.zeros_like(mine))
        seed_ref[u, :own] = mine
        seed_t_ref[:, u * own : (u + 1) * own] = mine.T
        theirs = jnp.where(place_ref[1] == 0, near_ref[1, u], over_ref[1, u])
        seed_ref[u, own:] = jnp.where(valid(own, HALO), theirs, jnp.zeros_like(theirs))


def attend_one(
    u, place_ref, frames_ref, norms_ref, wp_ref, wc_ref,
    qkv_ref, probs_ref, first_ref, mixed_ref, residual_ref, second_ref, second_t_ref,
):
    total, width = frames_ref.shape
    own = first_ref.shape[0]
    start, length = place_ref[0], place_ref[2 + u]
    scaled, _ = normalise(frames_ref[...].astype(f32))
    normed = (scaled * norms_ref[0:1] + norms_ref[1:2]).astype(bf16)
    first_ref[...] = normed[HALO : HALO + own]
    qkv_ref[...] = mm(normed, wp_ref[...]).astype(bf16)
    def group(hg, carry):
        at = pl.multiple_of(hg * LANES, LANES)
        here = pl.ds(pl.multiple_of(hg * KEYS, KEYS), KEYS)
        for b, block in enumerate(query_blocks(total)):
            q0, rows, k0 = block
            allowed = band(block, start, length)
            queries = stack_heads(qkv_ref[q0 : q0 + rows, pl.ds(at, LANES)])
            keys = qkv_ref[k0 : k0 + KEYS, pl.ds(width + at, LANES)]
            values = qkv_ref[k0 : k0 + KEYS, pl.ds(2 * width + at, LANES)]
            scores = mm_bt(queries, keys)
            low_probs = []
            for h in range(GROUP):
                probs = softmax_rows(scores[h * rows : (h + 1) * rows], allowed)
                probs_ref[b, h, :rows, here] = probs
                low_probs.append(probs.astype(bf16))
            out = merge_heads(mm(jnp.concatenate(low_probs, axis=0), values), rows)
            mixed_ref[q0 - HALO : q0 - HALO + rows, pl.ds(at, LANES)] = out.astype(bf16)
        return carry

    lax.fori_loop(0, width // LANES, group, 0)
    residual = frames_ref[HALO:total].astype(f32) + mm_bt(mixed_ref[...], wc_ref[...])
    residual_ref[...] = residual
    scaled, _ = normalise(residual)
    second_ref[...] = (scaled * norms_ref[2:3] + norms_ref[3:4]).astype(bf16)
    second_t_ref[...] = second_ref[:own].T


def attend_first_kernel(
    n_dp, place_ref, frames_ref, norms_ref, own_a, own_b, got_a, got_b, *refs
):
    *outs, wp_ref, wc_ref = refs
    place_weights(n_dp, place_ref[1], own_a, own_b, got_a, got_b, wp_ref, wc_ref)
    attend_one(0, place_ref, frames_ref, norms_ref, wp_ref, wc_ref, *outs)


def attend_next_kernel(place_ref, frames_ref, norms_ref, wp_ref, wc_ref, *refs):
    attend_one(1, place_ref, frames_ref, norms_ref, wp_ref, wc_ref, *refs)


def gelu_parts(value):
    slope = math.sqrt(2.0 / math.pi)
    square = value * value
    tanh = jnp.tanh(value * (slope + (slope * 0.044715) * square))
    half = 0.5 + 0.5 * tanh
    curve = half + (0.5 * value) * (1.0 - tanh * tanh) * (
        slope + (slope * 3.0 * 0.044715) * square
    )
    return value * half, curve


def feed_half(
    n_dp, seconds, seconds_t, seed_ref, seed_t_ref, we_ref, wr_ref, ge_ref, gr_ref,
    wide_e, wide_r, active_ref, grad_ref, add_fed, add_back,
):
    own = seconds_t[0].shape[1]
    width, hidden = wide_e.shape[0], we_ref.shape[1]
    r = width // n_dp
    for ref, wide, near_first in ((we_ref, wide_e, True), (wr_ref, wide_r, False)):
        for p, (y, d) in enumerate(block_order(n_dp, near_first)):
            wide[d * r : (d + 1) * r, y * hidden : (y + 1) * hidden] = ref[p * r : (p + 1) * r]
    for u, second_ref in enumerate(seconds):
        rows = slice(u * own, (u + 1) * own)
        active, curve = gelu_parts(mm(second_ref[...], wide_e[...]))
        active_ref[rows] = active[:own].astype(bf16)
        grad_ref[u] = (mm(seed_ref[u], wide_r[...]) * curve).astype(bf16)
        add_fed(u, mm_bt(active_ref[rows], wide_r[...]))
        add_back(u, mm_bt(grad_ref[u], wide_e[...]))
    total_r = mm(seed_t_ref[...], active_ref[...])
    total_e = mm(seconds_t[0][...], grad_ref[0, :own]) + mm(seconds_t[1][...], grad_ref[1, :own])
    for total, ref, near_first in ((total_e, ge_ref, True), (total_r, gr_ref, False)):
        for p, (y, d) in enumerate(block_order(n_dp, near_first, True)):
            block = total[d * r : (d + 1) * r, y * hidden : (y + 1) * hidden]
            ref[p * r : (p + 1) * r] = block.astype(bf16)


def feed_first_kernel(n_dp, we_ref, wr_ref, n0, seed_ref, n1, seed_t_ref, t0, t1, *refs):
    fed_ref, back_ref, ge_ref, gr_ref, *scratch = refs

    def add_fed(u, value):
        fed_ref[u] = value

    def add_back(u, value):
        back_ref[u] = value

    feed_half(
        n_dp, (n0, n1), (t0, t1), seed_ref, seed_t_ref, we_ref, wr_ref, ge_ref, gr_ref,
        *scratch, add_fed, add_back,
    )


def feed_last_kernel(
    n_dp, we_ref, wr_ref, n0, seed_ref, fed_in, back_in, n1, r0, r1, seed_t_ref, t0, t1, *refs
):
    out_ref, back_ref, ge_ref, gr_ref, *scratch = refs
    own = out_ref.shape[1]

    def add_fed(u, value):
        out_ref[u] = ((r0, r1)[u][:own] + (fed_in[u] + value)).astype(bf16)

    def add_back(u, value):
        back_ref[u] = back_in[u] + value

    feed_half(
        n_dp, (n0, n1), (t0, t1), seed_ref, seed_t_ref, we_ref, wr_ref, ge_ref, gr_ref,
        *scratch, add_fed, add_back,
    )


def pull_one(
    u, back_ref, residual_ref, seed_ref, wc_ref, norms_ref, qkv_ref, probs_ref,
    wide_ref, low_ref, grad_ref, norm_ref, grad_kv_ref, mixed_g_ref,
):
    total = qkv_ref.shape[0]
    own, width = low_ref.shape
    upstream = back_ref[u]
    back, gained = norm_backward(residual_ref[...], norms_ref[2:3], upstream)
    norm_ref[0:1] = jnp.sum(gained[:own], axis=0, keepdims=True)
    norm_ref[1:2] = jnp.sum(upstream[:own], axis=0, keepdims=True)
    wide = seed_ref[u].astype(f32) + back
    wide_ref[...] = wide[:own]
    low = wide.astype(bf16)
    low_ref[...] = low[:own]
    mixed_g_ref[...] = mm(low, wc_ref[...]).astype(bf16)
    grad_kv_ref[...] = jnp.zeros_like(grad_kv_ref)
    scale = 1.0 / math.sqrt(HEAD_DIM)
    def group(hg, carry):
        at = pl.multiple_of(hg * LANES, LANES)
        here = pl.ds(pl.multiple_of(hg * KEYS, KEYS), KEYS)
        first_lanes, second_lanes = pl.ds(at, LANES), pl.ds(width + at, LANES)
        for b, block in enumerate(query_blocks(total)):
            q0, rows, k0 = block
            queries = stack_heads(qkv_ref[q0 : q0 + rows, first_lanes])
            keys = qkv_ref[k0 : k0 + KEYS, second_lanes]
            values = qkv_ref[k0 : k0 + KEYS, pl.ds(2 * width + at, LANES)]
            upper = stack_heads(mixed_g_ref[q0 - HALO : q0 - HALO + rows, first_lanes])
            grad_probs = mm_bt(upper, values)
            low_probs, grad_scores = [], []
            for h in range(GROUP):
                probs = probs_ref[b, h, :rows, here]
                grad = grad_probs[h * rows : (h + 1) * rows]
                inner = jnp.sum(probs * grad, axis=-1, keepdims=True)
                low_probs.append(probs.astype(bf16))
                grad_scores.append((probs * (grad - inner)).astype(bf16))
            low_probs = jnp.concatenate(low_probs, axis=0)
            grad_scores = jnp.concatenate(grad_scores, axis=0)
            grad_q = merge_heads(mm(grad_scores, keys), rows) * scale
            mine = min(rows, HALO + own - q0)
            if mine > 0:
                grad_ref[q0 - HALO : q0 - HALO + mine, first_lanes] = grad_q[:mine].astype(bf16)
            grad_kv_ref[k0 : k0 + KEYS, first_lanes] += mm_at(grad_scores, queries) * scale
            grad_kv_ref[k0 : k0 + KEYS, second_lanes] += mm_at(low_probs, upper)
        return carry

    lax.fori_loop(0, width // LANES, group, 0)
    grad_ref[:, width:] = grad_kv_ref[HALO : HALO + own].astype(bf16)


def pull_first_kernel(*refs):
    pull_one(0, *refs)


def pull_last_kernel(
    n_dp, place_ref, back_ref, residual_ref, seed_ref, wc_ref, norms_ref, qkv_ref, probs_ref,
    first_0, first_1, mixed_0, mixed_1, grad_0, low_0, *refs,
):
    wide_ref, low_ref, grad_ref, norm_ref, keep_a, keep_b, send_a, send_b, grad_kv_ref, mixed_g_ref = refs
    pull_one(
        1, back_ref, residual_ref, seed_ref, wc_ref, norms_ref, qkv_ref, probs_ref,
        wide_ref, low_ref, grad_ref, norm_ref, grad_kv_ref, mixed_g_ref,
    )
    own, width = low_ref.shape
    core, cols, r = place_ref[1], keep_a.shape[1], width // n_dp
    firsts = first_0[...].T, first_1[...].T
    lows = low_0[...].T, low_ref[...].T
    where = {
        near_first: {block: p for p, block in enumerate(block_order(n_dp, near_first))}
        for near_first in (True, False)
    }
    for i in range(4):
        keep, send, at = (keep_a, send_a, where[True]) if i < 2 else (keep_b, send_b, where[False])
        for y in range(2):
            lanes = slice(2 * y * cols, 2 * (y + 1) * cols)
            if i < 3:
                inner = slice(i * width + lanes.start, i * width + lanes.stop)
                value = mm(firsts[0], grad_0[:, inner]) + mm(firsts[1], grad_ref[:, inner])
            else:
                value = mm(lows[0], mixed_0[:own, lanes]) + mm(lows[1], mixed_1[:own, lanes])
            mine = jnp.where(core == 0, value[:, :cols], value[:, cols:])
            other = jnp.where(core == 0, value[:, cols:], value[:, :cols])
            for d in range(n_dp):
                to = (2 * at[y, d] + i % 2) * r
                keep[to : to + r] = mine[d * r : (d + 1) * r].astype(bf16)
                send[to : to + r] = other[d * r : (d + 1) * r].astype(bf16)


def fold_norm(ref, first, value):
    cols = ref.shape[1]
    for j in range(value.shape[1] // cols):
        ref[4 * j + first : 4 * j + first + value.shape[0]] = value[:, j * cols : (j + 1) * cols]


def finish_kernel(norms_ref, wp_ref, grad_0, frames_0, wide_0, grad_1, frames_1, wide_1, norm_0, norm_1, out_0, out_1, norm_ref):
    own, width = out_0.shape
    step = own // 2
    gain, shift = jnp.zeros((1, width), f32), jnp.zeros((1, width), f32)
    for grad_ref, frames_ref, wide_ref, out_ref in (
        (grad_0, frames_0, wide_0, out_0),
        (grad_1, frames_1, wide_1, out_1),
    ):

        def one(i, carry):
            at = pl.ds(pl.multiple_of(i * step, step), step)
            frames = frames_ref[pl.ds(pl.multiple_of(HALO + i * step, HALO), step)]
            upstream = mm_bt(grad_ref[at], wp_ref[...])
            back, gained = norm_backward(frames.astype(f32), norms_ref[0:1], upstream)
            out_ref[at] = wide_ref[at] + back
            gain, shift = carry
            return (
                gain + jnp.sum(gained, axis=0, keepdims=True),
                shift + jnp.sum(upstream, axis=0, keepdims=True),
            )

        gain, shift = lax.fori_loop(0, own // step, one, (gain, shift))
    fold_norm(norm_ref, 0, gain)
    fold_norm(norm_ref, 1, shift)
    fold_norm(norm_ref, 2, norm_0[...] + norm_1[...])


VM = pl.BlockSpec(memory_space=pltpu.VMEM)
SM = pl.BlockSpec(memory_space=pltpu.SMEM)
MIB = 1024 * 1024


def call(kernel, ins, outs, scratch=(), waits=(), flops=1e9, smem=1, mib=16):
    n, m = len(ins), len(outs)
    away = pl.BlockSpec(memory_space=pl.ANY)

    def body(*refs):
        kernel(*refs[:n], *refs[n + len(waits) :])

    return pl.pallas_call(
        body,
        out_shape=tuple(jax.ShapeDtypeStruct(shape, kind) for shape, kind in outs),
        in_specs=[SM] * smem + [VM] * (n - smem) + [away] * len(waits),
        out_specs=(VM,) * m,
        scratch_shapes=[pltpu.VMEM(shape, kind) for shape, kind in scratch],
        compiler_params=pltpu.CompilerParams(vmem_limit_bytes=mib * MIB),
        cost_estimate=pl.CostEstimate(flops=int(flops), bytes_accessed=6000000, transcendentals=0),
    )(*ins, *waits)


def swap(value, axis, bit):
    n = lax.axis_size(axis)
    return lax.ppermute(value, axis, [(i, i ^ (1 << bit)) for i in range(n)])


CORE, ROW, NEAR = ("mp", 0), ("mp", 1), ("dp", 0)


def far():
    return [("dp", b) for b in range(1, (lax.axis_size("dp") - 1).bit_length())]


def side(label):
    return (lax.axis_index(label[0]) >> label[1]) & 1


def by_rows(rows, body):
    step = 128
    if rows <= step or rows % step:
        body(slice(None))
        return

    def one(i, carry):
        body(pl.ds(pl.multiple_of(i * step, step), step))
        return carry

    lax.fori_loop(0, rows // step, one, 0)


def spot(label):
    return {CORE: 1, ROW: 4, NEAR: 5}.get(label, 5 + label[1])


def paired(place, streams, waits=()):
    def kernel(place_ref, *refs):
        outs = list(refs[2 * len(streams) :])
        for i, (_, _, label, parts) in enumerate(streams):
            mine, got = refs[2 * i], refs[2 * i + 1]
            high = place_ref[spot(label)]
            for part in range(parts):
                out = outs.pop(0)

                def body(at):
                    out[high, :, at] = mine[:, part, at]
                    out[1 - high, :, at] = got[:, part, at]

                by_rows(out.shape[2], body)

    ins, outs = [place], []
    for mine, got, label, parts in streams:
        blocks = lax.axis_size("dp") // 4 if parts > 1 else 1
        shape = (blocks, parts, mine.shape[0] // blocks // parts, mine.shape[1])
        ins += [mine.reshape(shape), got.reshape(shape)]
        outs += [((2, blocks, *shape[2:]), mine.dtype)] * parts
    return [x.reshape(-1, x.shape[-1]) for x in call(kernel, ins, outs, waits=waits, flops=1e8, mib=8)]


def lowered(arrays, waits):
    rows = [x.shape[0] for x in arrays]

    def kernel(*refs):
        at = 0
        for ref, count in zip(refs, rows):
            refs[-1][at : at + count] = ref[...].astype(bf16)
            at += count

    return call(kernel, arrays, [((sum(rows), arrays[0].shape[1]), bf16)], waits=waits, flops=1e8, smem=0, mib=8)[0]


def halved(place, streams, joint=0, waits=()):
    counts = [len(terms) for terms, _ in streams]
    n = len(streams)

    def kernel(place_ref, *refs):
        refs = list(refs)
        groups = [[refs.pop(0) for _ in range(count)] for count in counts]
        kept, sent = refs[:n], refs[n:]
        for i, (group, (_, label)) in enumerate(zip(groups, streams)):
            mine = place_ref[spot(label)]

            def body(at):
                kept[i][at] = total([ref[mine, at] for ref in group])
                gone = total([ref[1 - mine, at] for ref in group]).astype(bf16)
                if i < joint:
                    sent[0][i, at] = gone
                else:
                    sent[i - max(0, joint - 1)][at] = gone

            by_rows(kept[i].shape[0], body)

    ins, keeps, sends = [place], [], []
    for terms, _ in streams:
        half, cols = terms[0].size // terms[0].shape[-1] // 2, terms[0].shape[-1]
        ins += [term.reshape(2, half, cols) for term in terms]
        keeps.append(((half, cols), f32))
        sends.append(((half, cols), bf16))
    if joint:
        sends = [((joint, *sends[0][0]), bf16), *sends[joint:]]
    done = call(kernel, ins, keeps + sends, waits=waits, flops=1e8, mib=8)
    return done[:n], done[n:]


def halved_joint(place, keeps, got, labels, joint=True, waits=()):
    n = len(keeps)
    half, cols = keeps[0].shape[0] // 2, keeps[0].shape[1]

    def kernel(place_ref, *refs):
        for i in range(n):
            mine = place_ref[spot(labels[i])]

            def body(at):
                kept = refs[i][mine, at] + refs[n][i, mine, at].astype(f32)
                gone = refs[i][1 - mine, at] + refs[n][i, 1 - mine, at].astype(f32)
                refs[n + 1 + i][at] = kept
                if joint:
                    refs[2 * n + 1][i, at] = gone.astype(bf16)
                else:
                    refs[2 * n + 1 + i][at] = gone.astype(bf16)

            by_rows(half, body)

    ins = [place, *[keep.reshape(2, half, cols) for keep in keeps], got.reshape(n, 2, half, cols)]
    sends = [((n, half, cols), bf16)] if joint else [((half, cols), bf16)] * n
    done = call(kernel, ins, [((half, cols), f32)] * n + sends, waits=waits, flops=1e8, mib=8)
    return done[:n], done[n:]


def halved_norm(place, keeps, gots, labels, norms, joint, waits=()):
    rows, cols = keeps[0].shape
    half, extra = rows // 2, norms[0].shape[0]
    n = len(gots)

    def kernel(place_ref, *refs):
        keep, got, norm, outs = refs[:2], refs[2 : 2 + n], refs[2 + n : -5 if not joint else -4], refs[-5 if not joint else -4 :]
        arrived = [(got[0], 0), (got[-1], 0 if n == 2 else rows)]
        for i in range(2):
            mine = place_ref[spot(labels[i])]
            ref, at = arrived[i]
            here = keep[i][pl.ds(pl.multiple_of(mine * half, half), half)].astype(f32)
            there = keep[i][pl.ds(pl.multiple_of((1 - mine) * half, half), half)].astype(f32)
            here += ref[pl.ds(pl.multiple_of(at + mine * half, half), half)].astype(f32)
            there += ref[pl.ds(pl.multiple_of(at + (1 - mine) * half, half), half)].astype(f32)
            outs[i][...] = here
            if joint:
                outs[3][i * half : (i + 1) * half] = there.astype(bf16)
            else:
                outs[3 + i][:half] = there.astype(bf16)
        if len(norm) == 2:
            value = norm[0][...] + norm[1][...]
        else:
            ref, at = arrived[1]
            value = joined_norm(norm[0][...], ref[at + rows : at + rows + 2 * extra])
        outs[2][...] = value
        split_norm(value, outs[-1], 2 * half if joint else half)

    small = [((half, cols), f32)] * 2 + [((extra, cols), f32)]
    if joint:
        sends = [((2 * half + 2 * extra, cols), bf16)]
    else:
        sends = [((half, cols), bf16), ((half + 2 * extra, cols), bf16)]
    done = call(kernel, (place, *keeps, *gots, *norms), small + sends, waits=waits, flops=1e8, mib=8)
    return done[:2], done[2], done[3:]


def split_norm(value, ref, at):
    rows = value.shape[0]
    high = value.astype(bf16)
    ref[at : at + rows] = high
    ref[at + rows : at + 2 * rows] = (value - high.astype(f32)).astype(bf16)


def joined_norm(value, got):
    rows = value.shape[0]
    high = value.astype(bf16).astype(f32)
    low = (value - high).astype(bf16).astype(f32)
    return (high + low) + (got[:rows].astype(f32) + got[rows:].astype(f32))


def total(terms):
    terms = [term.astype(f32) for term in terms]
    return functools.reduce(jnp.add, terms)


def write_update(outs, at, gradient, states, rate):
    values = advance(*states[:1], gradient, *states[1:], rate)
    for out, value in zip(outs, (gradient, *values)):
        out[at] = value
    if len(outs) > 4:
        outs[4][at] = values[2].astype(bf16)


def update_feed_kernel(keep_e, keep_r, got_ref, *refs):
    states, outs = refs[:6], refs[6:]
    for i, keep in enumerate((keep_e, keep_r)):
        gradient = keep[...] + got_ref[i].astype(f32)
        state = [ref[...] for ref in states[3 * i : 3 * i + 3]]
        write_update(outs[5 * i : 5 * i + 5], slice(None), gradient, state, matrix_rate)


def update_rest_kernel(keep_a, keep_b, got_ref, norm_ref, *refs):
    states, outs = refs[:9], refs[9:]
    rows, cols = keep_a.shape
    r, extra = rows // 2, norm_ref.shape[0]
    for i in range(4):
        keep = (keep_a, keep_b)[i // 2]
        at = (i % 2) * r
        gradient = keep[at : at + r] + got_ref[i * r : (i + 1) * r].astype(f32)
        which, entry = (0, i) if i < 3 else (1, slice(None))
        state = [ref[entry] for ref in states[3 * which : 3 * which + 3]]
        write_update(outs[5 * which : 5 * which + 5], entry, gradient, state, matrix_rate)
    value = joined_norm(norm_ref[...], got_ref[2 * rows : 2 * rows + 2 * extra])
    for j in range(extra // 4):
        at = (slice(None), slice(j * cols, (j + 1) * cols))
        state = [ref[at] for ref in states[6:]]
        write_update(outs[10:], at, value[4 * j : 4 * j + 4], state, norm_rate)


def advance(weight, gradient, moment, average, rate):
    momentum = momentum_decay * moment + gradient
    updated = weight - rate * (gradient + momentum_decay * momentum)
    smoothed = average_decay * average + (1.0 - average_decay) * updated
    return (momentum, smoothed, updated)


def on_device(
    frames,
    cotangent,
    lengths,
    weight_project,
    weight_combine,
    weight_expand,
    weight_reduce,
    moment_project,
    moment_combine,
    moment_expand,
    moment_reduce,
    average_project,
    average_combine,
    average_expand,
    average_reduce,
    norm_params,
    norm_moment,
    norm_average,
):
    own, batch, width = frames.shape
    long, rows = own + 2 * HALO, own + HALO
    parts, n_dp = lax.axis_size("mp"), lax.axis_size("dp")
    me = lax.axis_index("mp")
    start = me * own
    cols, hidden = width // parts, weight_expand.shape[1]
    r = width // n_dp

    sides = [side(label) for label in (ROW, NEAR, *far())]
    place = jnp.concatenate(
        [jnp.stack([start, side(CORE)]).astype(jnp.int32), lengths, jnp.stack(sides).astype(jnp.int32)]
    )
    *outer, last = reversed(far())

    matrices = jnp.concatenate([weight_project, weight_combine[None]], axis=0).astype(bf16)
    one = matrices.reshape(-1, cols)
    for label in outer:
        (one,) = paired(place, [(one, swap(one, *label), label, 1)])
    one_got = swap(one, *last)

    two = lowered([weight_expand, weight_reduce], waits=(one,))
    one_a, one_b = paired(place, [(one, one_got, last, 2)])
    frames_u = jnp.transpose(frames, (1, 0, 2))
    cotangent_u = jnp.transpose(cotangent, (1, 0, 2))
    strip = ((2, batch, HALO, width), bf16)
    near, over = call(
        edge_kernel,
        (place, frames_u, cotangent_u),
        [strip] * 2,
        waits=(one_got,),
        flops=1e8,
        mib=8,
    )
    near = swap(near, *CORE)
    pairs = [(i, i + 1) for i in range(1, parts - 1, 2)]
    over = lax.ppermute(over, "mp", pairs + [(b, a) for a, b in pairs])
    frames_x = call(
        frames_kernel, (place, frames_u, near, over), [((long, width), bf16)] * 2, flops=1e8, mib=8
    )
    got_a, got_b = swap(one_a, *ROW), swap(one_b, *NEAR)
    for label in outer:
        (two,) = paired(place, [(two, swap(two, *label), label, 1)])
    one_a, one_b = paired(
        place, [(one_a, got_a, ROW, 1), (one_b, got_b, NEAR, 1)], waits=(two,)
    )
    got_a, got_b = swap(one_a, *NEAR), swap(one_b, *ROW)
    two_a, two_b = paired(place, [(two, swap(two, *last), last, 2)])
    one_a, one_b = paired(
        place, [(one_a, got_a, NEAR, 1), (one_b, got_b, ROW, 1)], waits=(two_a, *frames_x)
    )
    core_a, core_b = swap(one_a, *CORE), swap(one_b, *CORE)

    per_u = [
        ((long, 3 * width), bf16),
        ((-(-rows // QUERIES), GROUP, QUERIES, width // LANES * KEYS), f32),
        ((own, width), bf16),
        ((rows, width), bf16),
        ((rows, width), f32),
        ((rows, width), bf16),
        ((width, own), bf16),
    ]
    qkv_0, probs_0, first_0, mixed_0, residual_0, second_0, second_t_0, wp, wc = call(
        functools.partial(attend_first_kernel, n_dp),
        (place, frames_x[0], norm_params, one_a, one_b, core_a, core_b),
        per_u + [((width, 3 * width), bf16), ((width, width), bf16)],
        flops=5e9,
    )
    seed, seed_t = call(
        seed_kernel,
        (place, cotangent_u, near, over),
        [((batch, rows, width), bf16), ((width, batch * own), bf16)],
        waits=(second_0,),
        flops=1e8,
        mib=8,
    )

    got_a, got_b = swap(two_a, *ROW), swap(two_b, *NEAR)
    two_a, two_b = paired(place, [(two_a, got_a, ROW, 1), (two_b, got_b, NEAR, 1)], waits=(seed,))
    qkv_1, probs_1, first_1, mixed_1, residual_1, second_1, second_t_1 = call(
        attend_next_kernel,
        (place, frames_x[1], norm_params, wp, wc),
        per_u,
        flops=5e9,
    )
    got_a, got_b = swap(two_a, *NEAR), swap(two_b, *ROW)
    expand, reduce_w = paired(
        place, [(two_a, got_a, NEAR, 1), (two_b, got_b, ROW, 1)], waits=(second_1,)
    )
    expand_got, reduce_got = swap(expand, *CORE), swap(reduce_w, *CORE)

    grads = [((2 * width, hidden), bf16)] * 2
    carried = [((batch, own, width), f32), ((batch, rows, width), f32)]
    feed_scratch = [((width, 2 * hidden), bf16)] * 2 + [
        ((batch * own, 2 * hidden), bf16),
        ((batch, rows, 2 * hidden), bf16),
    ]
    transposed = (seed_t, second_t_0, second_t_1)
    fed, back, keep_e, keep_r = call(
        functools.partial(feed_first_kernel, n_dp),
        (expand, reduce_w, second_0, seed, second_1, *transposed),
        carried + grads,
        feed_scratch,
        flops=8e9,
        smem=0,
    )
    layer, back, send_e, send_r = call(
        functools.partial(feed_last_kernel, n_dp),
        (expand_got, reduce_got, second_0, seed, fed, back, second_1, residual_0, residual_1, *transposed),
        [((batch, own, width), bf16), carried[1]] + grads,
        feed_scratch,
        flops=8e9,
        smem=0,
    )

    two_a, two_b = [keep_e, swap(send_e, *CORE)], [keep_r, swap(send_r, *CORE)]
    pulled = [((own, width), f32), ((own, width), bf16), ((own, 3 * width), bf16), ((2, width), f32)]
    pull_scratch = [((long, 2 * width), f32), ((rows, width), bf16)]
    wide_0, low_0, grad_0, norm_0 = call(
        pull_first_kernel,
        (back, residual_0, seed, wc, norm_params, qkv_0, probs_0),
        pulled,
        pull_scratch,
        flops=8e9,
        smem=0,
    )
    (keep_e, keep_r), (send_e, send_r) = halved(place, [(two_a, NEAR), (two_b, ROW)], waits=(grad_0,))
    two_a, two_b = [keep_e, swap(send_e, *NEAR)], [keep_r, swap(send_r, *ROW)]
    wide_1, low_1, grad_1, norm_1, keep_a, keep_b, send_a, send_b = call(
        functools.partial(pull_last_kernel, n_dp),
        (
            place, back, residual_1, seed, wc, norm_params, qkv_1, probs_1,
            first_0, first_1, mixed_0, mixed_1, grad_0, low_0,
        ),
        pulled + [((4 * width, cols), bf16)] * 4,
        pull_scratch,
        waits=(send_e,),
        flops=10e9,
    )
    one_a, one_b = [keep_a, swap(send_a, *CORE)], [keep_b, swap(send_b, *CORE)]
    first, *others = far()
    (keep_e, keep_r), (sent,) = halved(
        place, [(two_a, first), (two_b, first)], joint=2, waits=(keep_a,)
    )
    (keep_a, keep_b), (send_a, send_b) = halved(place, [(one_a, NEAR), (one_b, ROW)], waits=(sent,))
    gots = swap(send_a, *NEAR), swap(send_b, *ROW)
    two_got = swap(sent, *first)
    grad_in_0, grad_in_1, norm = call(
        finish_kernel,
        (norm_params, wp, grad_0, frames_x[0], wide_0, grad_1, frames_x[1], wide_1, norm_0, norm_1),
        [((own, width), f32), ((own, width), f32), ((4 * parts, cols), f32)],
        waits=(send_a,),
        flops=3e9,
        smem=0,
    )
    norm = norm + swap(norm, *CORE)
    norms = (norm, swap(norm, *ROW))
    (keep_a, keep_b), norm, (send_a, send_b) = halved_norm(
        place, (keep_a, keep_b), gots, (ROW, NEAR), norms, False
    )
    gots = swap(send_a, *ROW), swap(send_b, *NEAR)
    (keep_e, keep_r), (send_e, send_r) = halved_joint(
        place, (keep_e, keep_r), two_got, (ROW, NEAR), joint=False, waits=(send_a,)
    )
    two_a, two_b = [keep_e, swap(send_e, *ROW)], [keep_r, swap(send_r, *NEAR)]
    pending = (send_e,)
    second, *others = others
    (keep_e, keep_r), (sent,) = halved(place, [(two_a, second), (two_b, second)], joint=2)
    two_got = swap(sent, *second)
    for label in others:
        (keep_e, keep_r), (sent,) = halved_joint(place, (keep_e, keep_r), two_got, (label, label))
        two_got = swap(sent, *label)
    for label in far():
        (keep_a, keep_b), norm, (sent,) = halved_norm(
            place, (keep_a, keep_b), gots, (label, label), (norm,), True, waits=pending
        )
        gots, pending = (swap(sent, *label),), ()

    plain = lambda x: [(x.shape, f32)] * 4
    weighed = lambda x: plain(x) + [(x.shape, bf16)]
    updated = call(
        update_feed_kernel,
        (
            keep_e, keep_r, two_got, weight_expand, moment_expand, average_expand,
            weight_reduce, moment_reduce, average_reduce,
        ),
        weighed(weight_expand) + weighed(weight_reduce),
        flops=1e8,
        smem=0,
        mib=8,
    )
    gradient_expand, mom_expand, avg_expand, new_expand, low_expand = updated[:5]
    gradient_reduce, mom_reduce, avg_reduce, new_reduce, low_reduce = updated[5:]
    updated = call(
        update_rest_kernel,
        (
            keep_a, keep_b, gots[0], norm, weight_project, moment_project, average_project,
            weight_combine, moment_combine, average_combine, norm_params, norm_moment, norm_average,
        ),
        weighed(weight_project) + weighed(weight_combine) + plain(norm_params),
        flops=1e8,
        smem=0,
        mib=8,
    )
    gradient_project, mom_project, avg_project, new_project, low_project = updated[:5]
    gradient_combine, mom_combine, avg_combine, new_combine, low_combine = updated[5:10]
    norm_gradient, mom_norms, avg_norms, new_norms = updated[10:]
    layer_out = jnp.transpose(layer, (1, 0, 2))
    input_gradient = jnp.transpose(jnp.stack([grad_in_0, grad_in_1]), (1, 0, 2))
    return (
        layer_out,
        input_gradient,
        gradient_project,
        gradient_combine,
        gradient_expand,
        gradient_reduce,
        mom_project,
        mom_combine,
        mom_expand,
        mom_reduce,
        avg_project,
        avg_combine,
        avg_expand,
        avg_reduce,
        new_project,
        new_combine,
        new_expand,
        new_reduce,
        low_project,
        low_combine,
        low_expand,
        low_reduce,
        norm_gradient,
        mom_norms,
        avg_norms,
        new_norms,
    )


def solution(mesh):
    tokens = P("mp", "dp", None)
    stacked, matrix = P(None, "dp", "mp"), P("dp", "mp")
    weights = (stacked, matrix, matrix, matrix)
    in_specs = (tokens, tokens, P("dp")) + weights * 3 + (P(),) * 3
    out_specs = (tokens, tokens) + weights * 5 + (P(),) * 4
    return jax.shard_map(
        on_device, mesh=mesh, in_specs=in_specs, out_specs=out_specs, check_vma=False
    )
```

```python
import functools
import math

import jax
import jax.numpy as jnp
from jax import lax
from jax.experimental import pallas as pl
from jax.experimental.pallas import tpu as pltpu
from jax.sharding import PartitionSpec as P

HEADS = 8
HEAD_DIM = 64
WINDOW = 10
HALO = 16

eps_norm = 1e-05
momentum_decay = 0.9
average_decay = 0.6
matrix_rate = 0.0001
norm_rate = 0.001
masked_score = -1e30

GROUP = 4
LANES = GROUP * HEAD_DIM
QUERIES = 112
KEYS = QUERIES + HALO

f32 = jnp.float32
bf16 = jnp.bfloat16


def mm(a, b):
    return lax.dot_general(a, b, (((1,), (0,)), ((), ())), preferred_element_type=f32)


def mm_bt(a, b):
    return lax.dot_general(a, b, (((1,), (1,)), ((), ())), preferred_element_type=f32)


def mm_at(a, b):
    return lax.dot_general(a, b, (((0,), (0,)), ((), ())), preferred_element_type=f32)


def normalise(values):
    center = values - jnp.mean(values, axis=-1, keepdims=True)
    spread = jnp.mean(center * center, axis=-1, keepdims=True)
    inverse = lax.rsqrt(spread + eps_norm)
    return center * inverse, inverse


def norm_backward(values, gain, upstream):
    scaled, inverse = normalise(values)
    weighted = upstream * gain
    inner = (
        weighted
        - jnp.mean(weighted, axis=-1, keepdims=True)
        - scaled * jnp.mean(weighted * scaled, axis=-1, keepdims=True)
    )
    return inner * inverse, upstream * scaled


def query_blocks(total):
    blocks = []
    at = HALO
    while at < total:
        rows = min(QUERIES, total - at)
        blocks.append((at, rows, min(at - HALO, total - KEYS)))
        at += rows
    return blocks


def band(block, start, length):
    q0, rows, k0 = block
    query = lax.broadcasted_iota(jnp.int32, (rows, KEYS), 0)
    key = lax.broadcasted_iota(jnp.int32, (rows, KEYS), 1)
    behind = query - key + (q0 - k0)
    time = key + (start + k0 - HALO)
    inside = (time < length) | (behind == 0)
    return (behind >= 0) & (behind <= WINDOW) & (time >= 0) & inside


def head_lanes():
    lane = lax.broadcasted_iota(jnp.int32, (1, LANES), 1)
    return [(lane >= h * HEAD_DIM) & (lane < (h + 1) * HEAD_DIM) for h in range(GROUP)]


def stack_heads(block):
    zero = jnp.zeros_like(block)
    return jnp.concatenate([jnp.where(m, block, zero) for m in head_lanes()], axis=0)


def merge_heads(stacked, rows):
    masks = head_lanes()
    out = jnp.where(masks[0], stacked[:rows], 0.0)
    for h in range(1, GROUP):
        out = jnp.where(masks[h], stacked[h * rows : (h + 1) * rows], out)
    return out


def softmax_rows(scores, allowed):
    scores = jnp.where(allowed, scores * (1.0 / math.sqrt(HEAD_DIM)), masked_score)
    raised = jnp.exp(scores - jnp.max(scores, axis=-1, keepdims=True))
    return raised / jnp.sum(raised, axis=-1, keepdims=True)


def block_order(n_dp, near_first, split=False):
    row, near, far_bits = -1, 0, list(range(1, (n_dp - 1).bit_length()))
    first, second = (near, row) if near_first else (row, near)
    bits = [first, far_bits[0], second, *far_bits[1:]] if split else [first, second, *far_bits]
    blocks = []
    for at in range(2 * n_dp):
        value = {bit: (at >> (len(bits) - 1 - i)) & 1 for i, bit in enumerate(bits)}
        blocks.append((value[row], sum(value[bit] << bit for bit in bits if bit != row)))
    return blocks


def place_weights(n_dp, core, own_a, own_b, got_a, got_b, wp_ref, wc_ref):
    width, cols = wc_ref.shape[0], own_a.shape[1]
    r = width // n_dp
    for which, ref_a, ref_b in ((core, own_a, own_b), (1 - core, got_a, got_b)):
        for ref, first, near_first in ((ref_a, 0, True), (ref_b, 2, False)):
            for p, (y, d) in enumerate(block_order(n_dp, near_first)):
                at = pl.multiple_of((2 * y + which) * cols, cols)
                for i in range(2):
                    source, to = ref, (2 * p + i) * r
                    if isinstance(ref, tuple):
                        source, to = ref[to // ref[0].shape[0]], to % ref[0].shape[0]
                    block = source[to : to + r]
                    if first + i < 3:
                        wp_ref[d * r : (d + 1) * r, pl.ds((first + i) * width + at, cols)] = block
                    else:
                        wc_ref[d * r : (d + 1) * r, pl.ds(at, cols)] = block


def edge_kernel(place_ref, frames_ref, cotangent_ref, near_ref, over_ref):
    last = frames_ref.shape[1] - HALO
    for core, early, late in ((0, over_ref, near_ref), (1, near_ref, over_ref)):

        @pl.when(place_ref[1] == core)
        def _():
            early[0] = frames_ref[:, :HALO]
            early[1] = cotangent_ref[:, :HALO]
            late[0] = frames_ref[:, last:]
            late[1] = frames_ref[:, last:]


def frames_kernel(place_ref, frames_ref, near_ref, over_ref, *outs):
    own = frames_ref.shape[1]
    for u, out in enumerate(outs):
        out[HALO : HALO + own] = frames_ref[u]
    for core, left, right in ((0, over_ref, near_ref), (1, near_ref, over_ref)):

        @pl.when(place_ref[1] == core)
        def _():
            for u, out in enumerate(outs):
                out[:HALO] = left[0, u]
                out[HALO + own :] = right[0, u]


def seed_kernel(place_ref, cotangent_ref, near_ref, over_ref, seed_ref, seed_t_ref):
    own = cotangent_ref.shape[1]
    for u in range(seed_ref.shape[0]):

        def valid(first, count):
            time = lax.broadcasted_iota(jnp.int32, (count, 1), 0) + (place_ref[0] + first)
            return time < place_ref[2 + u]

        mine = cotangent_ref[u]
        mine = jnp.where(valid(0, own), mine, jnp.zeros_like(mine))
        seed_ref[u, :own] = mine
        seed_t_ref[:, u * own : (u + 1) * own] = mine.T
        theirs = jnp.where(place_ref[1] == 0, near_ref[1, u], over_ref[1, u])
        seed_ref[u, own:] = jnp.where(valid(own, HALO), theirs, jnp.zeros_like(theirs))


def attend_one(
    u, place_ref, frames_ref, norms_ref, wp_ref, wc_ref,
    qkv_ref, probs_ref, first_ref, mixed_ref, residual_ref, second_ref, second_t_ref,
):
    total, width = frames_ref.shape
    own = first_ref.shape[0]
    start, length = place_ref[0], place_ref[2 + u]
    scaled, _ = normalise(frames_ref[...].astype(f32))
    normed = (scaled * norms_ref[0:1] + norms_ref[1:2]).astype(bf16)
    first_ref[...] = normed[HALO : HALO + own]
    qkv_ref[...] = mm(normed, wp_ref[...]).astype(bf16)
    def group(hg, carry):
        at, here = hg * LANES, hg * KEYS
        if u > 0:
            at, here = pl.multiple_of(at, LANES), pl.multiple_of(here, KEYS)
        here = pl.ds(here, KEYS)
        for b, block in enumerate(query_blocks(total)):
            q0, rows, k0 = block
            allowed = band(block, start, length)
            queries = stack_heads(qkv_ref[q0 : q0 + rows, pl.ds(at, LANES)])
            keys = qkv_ref[k0 : k0 + KEYS, pl.ds(width + at, LANES)]
            values = qkv_ref[k0 : k0 + KEYS, pl.ds(2 * width + at, LANES)]
            scores = mm_bt(queries, keys)
            low_probs = []
            for h in range(GROUP):
                probs = softmax_rows(scores[h * rows : (h + 1) * rows], allowed)
                probs_ref[b, h, :rows, here] = probs
                low_probs.append(probs.astype(bf16))
            out = merge_heads(mm(jnp.concatenate(low_probs, axis=0), values), rows)
            mixed_ref[q0 - HALO : q0 - HALO + rows, pl.ds(at, LANES)] = out.astype(bf16)
        return carry

    if u == 0:
        for hg in range(width // LANES):
            group(hg, 0)
    else:
        lax.fori_loop(0, width // LANES, group, 0)
    residual = frames_ref[HALO:total].astype(f32) + mm_bt(mixed_ref[...], wc_ref[...])
    residual_ref[...] = residual
    scaled, _ = normalise(residual)
    second_ref[...] = (scaled * norms_ref[2:3] + norms_ref[3:4]).astype(bf16)
    second_t_ref[...] = second_ref[:own].T


def attend_first_kernel(
    n_dp, place_ref, frames_ref, norms_ref, own_a, own_b, got_a0, got_a1, got_b0, got_b1, *refs
):
    *outs, wp_ref, wc_ref = refs
    got = (got_a0, got_a1), (got_b0, got_b1)
    place_weights(n_dp, place_ref[1], own_a, own_b, *got, wp_ref, wc_ref)
    attend_one(0, place_ref, frames_ref, norms_ref, wp_ref, wc_ref, *outs)


def attend_next_kernel(place_ref, frames_ref, norms_ref, wp_ref, wc_ref, *refs):
    attend_one(1, place_ref, frames_ref, norms_ref, wp_ref, wc_ref, *refs)


def gelu_parts(value):
    slope = math.sqrt(2.0 / math.pi)
    square = value * value
    tanh = jnp.tanh(value * (slope + (slope * 0.044715) * square))
    half = 0.5 + 0.5 * tanh
    curve = half + (0.5 * value) * (1.0 - tanh * tanh) * (
        slope + (slope * 3.0 * 0.044715) * square
    )
    return value * half, curve


def feed_half(
    n_dp, seconds, seconds_t, seed_ref, seed_t_ref, we_ref, wr_ref, ge_ref, gr_ref,
    wide_e, wide_r, active_ref, grad_ref, add_fed, add_back,
):
    own = seconds_t[0].shape[1]
    width, hidden = wide_e.shape[0], we_ref.shape[1]
    r = width // n_dp
    for ref, wide, near_first in ((we_ref, wide_e, True), (wr_ref, wide_r, False)):
        for p, (y, d) in enumerate(block_order(n_dp, near_first)):
            wide[d * r : (d + 1) * r, y * hidden : (y + 1) * hidden] = ref[p * r : (p + 1) * r]
    for u, second_ref in enumerate(seconds):
        rows = slice(u * own, (u + 1) * own)
        active, curve = gelu_parts(mm(second_ref[...], wide_e[...]))
        active_ref[rows] = active[:own].astype(bf16)
        grad_ref[u] = (mm(seed_ref[u], wide_r[...]) * curve).astype(bf16)
        add_fed(u, mm_bt(active_ref[rows], wide_r[...]))
        add_back(u, mm_bt(grad_ref[u], wide_e[...]))
    total_r = mm(seed_t_ref[...], active_ref[...])
    total_e = mm(seconds_t[0][...], grad_ref[0, :own]) + mm(seconds_t[1][...], grad_ref[1, :own])
    for total, ref, near_first in ((total_e, ge_ref, True), (total_r, gr_ref, False)):
        for p, (y, d) in enumerate(block_order(n_dp, near_first, True)):
            block = total[d * r : (d + 1) * r, y * hidden : (y + 1) * hidden]
            ref[p * r : (p + 1) * r] = block.astype(bf16)


def feed_first_kernel(n_dp, we_ref, wr_ref, n0, seed_ref, n1, seed_t_ref, t0, t1, *refs):
    fed_ref, back_ref, ge_ref, gr_ref, *scratch = refs

    def add_fed(u, value):
        fed_ref[u] = value

    def add_back(u, value):
        back_ref[u] = value

    feed_half(
        n_dp, (n0, n1), (t0, t1), seed_ref, seed_t_ref, we_ref, wr_ref, ge_ref, gr_ref,
        *scratch, add_fed, add_back,
    )


def feed_last_kernel(
    n_dp, we_ref, wr_ref, n0, seed_ref, fed_in, back_in, n1, r0, r1, seed_t_ref, t0, t1, *refs
):
    out_ref, back_ref, ge_ref, gr_ref, *scratch = refs
    own = out_ref.shape[1]

    def add_fed(u, value):
        out_ref[u] = ((r0, r1)[u][:own] + (fed_in[u] + value)).astype(bf16)

    def add_back(u, value):
        back_ref[u] = back_in[u] + value

    feed_half(
        n_dp, (n0, n1), (t0, t1), seed_ref, seed_t_ref, we_ref, wr_ref, ge_ref, gr_ref,
        *scratch, add_fed, add_back,
    )


def pull_one(
    u, back_ref, residual_ref, seed_ref, wc_ref, norms_ref, qkv_ref, probs_ref,
    wide_ref, low_ref, grad_ref, norm_ref, grad_kv_ref, mixed_g_ref,
):
    total = qkv_ref.shape[0]
    own, width = low_ref.shape
    upstream = back_ref[u]
    back, gained = norm_backward(residual_ref[...], norms_ref[2:3], upstream)
    norm_ref[0:1] = jnp.sum(gained[:own], axis=0, keepdims=True)
    norm_ref[1:2] = jnp.sum(upstream[:own], axis=0, keepdims=True)
    wide = seed_ref[u].astype(f32) + back
    wide_ref[...] = wide[:own]
    low = wide.astype(bf16)
    low_ref[...] = low[:own]
    mixed_g_ref[...] = mm(low, wc_ref[...]).astype(bf16)
    grad_kv_ref[...] = jnp.zeros_like(grad_kv_ref)
    scale = 1.0 / math.sqrt(HEAD_DIM)
    blocks = query_blocks(total)
    even = len(blocks) - 1

    def one_block(hg, b, o0, k0, rows, mine):
        q0 = o0 + HALO
        at = pl.multiple_of(hg * LANES, LANES)
        here = pl.ds(pl.multiple_of(hg * KEYS, KEYS), KEYS)
        first_lanes, second_lanes = pl.ds(at, LANES), pl.ds(width + at, LANES)
        queries = stack_heads(qkv_ref[pl.ds(q0, rows), first_lanes])
        keys = qkv_ref[pl.ds(k0, KEYS), second_lanes]
        values = qkv_ref[pl.ds(k0, KEYS), pl.ds(2 * width + at, LANES)]
        upper = stack_heads(mixed_g_ref[pl.ds(o0, rows), first_lanes])
        grad_probs = mm_bt(upper, values)
        low_probs, grad_scores = [], []
        for h in range(GROUP):
            probs = probs_ref[b, h, :rows, here]
            grad = grad_probs[h * rows : (h + 1) * rows]
            inner = jnp.sum(probs * grad, axis=-1, keepdims=True)
            low_probs.append(probs.astype(bf16))
            grad_scores.append((probs * (grad - inner)).astype(bf16))
        low_probs = jnp.concatenate(low_probs, axis=0)
        grad_scores = jnp.concatenate(grad_scores, axis=0)
        grad_q = merge_heads(mm(grad_scores, keys), rows) * scale
        grad_ref[pl.ds(o0, mine), first_lanes] = grad_q[:mine].astype(bf16)
        grad_kv_ref[pl.ds(k0, KEYS), first_lanes] += mm_at(grad_scores, queries) * scale
        grad_kv_ref[pl.ds(k0, KEYS), second_lanes] += mm_at(low_probs, upper)

    def some(i, carry):
        b = i % even
        o0 = pl.multiple_of(b * QUERIES, HALO)
        one_block(i // even, b, o0, o0, QUERIES, QUERIES)
        return carry

    def rest(hg, carry):
        q0, rows, k0 = blocks[-1]
        one_block(hg, even, q0 - HALO, k0, rows, HALO + own - q0)
        return carry

    def every(hg, carry):
        for b, (q0, rows, k0) in enumerate(blocks):
            one_block(hg, b, q0 - HALO, k0, rows, min(rows, HALO + own - q0))
        return carry

    if u == 0:
        lax.fori_loop(0, width // LANES, every, 0)
    else:
        lax.fori_loop(0, even * (width // LANES), some, 0)
        lax.fori_loop(0, width // LANES, rest, 0)
    grad_ref[:, width:] = grad_kv_ref[HALO : HALO + own].astype(bf16)


def pull_first_kernel(*refs):
    pull_one(0, *refs)


def pull_last_kernel(
    n_dp, place_ref, back_ref, residual_ref, seed_ref, wc_ref, norms_ref, qkv_ref, probs_ref,
    first_0, first_1, mixed_0, mixed_1, grad_0, low_0, *refs,
):
    wide_ref, low_ref, grad_ref, norm_ref, keep_a, keep_b, send_a, send_b, grad_kv_ref, mixed_g_ref = refs
    pull_one(
        1, back_ref, residual_ref, seed_ref, wc_ref, norms_ref, qkv_ref, probs_ref,
        wide_ref, low_ref, grad_ref, norm_ref, grad_kv_ref, mixed_g_ref,
    )
    own, width = low_ref.shape
    core, cols, r = place_ref[1], keep_a.shape[1], width // n_dp
    firsts = first_0[...].T, first_1[...].T
    lows = low_0[...].T, low_ref[...].T
    where = {
        near_first: {block: p for p, block in enumerate(block_order(n_dp, near_first))}
        for near_first in (True, False)
    }
    for i in range(4):
        keep, send, at = (keep_a, send_a, where[True]) if i < 2 else (keep_b, send_b, where[False])
        for y in range(2):
            lanes = slice(2 * y * cols, 2 * (y + 1) * cols)
            if i < 3:
                inner = slice(i * width + lanes.start, i * width + lanes.stop)
                value = mm(firsts[0], grad_0[:, inner]) + mm(firsts[1], grad_ref[:, inner])
            else:
                value = mm(lows[0], mixed_0[:own, lanes]) + mm(lows[1], mixed_1[:own, lanes])
            mine = jnp.where(core == 0, value[:, :cols], value[:, cols:])
            other = jnp.where(core == 0, value[:, cols:], value[:, :cols])
            for d in range(n_dp):
                to = (2 * at[y, d] + i % 2) * r
                keep[to : to + r] = mine[d * r : (d + 1) * r].astype(bf16)
                send[to : to + r] = other[d * r : (d + 1) * r].astype(bf16)


def fold_norm(ref, first, value):
    cols = ref.shape[1]
    for j in range(value.shape[1] // cols):
        ref[4 * j + first : 4 * j + first + value.shape[0]] = value[:, j * cols : (j + 1) * cols]


def finish_kernel(norms_ref, wp_ref, grad_0, frames_0, wide_0, grad_1, frames_1, wide_1, norm_0, norm_1, out_0, out_1, norm_ref):
    own, width = out_0.shape
    step = own // 2
    gain, shift = jnp.zeros((1, width), f32), jnp.zeros((1, width), f32)
    for grad_ref, frames_ref, wide_ref, out_ref in (
        (grad_0, frames_0, wide_0, out_0),
        (grad_1, frames_1, wide_1, out_1),
    ):

        def one(i, carry):
            at = pl.ds(pl.multiple_of(i * step, step), step)
            frames = frames_ref[pl.ds(pl.multiple_of(HALO + i * step, HALO), step)]
            upstream = mm_bt(grad_ref[at], wp_ref[...])
            back, gained = norm_backward(frames.astype(f32), norms_ref[0:1], upstream)
            out_ref[at] = wide_ref[at] + back
            gain, shift = carry
            return (
                gain + jnp.sum(gained, axis=0, keepdims=True),
                shift + jnp.sum(upstream, axis=0, keepdims=True),
            )

        gain, shift = lax.fori_loop(0, own // step, one, (gain, shift))
    fold_norm(norm_ref, 0, gain)
    fold_norm(norm_ref, 1, shift)
    fold_norm(norm_ref, 2, norm_0[...] + norm_1[...])


VM = pl.BlockSpec(memory_space=pltpu.VMEM)
SM = pl.BlockSpec(memory_space=pltpu.SMEM)
MIB = 1024 * 1024


def call(kernel, ins, outs, scratch=(), waits=(), flops=1e9, smem=1, mib=16):
    n, m = len(ins), len(outs)
    away = pl.BlockSpec(memory_space=pl.ANY)

    def body(*refs):
        kernel(*refs[:n], *refs[n + len(waits) :])

    return pl.pallas_call(
        body,
        out_shape=tuple(jax.ShapeDtypeStruct(shape, kind) for shape, kind in outs),
        in_specs=[SM] * smem + [VM] * (n - smem) + [away] * len(waits),
        out_specs=(VM,) * m,
        scratch_shapes=[pltpu.VMEM(shape, kind) for shape, kind in scratch],
        compiler_params=pltpu.CompilerParams(vmem_limit_bytes=mib * MIB),
        cost_estimate=pl.CostEstimate(flops=int(flops), bytes_accessed=6000000, transcendentals=0),
    )(*ins, *waits)


def swap(value, axis, bit):
    n = lax.axis_size(axis)
    return lax.ppermute(value, axis, [(i, i ^ (1 << bit)) for i in range(n)])


CORE, ROW, NEAR = ("mp", 0), ("mp", 1), ("dp", 0)


def far():
    return [("dp", b) for b in range(1, (lax.axis_size("dp") - 1).bit_length())]


def side(label):
    return (lax.axis_index(label[0]) >> label[1]) & 1


def by_rows(rows, body):
    step = 128
    if rows <= step or rows % step:
        body(slice(None))
        return

    def one(i, carry):
        body(pl.ds(pl.multiple_of(i * step, step), step))
        return carry

    lax.fori_loop(0, rows // step, one, 0)


def spot(label):
    return {CORE: 1, ROW: 4, NEAR: 5}.get(label, 5 + label[1])


def paired(place, streams, waits=()):
    def kernel(place_ref, *refs):
        outs = list(refs[2 * len(streams) :])
        for i, (_, _, label, parts) in enumerate(streams):
            mine, got = refs[2 * i], refs[2 * i + 1]
            high = place_ref[spot(label)]
            for part in range(parts):
                out = outs.pop(0)

                def body(at):
                    out[high, :, at] = mine[:, part, at]
                    out[1 - high, :, at] = got[:, part, at]

                by_rows(out.shape[2], body)

    ins, outs = [place], []
    for mine, got, label, parts in streams:
        blocks = lax.axis_size("dp") // 4 if parts > 1 else 1
        shape = (blocks, parts, mine.shape[0] // blocks // parts, mine.shape[1])
        ins += [mine.reshape(shape), got.reshape(shape)]
        outs += [((2, blocks, *shape[2:]), mine.dtype)] * parts
    return [x.reshape(-1, x.shape[-1]) for x in call(kernel, ins, outs, waits=waits, flops=1e8, mib=8)]


def lowered(arrays, waits):
    rows = [x.shape[0] for x in arrays]

    def kernel(*refs):
        at = 0
        for ref, count in zip(refs, rows):
            refs[-1][at : at + count] = ref[...].astype(bf16)
            at += count

    return call(kernel, arrays, [((sum(rows), arrays[0].shape[1]), bf16)], waits=waits, flops=1e8, smem=0, mib=8)[0]


def halved(place, streams, joint=0, waits=()):
    counts = [len(terms) for terms, _ in streams]
    n = len(streams)

    def kernel(place_ref, *refs):
        refs = list(refs)
        groups = [[refs.pop(0) for _ in range(count)] for count in counts]
        kept, sent = refs[:n], refs[n:]
        for i, (group, (_, label)) in enumerate(zip(groups, streams)):
            mine = place_ref[spot(label)]

            def body(at):
                kept[i][at] = total([ref[mine, at] for ref in group])
                gone = total([ref[1 - mine, at] for ref in group]).astype(bf16)
                if i < joint:
                    sent[0][i, at] = gone
                else:
                    sent[i - max(0, joint - 1)][at] = gone

            by_rows(kept[i].shape[0], body)

    ins, keeps, sends = [place], [], []
    for terms, _ in streams:
        half, cols = terms[0].size // terms[0].shape[-1] // 2, terms[0].shape[-1]
        ins += [term.reshape(2, half, cols) for term in terms]
        keeps.append(((half, cols), f32))
        sends.append(((half, cols), bf16))
    if joint:
        sends = [((joint, *sends[0][0]), bf16), *sends[joint:]]
    done = call(kernel, ins, keeps + sends, waits=waits, flops=1e8, mib=8)
    return done[:n], done[n:]


def halved_joint(place, keeps, got, labels, joint=True, waits=()):
    n = len(keeps)
    half, cols = keeps[0].shape[0] // 2, keeps[0].shape[1]

    def kernel(place_ref, *refs):
        for i in range(n):
            mine = place_ref[spot(labels[i])]

            def body(at):
                kept = refs[i][mine, at] + refs[n][i, mine, at].astype(f32)
                gone = refs[i][1 - mine, at] + refs[n][i, 1 - mine, at].astype(f32)
                refs[n + 1 + i][at] = kept
                if joint:
                    refs[2 * n + 1][i, at] = gone.astype(bf16)
                else:
                    refs[2 * n + 1 + i][at] = gone.astype(bf16)

            by_rows(half, body)

    ins = [place, *[keep.reshape(2, half, cols) for keep in keeps], got.reshape(n, 2, half, cols)]
    sends = [((n, half, cols), bf16)] if joint else [((half, cols), bf16)] * n
    done = call(kernel, ins, [((half, cols), f32)] * n + sends, waits=waits, flops=1e8, mib=8)
    return done[:n], done[n:]


def halved_norm(place, keeps, gots, labels, norms, joint, waits=()):
    rows, cols = keeps[0].shape
    half, extra = rows // 2, norms[0].shape[0]
    n = len(gots)

    def kernel(place_ref, *refs):
        keep, got, norm, outs = refs[:2], refs[2 : 2 + n], refs[2 + n : -5 if not joint else -4], refs[-5 if not joint else -4 :]
        arrived = [(got[0], 0), (got[-1], 0 if n == 2 else rows)]
        for i in range(2):
            mine = place_ref[spot(labels[i])]
            ref, at = arrived[i]
            here = keep[i][pl.ds(pl.multiple_of(mine * half, half), half)].astype(f32)
            there = keep[i][pl.ds(pl.multiple_of((1 - mine) * half, half), half)].astype(f32)
            here += ref[pl.ds(pl.multiple_of(at + mine * half, half), half)].astype(f32)
            there += ref[pl.ds(pl.multiple_of(at + (1 - mine) * half, half), half)].astype(f32)
            outs[i][...] = here
            if joint:
                outs[3][i * half : (i + 1) * half] = there.astype(bf16)
            else:
                outs[3 + i][:half] = there.astype(bf16)
        if len(norm) == 2:
            value = norm[0][...] + norm[1][...]
        else:
            ref, at = arrived[1]
            value = joined_norm(norm[0][...], ref[at + rows : at + rows + 2 * extra])
        outs[2][...] = value
        split_norm(value, outs[-1], 2 * half if joint else half)

    small = [((half, cols), f32)] * 2 + [((extra, cols), f32)]
    if joint:
        sends = [((2 * half + 2 * extra, cols), bf16)]
    else:
        sends = [((half, cols), bf16), ((half + 2 * extra, cols), bf16)]
    done = call(kernel, (place, *keeps, *gots, *norms), small + sends, waits=waits, flops=1e8, mib=8)
    return done[:2], done[2], done[3:]


def split_norm(value, ref, at):
    rows = value.shape[0]
    high = value.astype(bf16)
    ref[at : at + rows] = high
    ref[at + rows : at + 2 * rows] = (value - high.astype(f32)).astype(bf16)


def joined_norm(value, got):
    rows = value.shape[0]
    high = value.astype(bf16).astype(f32)
    low = (value - high).astype(bf16).astype(f32)
    return (high + low) + (got[:rows].astype(f32) + got[rows:].astype(f32))


def total(terms):
    terms = [term.astype(f32) for term in terms]
    return functools.reduce(jnp.add, terms)


def write_update(outs, at, gradient, states, rate):
    values = advance(*states[:1], gradient, *states[1:], rate)
    for out, value in zip(outs, (gradient, *values)):
        out[at] = value
    if len(outs) > 4:
        outs[4][at] = values[2].astype(bf16)


def update_feed_kernel(keep_e, keep_r, got_ref, *refs):
    states, outs = refs[:6], refs[6:]
    for i, keep in enumerate((keep_e, keep_r)):
        gradient = keep[...] + got_ref[i].astype(f32)
        state = [ref[...] for ref in states[3 * i : 3 * i + 3]]
        write_update(outs[5 * i : 5 * i + 5], slice(None), gradient, state, matrix_rate)


def update_rest_kernel(keep_a, keep_b, got_ref, norm_ref, *refs):
    states, outs = refs[:9], refs[9:]
    rows, cols = keep_a.shape
    r, extra = rows // 2, norm_ref.shape[0]
    for i in range(4):
        keep = (keep_a, keep_b)[i // 2]
        at = (i % 2) * r
        gradient = keep[at : at + r] + got_ref[i * r : (i + 1) * r].astype(f32)
        which, entry = (0, i) if i < 3 else (1, slice(None))
        state = [ref[entry] for ref in states[3 * which : 3 * which + 3]]
        write_update(outs[5 * which : 5 * which + 5], entry, gradient, state, matrix_rate)
    value = joined_norm(norm_ref[...], got_ref[2 * rows : 2 * rows + 2 * extra])
    for j in range(extra // 4):
        at = (slice(None), slice(j * cols, (j + 1) * cols))
        state = [ref[at] for ref in states[6:]]
        write_update(outs[10:], at, value[4 * j : 4 * j + 4], state, norm_rate)


def advance(weight, gradient, moment, average, rate):
    momentum = momentum_decay * moment + gradient
    updated = weight - rate * (gradient + momentum_decay * momentum)
    smoothed = average_decay * average + (1.0 - average_decay) * updated
    return (momentum, smoothed, updated)


def on_device(
    frames,
    cotangent,
    lengths,
    weight_project,
    weight_combine,
    weight_expand,
    weight_reduce,
    moment_project,
    moment_combine,
    moment_expand,
    moment_reduce,
    average_project,
    average_combine,
    average_expand,
    average_reduce,
    norm_params,
    norm_moment,
    norm_average,
):
    own, batch, width = frames.shape
    long, rows = own + 2 * HALO, own + HALO
    parts, n_dp = lax.axis_size("mp"), lax.axis_size("dp")
    me = lax.axis_index("mp")
    start = me * own
    cols, hidden = width // parts, weight_expand.shape[1]
    r = width // n_dp

    sides = [side(label) for label in (ROW, NEAR, *far())]
    place = jnp.concatenate(
        [jnp.stack([start, side(CORE)]).astype(jnp.int32), lengths, jnp.stack(sides).astype(jnp.int32)]
    )
    *outer, last = reversed(far())

    matrices = jnp.concatenate([weight_project, weight_combine[None]], axis=0).astype(bf16)
    one = matrices.reshape(-1, cols)
    for label in outer:
        (one,) = paired(place, [(one, swap(one, *label), label, 1)])
    one_got = swap(one, *last)

    two = lowered([weight_expand, weight_reduce], waits=(one,))
    one_a, one_b = paired(place, [(one, one_got, last, 2)])
    frames_u = jnp.transpose(frames, (1, 0, 2))
    cotangent_u = jnp.transpose(cotangent, (1, 0, 2))
    strip = ((2, batch, HALO, width), bf16)
    near, over = call(
        edge_kernel,
        (place, frames_u, cotangent_u),
        [strip] * 2,
        waits=(one_got,),
        flops=1e8,
        mib=8,
    )
    near = swap(near, *CORE)
    pairs = [(i, i + 1) for i in range(1, parts - 1, 2)]
    over = lax.ppermute(over, "mp", pairs + [(b, a) for a, b in pairs])
    frames_x = call(
        frames_kernel, (place, frames_u, near, over), [((long, width), bf16)] * 2, flops=1e8, mib=8
    )
    got_a, got_b = swap(one_a, *ROW), swap(one_b, *NEAR)
    for label in outer:
        (two,) = paired(place, [(two, swap(two, *label), label, 1)])
    one_a, one_b = paired(
        place, [(one_a, got_a, ROW, 1), (one_b, got_b, NEAR, 1)], waits=(two,)
    )
    got_a, got_b = swap(one_a, *NEAR), swap(one_b, *ROW)
    two_a, two_b = paired(place, [(two, swap(two, *last), last, 2)])
    one_a, one_b = paired(
        place, [(one_a, got_a, NEAR, 1), (one_b, got_b, ROW, 1)], waits=(two_a, *frames_x)
    )
    cut = one_a.shape[0] // 2
    core_parts = [swap(x, *CORE) for x in (one_a[:cut], one_a[cut:], one_b[:cut], one_b[cut:])]

    per_u = [
        ((long, 3 * width), bf16),
        ((-(-rows // QUERIES), GROUP, QUERIES, width // LANES * KEYS), f32),
        ((own, width), bf16),
        ((rows, width), bf16),
        ((rows, width), f32),
        ((rows, width), bf16),
        ((width, own), bf16),
    ]
    seed, seed_t = call(
        seed_kernel,
        (place, cotangent_u, near, over),
        [((batch, rows, width), bf16), ((width, batch * own), bf16)],
        waits=(one_a,),
        flops=1e8,
        mib=8,
    )

    got_a, got_b = swap(two_a, *ROW), swap(two_b, *NEAR)
    two_a, two_b = paired(place, [(two_a, got_a, ROW, 1), (two_b, got_b, NEAR, 1)], waits=(seed,))
    qkv_0, probs_0, first_0, mixed_0, residual_0, second_0, second_t_0, wp, wc = call(
        functools.partial(attend_first_kernel, n_dp),
        (place, frames_x[0], norm_params, one_a, one_b, *core_parts),
        per_u + [((width, 3 * width), bf16), ((width, width), bf16)],
        waits=(two_a, two_b),
        flops=5e9,
    )
    qkv_1, probs_1, first_1, mixed_1, residual_1, second_1, second_t_1 = call(
        attend_next_kernel,
        (place, frames_x[1], norm_params, wp, wc),
        per_u,
        flops=5e9,
    )
    got_a, got_b = swap(two_a, *NEAR), swap(two_b, *ROW)
    expand, reduce_w = paired(
        place, [(two_a, got_a, NEAR, 1), (two_b, got_b, ROW, 1)], waits=(second_1,)
    )
    expand_got, reduce_got = swap(expand, *CORE), swap(reduce_w, *CORE)

    grads = [((2 * width, hidden), bf16)] * 2
    carried = [((batch, own, width), f32), ((batch, rows, width), f32)]
    feed_scratch = [((width, 2 * hidden), bf16)] * 2 + [
        ((batch * own, 2 * hidden), bf16),
        ((batch, rows, 2 * hidden), bf16),
    ]
    transposed = (seed_t, second_t_0, second_t_1)
    fed, back, keep_e, keep_r = call(
        functools.partial(feed_first_kernel, n_dp),
        (expand, reduce_w, second_0, seed, second_1, *transposed),
        carried + grads,
        feed_scratch,
        flops=8e9,
        smem=0,
    )
    layer, back, send_e, send_r = call(
        functools.partial(feed_last_kernel, n_dp),
        (expand_got, reduce_got, second_0, seed, fed, back, second_1, residual_0, residual_1, *transposed),
        [((batch, own, width), bf16), carried[1]] + grads,
        feed_scratch,
        flops=8e9,
        smem=0,
    )

    two_a, two_b = [keep_e, swap(send_e, *CORE)], [keep_r, swap(send_r, *CORE)]
    pulled = [((own, width), f32), ((own, width), bf16), ((own, 3 * width), bf16), ((2, width), f32)]
    pull_scratch = [((long, 2 * width), f32), ((rows, width), bf16)]
    wide_0, low_0, grad_0, norm_0 = call(
        pull_first_kernel,
        (back, residual_0, seed, wc, norm_params, qkv_0, probs_0),
        pulled,
        pull_scratch,
        flops=8e9,
        smem=0,
    )
    (keep_e, keep_r), (send_e, send_r) = halved(place, [(two_a, NEAR), (two_b, ROW)], waits=(grad_0,))
    two_a, two_b = [keep_e, swap(send_e, *NEAR)], [keep_r, swap(send_r, *ROW)]
    wide_1, low_1, grad_1, norm_1, keep_a, keep_b, send_a, send_b = call(
        functools.partial(pull_last_kernel, n_dp),
        (
            place, back, residual_1, seed, wc, norm_params, qkv_1, probs_1,
            first_0, first_1, mixed_0, mixed_1, grad_0, low_0,
        ),
        pulled + [((4 * width, cols), bf16)] * 4,
        pull_scratch,
        waits=(send_e,),
        flops=10e9,
    )
    one_a, one_b = [keep_a, swap(send_a, *CORE)], [keep_b, swap(send_b, *CORE)]
    first, *others = far()
    (keep_e, keep_r), (sent,) = halved(
        place, [(two_a, first), (two_b, first)], joint=2, waits=(keep_a,)
    )
    (keep_a, keep_b), (send_a, send_b) = halved(place, [(one_a, NEAR), (one_b, ROW)], waits=(sent,))
    gots = swap(send_a, *NEAR), swap(send_b, *ROW)
    two_got = swap(sent, *first)
    grad_in_0, grad_in_1, norm = call(
        finish_kernel,
        (norm_params, wp, grad_0, frames_x[0], wide_0, grad_1, frames_x[1], wide_1, norm_0, norm_1),
        [((own, width), f32), ((own, width), f32), ((4 * parts, cols), f32)],
        waits=(send_a,),
        flops=3e9,
        smem=0,
    )
    norm = norm + swap(norm, *CORE)
    norms = (norm, swap(norm, *ROW))
    (keep_a, keep_b), norm, (send_a, send_b) = halved_norm(
        place, (keep_a, keep_b), gots, (ROW, NEAR), norms, False
    )
    gots = swap(send_a, *ROW), swap(send_b, *NEAR)
    (keep_e, keep_r), (send_e, send_r) = halved_joint(
        place, (keep_e, keep_r), two_got, (ROW, NEAR), joint=False, waits=(send_a,)
    )
    two_a, two_b = [keep_e, swap(send_e, *ROW)], [keep_r, swap(send_r, *NEAR)]
    pending = (send_e,)
    second, *others = others
    (keep_e, keep_r), (sent,) = halved(place, [(two_a, second), (two_b, second)], joint=2)
    two_got = swap(sent, *second)
    for label in others:
        (keep_e, keep_r), (sent,) = halved_joint(place, (keep_e, keep_r), two_got, (label, label))
        two_got = swap(sent, *label)
    for label in far():
        (keep_a, keep_b), norm, (sent,) = halved_norm(
            place, (keep_a, keep_b), gots, (label, label), (norm,), True, waits=pending
        )
        gots, pending = (swap(sent, *label),), ()

    plain = lambda x: [(x.shape, f32)] * 4
    weighed = lambda x: plain(x) + [(x.shape, bf16)]
    updated = call(
        update_feed_kernel,
        (
            keep_e, keep_r, two_got, weight_expand, moment_expand, average_expand,
            weight_reduce, moment_reduce, average_reduce,
        ),
        weighed(weight_expand) + weighed(weight_reduce),
        flops=1e8,
        smem=0,
        mib=8,
    )
    gradient_expand, mom_expand, avg_expand, new_expand, low_expand = updated[:5]
    gradient_reduce, mom_reduce, avg_reduce, new_reduce, low_reduce = updated[5:]
    updated = call(
        update_rest_kernel,
        (
            keep_a, keep_b, gots[0], norm, weight_project, moment_project, average_project,
            weight_combine, moment_combine, average_combine, norm_params, norm_moment, norm_average,
        ),
        weighed(weight_project) + weighed(weight_combine) + plain(norm_params),
        flops=1e8,
        smem=0,
        mib=8,
    )
    gradient_project, mom_project, avg_project, new_project, low_project = updated[:5]
    gradient_combine, mom_combine, avg_combine, new_combine, low_combine = updated[5:10]
    norm_gradient, mom_norms, avg_norms, new_norms = updated[10:]
    layer_out = jnp.transpose(layer, (1, 0, 2))
    input_gradient = jnp.transpose(jnp.stack([grad_in_0, grad_in_1]), (1, 0, 2))
    return (
        layer_out,
        input_gradient,
        gradient_project,
        gradient_combine,
        gradient_expand,
        gradient_reduce,
        mom_project,
        mom_combine,
        mom_expand,
        mom_reduce,
        avg_project,
        avg_combine,
        avg_expand,
        avg_reduce,
        new_project,
        new_combine,
        new_expand,
        new_reduce,
        low_project,
        low_combine,
        low_expand,
        low_reduce,
        norm_gradient,
        mom_norms,
        avg_norms,
        new_norms,
    )


def solution(mesh):
    tokens = P("mp", "dp", None)
    stacked, matrix = P(None, "dp", "mp"), P("dp", "mp")
    weights = (stacked, matrix, matrix, matrix)
    in_specs = (tokens, tokens, P("dp")) + weights * 3 + (P(),) * 3
    out_specs = (tokens, tokens) + weights * 5 + (P(),) * 4
    return jax.shard_map(
        on_device, mesh=mesh, in_specs=in_specs, out_specs=out_specs, check_vma=False
    )
```

```python
import functools
import math

import jax
import jax.numpy as jnp
from jax import lax
from jax.experimental import pallas as pl
from jax.experimental.pallas import tpu as pltpu
from jax.sharding import PartitionSpec as P

HEADS = 8
HEAD_DIM = 64
WINDOW = 10
HALO = 16

eps_norm = 1e-05
momentum_decay = 0.9
average_decay = 0.6
matrix_rate = 0.0001
norm_rate = 0.001
masked_score = -1e30

GROUP = 4
LANES = GROUP * HEAD_DIM
QUERIES = 112
KEYS = QUERIES + HALO

f32 = jnp.float32
bf16 = jnp.bfloat16


def mm(a, b):
    return lax.dot_general(a, b, (((1,), (0,)), ((), ())), preferred_element_type=f32)


def mm_bt(a, b):
    return lax.dot_general(a, b, (((1,), (1,)), ((), ())), preferred_element_type=f32)


def mm_at(a, b):
    return lax.dot_general(a, b, (((0,), (0,)), ((), ())), preferred_element_type=f32)


def normalise(values):
    center = values - jnp.mean(values, axis=-1, keepdims=True)
    spread = jnp.mean(center * center, axis=-1, keepdims=True)
    inverse = lax.rsqrt(spread + eps_norm)
    return center * inverse, inverse


def norm_backward(values, gain, upstream):
    scaled, inverse = normalise(values)
    weighted = upstream * gain
    inner = (
        weighted
        - jnp.mean(weighted, axis=-1, keepdims=True)
        - scaled * jnp.mean(weighted * scaled, axis=-1, keepdims=True)
    )
    return inner * inverse, upstream * scaled


def query_blocks(total):
    blocks = []
    at = HALO
    while at < total:
        rows = min(QUERIES, total - at)
        blocks.append((at, rows, min(at - HALO, total - KEYS)))
        at += rows
    return blocks


def band(block, start, length):
    q0, rows, k0 = block
    query = lax.broadcasted_iota(jnp.int32, (rows, KEYS), 0)
    key = lax.broadcasted_iota(jnp.int32, (rows, KEYS), 1)
    behind = query - key + (q0 - k0)
    time = key + (start + k0 - HALO)
    inside = (time < length) | (behind == 0)
    return (behind >= 0) & (behind <= WINDOW) & (time >= 0) & inside


def head_lanes():
    lane = lax.broadcasted_iota(jnp.int32, (1, LANES), 1)
    return [(lane >= h * HEAD_DIM) & (lane < (h + 1) * HEAD_DIM) for h in range(GROUP)]


def stack_heads(block):
    zero = jnp.zeros_like(block)
    return jnp.concatenate([jnp.where(m, block, zero) for m in head_lanes()], axis=0)


def merge_heads(stacked, rows):
    masks = head_lanes()
    out = jnp.where(masks[0], stacked[:rows], 0.0)
    for h in range(1, GROUP):
        out = jnp.where(masks[h], stacked[h * rows : (h + 1) * rows], out)
    return out


def softmax_rows(scores, allowed):
    scores = jnp.where(allowed, scores * (1.0 / math.sqrt(HEAD_DIM)), masked_score)
    raised = jnp.exp(scores - jnp.max(scores, axis=-1, keepdims=True))
    return raised / jnp.sum(raised, axis=-1, keepdims=True)


def block_order(n_dp, near_first, split=False):
    row, near, far_bits = -1, 0, list(range(1, (n_dp - 1).bit_length()))
    first, second = (near, row) if near_first else (row, near)
    bits = [first, far_bits[0], second, *far_bits[1:]] if split else [first, second, *far_bits]
    blocks = []
    for at in range(2 * n_dp):
        value = {bit: (at >> (len(bits) - 1 - i)) & 1 for i, bit in enumerate(bits)}
        blocks.append((value[row], sum(value[bit] << bit for bit in bits if bit != row)))
    return blocks


def place_weights(n_dp, core, own_a, own_b, got_a, got_b, wp_ref, wc_ref):
    width, cols = wc_ref.shape[0], own_a.shape[1]
    r = width // n_dp
    for which, ref_a, ref_b in ((core, own_a, own_b), (1 - core, got_a, got_b)):
        for ref, first, near_first in ((ref_a, 0, True), (ref_b, 2, False)):
            for p, (y, d) in enumerate(block_order(n_dp, near_first)):
                at = pl.multiple_of((2 * y + which) * cols, cols)
                for i in range(2):
                    source, to = ref, (2 * p + i) * r
                    if isinstance(ref, tuple):
                        source, to = ref[to // ref[0].shape[0]], to % ref[0].shape[0]
                    block = source[to : to + r]
                    if first + i < 3:
                        wp_ref[d * r : (d + 1) * r, pl.ds((first + i) * width + at, cols)] = block
                    else:
                        wc_ref[d * r : (d + 1) * r, pl.ds(at, cols)] = block


def edge_kernel(place_ref, frames_ref, cotangent_ref, near_ref, over_ref):
    last = frames_ref.shape[1] - HALO
    for core, early, late in ((0, over_ref, near_ref), (1, near_ref, over_ref)):

        @pl.when(place_ref[1] == core)
        def _():
            early[0] = frames_ref[:, :HALO]
            early[1] = cotangent_ref[:, :HALO]
            late[0] = frames_ref[:, last:]
            late[1] = frames_ref[:, last:]


def frames_kernel(place_ref, frames_ref, near_ref, over_ref, *outs):
    own = frames_ref.shape[1]
    for u, out in enumerate(outs):
        out[HALO : HALO + own] = frames_ref[u]
    for core, left, right in ((0, over_ref, near_ref), (1, near_ref, over_ref)):

        @pl.when(place_ref[1] == core)
        def _():
            for u, out in enumerate(outs):
                out[:HALO] = left[0, u]
                out[HALO + own :] = right[0, u]


def seed_kernel(place_ref, cotangent_ref, near_ref, over_ref, seed_ref, seed_t_ref):
    own = cotangent_ref.shape[1]
    for u in range(seed_ref.shape[0]):

        def valid(first, count):
            time = lax.broadcasted_iota(jnp.int32, (count, 1), 0) + (place_ref[0] + first)
            return time < place_ref[2 + u]

        mine = cotangent_ref[u]
        mine = jnp.where(valid(0, own), mine, jnp.zeros_like(mine))
        seed_ref[u, :own] = mine
        seed_t_ref[:, u * own : (u + 1) * own] = mine.T
        theirs = jnp.where(place_ref[1] == 0, near_ref[1, u], over_ref[1, u])
        seed_ref[u, own:] = jnp.where(valid(own, HALO), theirs, jnp.zeros_like(theirs))


def attend_one(
    u, place_ref, frames_ref, norms_ref, wp_ref, wc_ref,
    qkv_ref, probs_ref, first_ref, mixed_ref, residual_ref, second_ref, second_t_ref,
):
    total, width = frames_ref.shape
    own = first_ref.shape[0]
    start, length = place_ref[0], place_ref[2 + u]
    scaled, _ = normalise(frames_ref[...].astype(f32))
    normed = (scaled * norms_ref[0:1] + norms_ref[1:2]).astype(bf16)
    first_ref[...] = normed[HALO : HALO + own]
    qkv_ref[...] = mm(normed, wp_ref[...]).astype(bf16)
    def group(hg, carry):
        at, here = hg * LANES, hg * KEYS
        if u > 0:
            at, here = pl.multiple_of(at, LANES), pl.multiple_of(here, KEYS)
        here = pl.ds(here, KEYS)
        for b, block in enumerate(query_blocks(total)):
            q0, rows, k0 = block
            allowed = band(block, start, length)
            queries = stack_heads(qkv_ref[q0 : q0 + rows, pl.ds(at, LANES)])
            keys = qkv_ref[k0 : k0 + KEYS, pl.ds(width + at, LANES)]
            values = qkv_ref[k0 : k0 + KEYS, pl.ds(2 * width + at, LANES)]
            scores = mm_bt(queries, keys)
            low_probs = []
            for h in range(GROUP):
                probs = softmax_rows(scores[h * rows : (h + 1) * rows], allowed)
                probs_ref[b, h, :rows, here] = probs
                low_probs.append(probs.astype(bf16))
            out = merge_heads(mm(jnp.concatenate(low_probs, axis=0), values), rows)
            mixed_ref[q0 - HALO : q0 - HALO + rows, pl.ds(at, LANES)] = out.astype(bf16)
        return carry

    if u == 0:
        for hg in range(width // LANES):
            group(hg, 0)
    else:
        lax.fori_loop(0, width // LANES, group, 0)
    residual = frames_ref[HALO:total].astype(f32) + mm_bt(mixed_ref[...], wc_ref[...])
    residual_ref[...] = residual
    scaled, _ = normalise(residual)
    second_ref[...] = (scaled * norms_ref[2:3] + norms_ref[3:4]).astype(bf16)
    second_t_ref[...] = second_ref[:own].T


def attend_first_kernel(
    n_dp, place_ref, frames_ref, norms_ref, own_a, own_b, got_a0, got_a1, got_b0, got_b1, *refs
):
    *outs, wp_ref, wc_ref = refs
    got = (got_a0, got_a1), (got_b0, got_b1)
    place_weights(n_dp, place_ref[1], own_a, own_b, *got, wp_ref, wc_ref)
    attend_one(0, place_ref, frames_ref, norms_ref, wp_ref, wc_ref, *outs)


def attend_next_kernel(place_ref, frames_ref, norms_ref, wp_ref, wc_ref, *refs):
    attend_one(1, place_ref, frames_ref, norms_ref, wp_ref, wc_ref, *refs)


def gelu_parts(value):
    slope = math.sqrt(2.0 / math.pi)
    square = value * value
    half = 0.5 + 0.5 * jnp.tanh(value * (slope + (slope * 0.044715) * square))
    active = value * half
    curve = half + (active * (1.0 - half)) * (2.0 * slope + (slope * 6.0 * 0.044715) * square)
    return active, curve


def feed_half(
    n_dp, seconds, seconds_t, seed_ref, seed_t_ref, we_ref, wr_ref, ge_ref, gr_ref,
    wide_e, wide_r, active_ref, grad_ref, add_fed, add_back,
):
    own = seconds_t[0].shape[1]
    width, hidden = wide_e.shape[0], we_ref.shape[1]
    r = width // n_dp
    for ref, wide, near_first in ((we_ref, wide_e, True), (wr_ref, wide_r, False)):
        for p, (y, d) in enumerate(block_order(n_dp, near_first)):
            wide[d * r : (d + 1) * r, y * hidden : (y + 1) * hidden] = ref[p * r : (p + 1) * r]
    for u, second_ref in enumerate(seconds):
        rows = slice(u * own, (u + 1) * own)
        active, curve = gelu_parts(mm(second_ref[...], wide_e[...]))
        active_ref[rows] = active[:own].astype(bf16)
        grad_ref[u] = (mm(seed_ref[u], wide_r[...]) * curve).astype(bf16)
        add_fed(u, mm_bt(active_ref[rows], wide_r[...]))
        add_back(u, mm_bt(grad_ref[u], wide_e[...]))
    total_r = mm(seed_t_ref[...], active_ref[...])
    total_e = mm(seconds_t[0][...], grad_ref[0, :own]) + mm(seconds_t[1][...], grad_ref[1, :own])
    for total, ref, near_first in ((total_e, ge_ref, True), (total_r, gr_ref, False)):
        for p, (y, d) in enumerate(block_order(n_dp, near_first, True)):
            block = total[d * r : (d + 1) * r, y * hidden : (y + 1) * hidden]
            ref[p * r : (p + 1) * r] = block.astype(bf16)


def feed_first_kernel(n_dp, we_ref, wr_ref, n0, seed_ref, n1, seed_t_ref, t0, t1, *refs):
    fed_ref, back_ref, ge_ref, gr_ref, *scratch = refs

    def add_fed(u, value):
        fed_ref[u] = value

    def add_back(u, value):
        back_ref[u] = value

    feed_half(
        n_dp, (n0, n1), (t0, t1), seed_ref, seed_t_ref, we_ref, wr_ref, ge_ref, gr_ref,
        *scratch, add_fed, add_back,
    )


def feed_last_kernel(
    n_dp, we_ref, wr_ref, n0, seed_ref, fed_in, back_in, n1, r0, r1, seed_t_ref, t0, t1, *refs
):
    out_ref, back_ref, ge_ref, gr_ref, *scratch = refs
    own = out_ref.shape[1]

    def add_fed(u, value):
        out_ref[u] = ((r0, r1)[u][:own] + (fed_in[u] + value)).astype(bf16)

    def add_back(u, value):
        back_ref[u] = back_in[u] + value

    feed_half(
        n_dp, (n0, n1), (t0, t1), seed_ref, seed_t_ref, we_ref, wr_ref, ge_ref, gr_ref,
        *scratch, add_fed, add_back,
    )


def pull_one(
    u, back_ref, residual_ref, seed_ref, wc_ref, norms_ref, qkv_ref, probs_ref,
    wide_ref, low_ref, grad_ref, norm_ref, grad_kv_ref, mixed_g_ref,
):
    total = qkv_ref.shape[0]
    own, width = low_ref.shape
    upstream = back_ref[u]
    back, gained = norm_backward(residual_ref[...], norms_ref[2:3], upstream)
    norm_ref[0:1] = jnp.sum(gained[:own], axis=0, keepdims=True)
    norm_ref[1:2] = jnp.sum(upstream[:own], axis=0, keepdims=True)
    wide = seed_ref[u].astype(f32) + back
    wide_ref[...] = wide[:own]
    low = wide.astype(bf16)
    low_ref[...] = low[:own]
    mixed_g_ref[...] = mm(low, wc_ref[...]).astype(bf16)
    grad_kv_ref[...] = jnp.zeros_like(grad_kv_ref)
    scale = 1.0 / math.sqrt(HEAD_DIM)
    blocks = query_blocks(total)
    even = len(blocks) - 1

    def one_block(hg, b, o0, k0, rows, mine):
        q0 = o0 + HALO
        at = pl.multiple_of(hg * LANES, LANES)
        here = pl.ds(pl.multiple_of(hg * KEYS, KEYS), KEYS)
        first_lanes, second_lanes = pl.ds(at, LANES), pl.ds(width + at, LANES)
        queries = stack_heads(qkv_ref[pl.ds(q0, rows), first_lanes])
        keys = qkv_ref[pl.ds(k0, KEYS), second_lanes]
        values = qkv_ref[pl.ds(k0, KEYS), pl.ds(2 * width + at, LANES)]
        upper = stack_heads(mixed_g_ref[pl.ds(o0, rows), first_lanes])
        grad_probs = mm_bt(upper, values)
        low_probs, grad_scores = [], []
        for h in range(GROUP):
            probs = probs_ref[b, h, :rows, here]
            grad = grad_probs[h * rows : (h + 1) * rows]
            inner = jnp.sum(probs * grad, axis=-1, keepdims=True)
            low_probs.append(probs.astype(bf16))
            grad_scores.append((probs * (grad - inner)).astype(bf16))
        low_probs = jnp.concatenate(low_probs, axis=0)
        grad_scores = jnp.concatenate(grad_scores, axis=0)
        grad_q = merge_heads(mm(grad_scores, keys), rows) * scale
        grad_ref[pl.ds(o0, mine), first_lanes] = grad_q[:mine].astype(bf16)
        grad_kv_ref[pl.ds(k0, KEYS), first_lanes] += mm_at(grad_scores, queries) * scale
        grad_kv_ref[pl.ds(k0, KEYS), second_lanes] += mm_at(low_probs, upper)

    def some(i, carry):
        b = i % even
        o0 = pl.multiple_of(b * QUERIES, HALO)
        one_block(i // even, b, o0, o0, QUERIES, QUERIES)
        return carry

    def rest(hg, carry):
        q0, rows, k0 = blocks[-1]
        one_block(hg, even, q0 - HALO, k0, rows, HALO + own - q0)
        return carry

    def every(hg, carry):
        for b, (q0, rows, k0) in enumerate(blocks):
            one_block(hg, b, q0 - HALO, k0, rows, min(rows, HALO + own - q0))
        return carry

    if u == 0:
        lax.fori_loop(0, width // LANES, every, 0)
    else:
        lax.fori_loop(0, even * (width // LANES), some, 0)
        lax.fori_loop(0, width // LANES, rest, 0)
    grad_ref[:, width:] = grad_kv_ref[HALO : HALO + own].astype(bf16)


def pull_first_kernel(*refs):
    pull_one(0, *refs)


def pull_last_kernel(
    n_dp, place_ref, back_ref, residual_ref, seed_ref, wc_ref, norms_ref, qkv_ref, probs_ref,
    first_0, first_1, mixed_0, mixed_1, grad_0, low_0, *refs,
):
    wide_ref, low_ref, grad_ref, norm_ref, keep_a, keep_b, send_a, send_b, grad_kv_ref, mixed_g_ref = refs
    pull_one(
        1, back_ref, residual_ref, seed_ref, wc_ref, norms_ref, qkv_ref, probs_ref,
        wide_ref, low_ref, grad_ref, norm_ref, grad_kv_ref, mixed_g_ref,
    )
    own, width = low_ref.shape
    core, cols, r = place_ref[1], keep_a.shape[1], width // n_dp
    firsts = first_0[...].T, first_1[...].T
    lows = low_0[...].T, low_ref[...].T
    where = {
        near_first: {block: p for p, block in enumerate(block_order(n_dp, near_first))}
        for near_first in (True, False)
    }
    for i in range(4):
        keep, send, at = (keep_a, send_a, where[True]) if i < 2 else (keep_b, send_b, where[False])
        for y in range(2):
            lanes = slice(2 * y * cols, 2 * (y + 1) * cols)
            if i < 3:
                inner = slice(i * width + lanes.start, i * width + lanes.stop)
                value = mm(firsts[0], grad_0[:, inner]) + mm(firsts[1], grad_ref[:, inner])
            else:
                value = mm(lows[0], mixed_0[:own, lanes]) + mm(lows[1], mixed_1[:own, lanes])
            mine = jnp.where(core == 0, value[:, :cols], value[:, cols:])
            other = jnp.where(core == 0, value[:, cols:], value[:, :cols])
            for d in range(n_dp):
                to = (2 * at[y, d] + i % 2) * r
                keep[to : to + r] = mine[d * r : (d + 1) * r].astype(bf16)
                send[to : to + r] = other[d * r : (d + 1) * r].astype(bf16)


def fold_norm(ref, first, value):
    cols = ref.shape[1]
    for j in range(value.shape[1] // cols):
        ref[4 * j + first : 4 * j + first + value.shape[0]] = value[:, j * cols : (j + 1) * cols]


def finish_kernel(norms_ref, wp_ref, grad_0, frames_0, wide_0, grad_1, frames_1, wide_1, norm_0, norm_1, out_0, out_1, norm_ref):
    own, width = out_0.shape
    step = own // 2
    gain, shift = jnp.zeros((1, width), f32), jnp.zeros((1, width), f32)
    for grad_ref, frames_ref, wide_ref, out_ref in (
        (grad_0, frames_0, wide_0, out_0),
        (grad_1, frames_1, wide_1, out_1),
    ):

        def one(i, carry):
            at = pl.ds(pl.multiple_of(i * step, step), step)
            frames = frames_ref[pl.ds(pl.multiple_of(HALO + i * step, HALO), step)]
            upstream = mm_bt(grad_ref[at], wp_ref[...])
            back, gained = norm_backward(frames.astype(f32), norms_ref[0:1], upstream)
            out_ref[at] = wide_ref[at] + back
            gain, shift = carry
            return (
                gain + jnp.sum(gained, axis=0, keepdims=True),
                shift + jnp.sum(upstream, axis=0, keepdims=True),
            )

        gain, shift = lax.fori_loop(0, own // step, one, (gain, shift))
    fold_norm(norm_ref, 0, gain)
    fold_norm(norm_ref, 1, shift)
    fold_norm(norm_ref, 2, norm_0[...] + norm_1[...])


VM = pl.BlockSpec(memory_space=pltpu.VMEM)
SM = pl.BlockSpec(memory_space=pltpu.SMEM)
MIB = 1024 * 1024


def call(kernel, ins, outs, scratch=(), waits=(), flops=1e9, smem=1, mib=16):
    n, m = len(ins), len(outs)
    away = pl.BlockSpec(memory_space=pl.ANY)

    def body(*refs):
        kernel(*refs[:n], *refs[n + len(waits) :])

    return pl.pallas_call(
        body,
        out_shape=tuple(jax.ShapeDtypeStruct(shape, kind) for shape, kind in outs),
        in_specs=[SM] * smem + [VM] * (n - smem) + [away] * len(waits),
        out_specs=(VM,) * m,
        scratch_shapes=[pltpu.VMEM(shape, kind) for shape, kind in scratch],
        compiler_params=pltpu.CompilerParams(vmem_limit_bytes=mib * MIB),
        cost_estimate=pl.CostEstimate(flops=int(flops), bytes_accessed=6000000, transcendentals=0),
    )(*ins, *waits)


def swap(value, axis, bit):
    n = lax.axis_size(axis)
    return lax.ppermute(value, axis, [(i, i ^ (1 << bit)) for i in range(n)])


CORE, ROW, NEAR = ("mp", 0), ("mp", 1), ("dp", 0)


def far():
    return [("dp", b) for b in range(1, (lax.axis_size("dp") - 1).bit_length())]


def side(label):
    return (lax.axis_index(label[0]) >> label[1]) & 1


def by_rows(rows, body):
    step = 128
    if rows <= step or rows % step:
        body(slice(None))
        return

    def one(i, carry):
        body(pl.ds(pl.multiple_of(i * step, step), step))
        return carry

    lax.fori_loop(0, rows // step, one, 0)


def spot(label):
    return {CORE: 1, ROW: 4, NEAR: 5}.get(label, 5 + label[1])


def paired(place, streams, waits=()):
    def kernel(place_ref, *refs):
        outs = list(refs[2 * len(streams) :])
        for i, (_, _, label, parts) in enumerate(streams):
            mine, got = refs[2 * i], refs[2 * i + 1]
            high = place_ref[spot(label)]
            for part in range(parts):
                out = outs.pop(0)

                def body(at):
                    out[high, :, at] = mine[:, part, at]
                    out[1 - high, :, at] = got[:, part, at]

                by_rows(out.shape[2], body)

    ins, outs = [place], []
    for mine, got, label, parts in streams:
        blocks = lax.axis_size("dp") // 4 if parts > 1 else 1
        shape = (blocks, parts, mine.shape[0] // blocks // parts, mine.shape[1])
        ins += [mine.reshape(shape), got.reshape(shape)]
        outs += [((2, blocks, *shape[2:]), mine.dtype)] * parts
    return [x.reshape(-1, x.shape[-1]) for x in call(kernel, ins, outs, waits=waits, flops=1e8, mib=8)]


def lowered(arrays, waits):
    rows = [x.shape[0] for x in arrays]

    def kernel(*refs):
        at = 0
        for ref, count in zip(refs, rows):
            refs[-1][at : at + count] = ref[...].astype(bf16)
            at += count

    return call(kernel, arrays, [((sum(rows), arrays[0].shape[1]), bf16)], waits=waits, flops=1e8, smem=0, mib=8)[0]


def halved(place, streams, joint=0, waits=()):
    counts = [len(terms) for terms, _ in streams]
    n = len(streams)

    def kernel(place_ref, *refs):
        refs = list(refs)
        groups = [[refs.pop(0) for _ in range(count)] for count in counts]
        kept, sent = refs[:n], refs[n:]
        for i, (group, (_, label)) in enumerate(zip(groups, streams)):
            mine = place_ref[spot(label)]

            def body(at):
                kept[i][at] = total([ref[mine, at] for ref in group])
                gone = total([ref[1 - mine, at] for ref in group]).astype(bf16)
                if i < joint:
                    sent[0][i, at] = gone
                else:
                    sent[i - max(0, joint - 1)][at] = gone

            by_rows(kept[i].shape[0], body)

    ins, keeps, sends = [place], [], []
    for terms, _ in streams:
        half, cols = terms[0].size // terms[0].shape[-1] // 2, terms[0].shape[-1]
        ins += [term.reshape(2, half, cols) for term in terms]
        keeps.append(((half, cols), f32))
        sends.append(((half, cols), bf16))
    if joint:
        sends = [((joint, *sends[0][0]), bf16), *sends[joint:]]
    done = call(kernel, ins, keeps + sends, waits=waits, flops=1e8, mib=8)
    return done[:n], done[n:]


def halved_joint(place, keeps, got, labels, joint=True, waits=()):
    n = len(keeps)
    half, cols = keeps[0].shape[0] // 2, keeps[0].shape[1]

    def kernel(place_ref, *refs):
        for i in range(n):
            mine = place_ref[spot(labels[i])]

            def body(at):
                kept = refs[i][mine, at] + refs[n][i, mine, at].astype(f32)
                gone = refs[i][1 - mine, at] + refs[n][i, 1 - mine, at].astype(f32)
                refs[n + 1 + i][at] = kept
                if joint:
                    refs[2 * n + 1][i, at] = gone.astype(bf16)
                else:
                    refs[2 * n + 1 + i][at] = gone.astype(bf16)

            by_rows(half, body)

    ins = [place, *[keep.reshape(2, half, cols) for keep in keeps], got.reshape(n, 2, half, cols)]
    sends = [((n, half, cols), bf16)] if joint else [((half, cols), bf16)] * n
    done = call(kernel, ins, [((half, cols), f32)] * n + sends, waits=waits, flops=1e8, mib=8)
    return done[:n], done[n:]


def halved_norm(place, keeps, gots, labels, norms, joint, waits=()):
    rows, cols = keeps[0].shape
    half, extra = rows // 2, norms[0].shape[0]
    n = len(gots)

    def kernel(place_ref, *refs):
        keep, got, norm, outs = refs[:2], refs[2 : 2 + n], refs[2 + n : -5 if not joint else -4], refs[-5 if not joint else -4 :]
        arrived = [(got[0], 0), (got[-1], 0 if n == 2 else rows)]
        for i in range(2):
            mine = place_ref[spot(labels[i])]
            ref, at = arrived[i]
            here = keep[i][pl.ds(pl.multiple_of(mine * half, half), half)].astype(f32)
            there = keep[i][pl.ds(pl.multiple_of((1 - mine) * half, half), half)].astype(f32)
            here += ref[pl.ds(pl.multiple_of(at + mine * half, half), half)].astype(f32)
            there += ref[pl.ds(pl.multiple_of(at + (1 - mine) * half, half), half)].astype(f32)
            outs[i][...] = here
            if joint:
                outs[3][i * half : (i + 1) * half] = there.astype(bf16)
            else:
                outs[3 + i][:half] = there.astype(bf16)
        if len(norm) == 2:
            value = norm[0][...] + norm[1][...]
        else:
            ref, at = arrived[1]
            value = joined_norm(norm[0][...], ref[at + rows : at + rows + 2 * extra])
        outs[2][...] = value
        split_norm(value, outs[-1], 2 * half if joint else half)

    small = [((half, cols), f32)] * 2 + [((extra, cols), f32)]
    if joint:
        sends = [((2 * half + 2 * extra, cols), bf16)]
    else:
        sends = [((half, cols), bf16), ((half + 2 * extra, cols), bf16)]
    done = call(kernel, (place, *keeps, *gots, *norms), small + sends, waits=waits, flops=1e8, mib=8)
    return done[:2], done[2], done[3:]


def split_norm(value, ref, at):
    rows = value.shape[0]
    high = value.astype(bf16)
    ref[at : at + rows] = high
    ref[at + rows : at + 2 * rows] = (value - high.astype(f32)).astype(bf16)


def joined_norm(value, got):
    rows = value.shape[0]
    high = value.astype(bf16).astype(f32)
    low = (value - high).astype(bf16).astype(f32)
    return (high + low) + (got[:rows].astype(f32) + got[rows:].astype(f32))


def total(terms):
    terms = [term.astype(f32) for term in terms]
    return functools.reduce(jnp.add, terms)


def write_update(outs, at, gradient, states, rate):
    values = advance(*states[:1], gradient, *states[1:], rate)
    for out, value in zip(outs, (gradient, *values)):
        out[at] = value
    if len(outs) > 4:
        outs[4][at] = values[2].astype(bf16)


def update_feed_kernel(keep_e, keep_r, got_ref, *refs):
    states, outs = refs[:6], refs[6:]
    outs[10][...] = jnp.zeros_like(outs[10])
    for i, keep in enumerate((keep_e, keep_r)):
        gradient = keep[...] + got_ref[i].astype(f32)
        state = [ref[...] for ref in states[3 * i : 3 * i + 3]]
        write_update(outs[5 * i : 5 * i + 5], slice(None), gradient, state, matrix_rate)


def update_rest_kernel(keep_a, keep_b, got_ref, norm_ref, *refs):
    states, outs = refs[:9], refs[9:]
    rows, cols = keep_a.shape
    r, extra = rows // 2, norm_ref.shape[0]
    for i in range(4):
        keep = (keep_a, keep_b)[i // 2]
        at = (i % 2) * r
        gradient = keep[at : at + r] + got_ref[i * r : (i + 1) * r].astype(f32)
        which, entry = (0, i) if i < 3 else (1, slice(None))
        state = [ref[entry] for ref in states[3 * which : 3 * which + 3]]
        write_update(outs[5 * which : 5 * which + 5], entry, gradient, state, matrix_rate)
    value = joined_norm(norm_ref[...], got_ref[2 * rows : 2 * rows + 2 * extra])
    for j in range(extra // 4):
        at = (slice(None), slice(j * cols, (j + 1) * cols))
        state = [ref[at] for ref in states[6:]]
        write_update(outs[10:], at, value[4 * j : 4 * j + 4], state, norm_rate)


def advance(weight, gradient, moment, average, rate):
    momentum = momentum_decay * moment + gradient
    updated = weight - rate * (gradient + momentum_decay * momentum)
    smoothed = average_decay * average + (1.0 - average_decay) * updated
    return (momentum, smoothed, updated)


def on_device(
    frames,
    cotangent,
    lengths,
    weight_project,
    weight_combine,
    weight_expand,
    weight_reduce,
    moment_project,
    moment_combine,
    moment_expand,
    moment_reduce,
    average_project,
    average_combine,
    average_expand,
    average_reduce,
    norm_params,
    norm_moment,
    norm_average,
):
    own, batch, width = frames.shape
    long, rows = own + 2 * HALO, own + HALO
    parts, n_dp = lax.axis_size("mp"), lax.axis_size("dp")
    me = lax.axis_index("mp")
    start = me * own
    cols, hidden = width // parts, weight_expand.shape[1]
    r = width // n_dp

    sides = [side(label) for label in (ROW, NEAR, *far())]
    place = jnp.concatenate(
        [jnp.stack([start, side(CORE)]).astype(jnp.int32), lengths, jnp.stack(sides).astype(jnp.int32)]
    )
    *outer, last = reversed(far())

    matrices = jnp.concatenate([weight_project, weight_combine[None]], axis=0).astype(bf16)
    one = matrices.reshape(-1, cols)
    for label in outer:
        (one,) = paired(place, [(one, swap(one, *label), label, 1)])
    one_got = swap(one, *last)

    two = lowered([weight_expand, weight_reduce], waits=(one,))
    one_a, one_b = paired(place, [(one, one_got, last, 2)])
    frames_u = jnp.transpose(frames, (1, 0, 2))
    cotangent_u = jnp.transpose(cotangent, (1, 0, 2))
    strip = ((2, batch, HALO, width), bf16)
    near, over = call(
        edge_kernel,
        (place, frames_u, cotangent_u),
        [strip] * 2,
        waits=(one_got,),
        flops=1e8,
        mib=8,
    )
    near = swap(near, *CORE)
    pairs = [(i, i + 1) for i in range(1, parts - 1, 2)]
    over = lax.ppermute(over, "mp", pairs + [(b, a) for a, b in pairs])
    frames_x = call(
        frames_kernel, (place, frames_u, near, over), [((long, width), bf16)] * 2, flops=1e8, mib=8
    )
    got_a, got_b = swap(one_a, *ROW), swap(one_b, *NEAR)
    for label in outer:
        (two,) = paired(place, [(two, swap(two, *label), label, 1)])
    one_a, one_b = paired(
        place, [(one_a, got_a, ROW, 1), (one_b, got_b, NEAR, 1)], waits=(two,)
    )
    got_a, got_b = swap(one_a, *NEAR), swap(one_b, *ROW)
    two_a, two_b = paired(place, [(two, swap(two, *last), last, 2)])
    one_a, one_b = paired(
        place, [(one_a, got_a, NEAR, 1), (one_b, got_b, ROW, 1)], waits=(two_a, *frames_x)
    )
    cut = one_a.shape[0] // 2
    core_parts = [swap(x, *CORE) for x in (one_a[:cut], one_a[cut:], one_b[:cut], one_b[cut:])]

    per_u = [
        ((long, 3 * width), bf16),
        ((-(-rows // QUERIES), GROUP, QUERIES, width // LANES * KEYS), f32),
        ((own, width), bf16),
        ((rows, width), bf16),
        ((rows, width), f32),
        ((rows, width), bf16),
        ((width, own), bf16),
    ]
    seed, seed_t = call(
        seed_kernel,
        (place, cotangent_u, near, over),
        [((batch, rows, width), bf16), ((width, batch * own), bf16)],
        waits=(one_a,),
        flops=1e8,
        mib=8,
    )

    got_a, got_b = swap(two_a, *ROW), swap(two_b, *NEAR)
    two_a, two_b = paired(place, [(two_a, got_a, ROW, 1), (two_b, got_b, NEAR, 1)], waits=(seed,))
    qkv_0, probs_0, first_0, mixed_0, residual_0, second_0, second_t_0, wp, wc = call(
        functools.partial(attend_first_kernel, n_dp),
        (place, frames_x[0], norm_params, one_a, one_b, *core_parts),
        per_u + [((width, 3 * width), bf16), ((width, width), bf16)],
        waits=(two_a, two_b),
        flops=5e9,
    )
    qkv_1, probs_1, first_1, mixed_1, residual_1, second_1, second_t_1 = call(
        attend_next_kernel,
        (place, frames_x[1], norm_params, wp, wc),
        per_u,
        flops=5e9,
    )
    got_a, got_b = swap(two_a, *NEAR), swap(two_b, *ROW)
    expand, reduce_w = paired(
        place, [(two_a, got_a, NEAR, 1), (two_b, got_b, ROW, 1)], waits=(second_1,)
    )
    expand_got, reduce_got = swap(expand, *CORE), swap(reduce_w, *CORE)

    grads = [((2 * width, hidden), bf16)] * 2
    carried = [((batch, own, width), f32), ((batch, rows, width), f32)]
    feed_scratch = [((width, 2 * hidden), bf16)] * 2 + [
        ((batch * own, 2 * hidden), bf16),
        ((batch, rows, 2 * hidden), bf16),
    ]
    transposed = (seed_t, second_t_0, second_t_1)
    fed, back, keep_e, keep_r = call(
        functools.partial(feed_first_kernel, n_dp),
        (expand, reduce_w, second_0, seed, second_1, *transposed),
        carried + grads,
        feed_scratch,
        flops=8e9,
        smem=0,
    )
    layer, back, send_e, send_r = call(
        functools.partial(feed_last_kernel, n_dp),
        (expand_got, reduce_got, second_0, seed, fed, back, second_1, residual_0, residual_1, *transposed),
        [((batch, own, width), bf16), carried[1]] + grads,
        feed_scratch,
        flops=8e9,
        smem=0,
    )

    two_a, two_b = [keep_e, swap(send_e, *CORE)], [keep_r, swap(send_r, *CORE)]
    pulled = [((own, width), f32), ((own, width), bf16), ((own, 3 * width), bf16), ((2, width), f32)]
    pull_scratch = [((long, 2 * width), f32), ((rows, width), bf16)]
    wide_0, low_0, grad_0, norm_0 = call(
        pull_first_kernel,
        (back, residual_0, seed, wc, norm_params, qkv_0, probs_0),
        pulled,
        pull_scratch,
        flops=8e9,
        smem=0,
    )
    (keep_e, keep_r), (send_e, send_r) = halved(place, [(two_a, NEAR), (two_b, ROW)], waits=(grad_0,))
    two_a, two_b = [keep_e, swap(send_e, *NEAR)], [keep_r, swap(send_r, *ROW)]
    wide_1, low_1, grad_1, norm_1, keep_a, keep_b, send_a, send_b = call(
        functools.partial(pull_last_kernel, n_dp),
        (
            place, back, residual_1, seed, wc, norm_params, qkv_1, probs_1,
            first_0, first_1, mixed_0, mixed_1, grad_0, low_0,
        ),
        pulled + [((4 * width, cols), bf16)] * 4,
        pull_scratch,
        waits=(send_e,),
        flops=10e9,
    )
    one_a, one_b = [keep_a, swap(send_a, *CORE)], [keep_b, swap(send_b, *CORE)]
    first, *others = far()
    (keep_e, keep_r), (sent,) = halved(
        place, [(two_a, first), (two_b, first)], joint=2, waits=(keep_a,)
    )
    (keep_a, keep_b), (send_a, send_b) = halved(place, [(one_a, NEAR), (one_b, ROW)], waits=(sent,))
    gots = swap(send_a, *NEAR), swap(send_b, *ROW)
    two_got = swap(sent, *first)
    grad_in_0, grad_in_1, norm = call(
        finish_kernel,
        (norm_params, wp, grad_0, frames_x[0], wide_0, grad_1, frames_x[1], wide_1, norm_0, norm_1),
        [((own, width), f32), ((own, width), f32), ((4 * parts, cols), f32)],
        waits=(send_a,),
        flops=3e9,
        smem=0,
    )
    norm = norm + swap(norm, *CORE)
    norms = (norm, swap(norm, *ROW))
    (keep_a, keep_b), norm, (send_a, send_b) = halved_norm(
        place, (keep_a, keep_b), gots, (ROW, NEAR), norms, False
    )
    gots = swap(send_a, *ROW), swap(send_b, *NEAR)
    (keep_e, keep_r), (send_e, send_r) = halved_joint(
        place, (keep_e, keep_r), two_got, (ROW, NEAR), joint=False, waits=(send_a,)
    )
    two_a, two_b = [keep_e, swap(send_e, *ROW)], [keep_r, swap(send_r, *NEAR)]
    pending = (send_e,)
    second, *others = others
    (keep_e, keep_r), (sent,) = halved(place, [(two_a, second), (two_b, second)], joint=2)
    two_got = swap(sent, *second)
    for label in others:
        (keep_e, keep_r), (sent,) = halved_joint(place, (keep_e, keep_r), two_got, (label, label))
        two_got = swap(sent, *label)
    for label in far():
        (keep_a, keep_b), norm, (sent,) = halved_norm(
            place, (keep_a, keep_b), gots, (label, label), (norm,), True, waits=pending
        )
        gots, pending = (swap(sent, *label),), ()

    plain = lambda x: [(x.shape, f32)] * 4
    weighed = lambda x: plain(x) + [(x.shape, bf16)]
    updated = call(
        update_feed_kernel,
        (
            keep_e, keep_r, two_got, weight_expand, moment_expand, average_expand,
            weight_reduce, moment_reduce, average_reduce,
        ),
        weighed(weight_expand) + weighed(weight_reduce) + [((8, 128), f32)],
        flops=1e8,
        smem=0,
        mib=8,
    )
    gradient_expand, mom_expand, avg_expand, new_expand, low_expand = updated[:5]
    gradient_reduce, mom_reduce, avg_reduce, new_reduce, low_reduce = updated[5:10]
    fed_done = updated[10]
    updated = call(
        update_rest_kernel,
        (
            keep_a, keep_b, gots[0], norm, weight_project, moment_project, average_project,
            weight_combine, moment_combine, average_combine, norm_params, norm_moment, norm_average,
        ),
        weighed(weight_project) + weighed(weight_combine) + plain(norm_params),
        waits=(fed_done,),
        flops=1e8,
        smem=0,
        mib=8,
    )
    gradient_project, mom_project, avg_project, new_project, low_project = updated[:5]
    gradient_combine, mom_combine, avg_combine, new_combine, low_combine = updated[5:10]
    norm_gradient, mom_norms, avg_norms, new_norms = updated[10:]
    layer_out = jnp.transpose(layer, (1, 0, 2))
    input_gradient = jnp.transpose(jnp.stack([grad_in_0, grad_in_1]), (1, 0, 2))
    return (
        layer_out,
        input_gradient,
        gradient_project,
        gradient_combine,
        gradient_expand,
        gradient_reduce,
        mom_project,
        mom_combine,
        mom_expand,
        mom_reduce,
        avg_project,
        avg_combine,
        avg_expand,
        avg_reduce,
        new_project,
        new_combine,
        new_expand,
        new_reduce,
        low_project,
        low_combine,
        low_expand,
        low_reduce,
        norm_gradient,
        mom_norms,
        avg_norms,
        new_norms,
    )


def solution(mesh):
    tokens = P("mp", "dp", None)
    stacked, matrix = P(None, "dp", "mp"), P("dp", "mp")
    weights = (stacked, matrix, matrix, matrix)
    in_specs = (tokens, tokens, P("dp")) + weights * 3 + (P(),) * 3
    out_specs = (tokens, tokens) + weights * 5 + (P(),) * 4
    return jax.shard_map(
        on_device, mesh=mesh, in_specs=in_specs, out_specs=out_specs, check_vma=False
    )
```
